32 devices in a mesh: items: 4 (over x, core), heads: 2 (over y), rows: 4 (over z).
Axes of the slice: x: 2, y: 2, z: 4, core: 2. Of those that a mesh axis runs over, the one named last changes fastest.
Arguments:
- inputs: bfloat16 [4, 1024, 1536], P('items', 'rows', 'heads'), may hold values from -6 to 6
- skip_input: bfloat16 [4, 2048, 1280], P('items', 'rows'), may hold values from -6 to 6
- cotangent: bfloat16 [4, 2048, 1536], P('items', 'rows', 'heads'), may hold values from -6 to 6
- track_mask: int32 [4, 1536], P('items', 'heads'), may hold values 0 or 1
- norm1_gain: float32 [1536], P(('items', 'rows')), may hold values from 0.1 to 1.9
- norm1_bias: float32 [1536], P(('items', 'rows')), may hold values from -1.8 to 1.8
- query_weight: float32 [1536, 512], P(('items', 'rows'), 'heads'), may hold values from -0.15625 to 0.15625
- key_weight: float32 [1536, 512], P(('items', 'rows'), 'heads'), may hold values from -0.15625 to 0.15625
- value_weight: float32 [1536, 1536], P(('items', 'rows'), 'heads'), may hold values from -0.15625 to 0.15625
- rel_weight: float32 [8, 2048], P('heads', ('items', 'rows')), may hold values from -1 to 1
- out_weight: float32 [1536, 1536], P('heads', ('items', 'rows')), may hold values from -0.625 to 0.625
- norm2_gain: float32 [1536], P(('items', 'rows')), may hold values from 0.1 to 1.9
- norm2_bias: float32 [1536], P(('items', 'rows')), may hold values from -1.8 to 1.8
- up_weight: float32 [1536, 3072], P(('items', 'rows'), 'heads'), may hold values from -0.15625 to 0.15625
- up_bias: float32 [2, 1536], P('heads', ('items', 'rows')), may hold values from -1.8 to 1.8
- down_weight: float32 [3072, 1536], P('heads', ('items', 'rows')), may hold values from -0.109375 to 0.109375
- down_bias: float32 [1536], P(('items', 'rows')), may hold values from -1.8 to 1.8
- skip_weight: float32 [1280, 1536], P(('items', 'rows'), 'heads'), may hold values from -0.15625 to 0.15625
- skip_bias: float32 [2, 768], P('heads', ('items', 'rows')), may hold values from -1.8 to 1.8
- depth_weight: float32 [3, 2, 768], P(None, 'heads', ('items', 'rows')), may hold values from -3 to 3
- point_weight: float32 [1536, 1536], P(('items', 'rows'), 'heads'), may hold values from -0.15625 to 0.15625
- point_bias: float32 [2, 768], P('heads', ('items', 'rows')), may hold values from -1.8 to 1.8
Outputs:
- block_output: bfloat16 [4, 2048, 1536], P('items', 'rows', 'heads')
- input_grad: float32 [4, 1024, 1536], P('items', 'rows', 'heads')
- grad_norm1_gain: float32 [1536], P(('items', 'rows'))
- grad_norm1_bias: float32 [1536], P(('items', 'rows'))
- grad_query_weight: float32 [1536, 512], P(('items', 'rows'), 'heads')
- grad_key_weight: float32 [1536, 512], P(('items', 'rows'), 'heads')
- grad_value_weight: float32 [1536, 1536], P(('items', 'rows'), 'heads')
- grad_rel_weight: float32 [8, 2048], P('heads', ('items', 'rows'))
- grad_out_weight: float32 [1536, 1536], P('heads', ('items', 'rows'))
- grad_norm2_gain: float32 [1536], P(('items', 'rows'))
- grad_norm2_bias: float32 [1536], P(('items', 'rows'))
- grad_up_weight: float32 [1536, 3072], P(('items', 'rows'), 'heads')
- grad_up_bias: float32 [2, 1536], P('heads', ('items', 'rows'))
- grad_down_weight: float32 [3072, 1536], P('heads', ('items', 'rows'))
- grad_down_bias: float32 [1536], P(('items', 'rows'))
- grad_skip_weight: float32 [1280, 1536], P(('items', 'rows'), 'heads')
- grad_skip_bias: float32 [2, 768], P('heads', ('items', 'rows'))
- grad_depth_weight: float32 [3, 2, 768], P(None, 'heads', ('items', 'rows'))
- grad_point_weight: float32 [1536, 1536], P(('items', 'rows'), 'heads')
- grad_point_bias: float32 [2, 768], P('heads', ('items', 'rows'))
The draws below stay inside these ranges and needn't reach their ends.
Inputs may be any that keep to these rules, and one draw needn't show every extreme that they name: `track_mask`: 1 where the item's track in that channel is observed.
All inputs are finite; a program needn't handle non-finite values. No bound on the sum of `track_mask` on one device may be relied on, other than what follows from the above.
Results may differ from the reference program's by a relative error of at most 0.02.
Values may be sent and summed in bfloat16 or wider, within the bound.
No kernel may reach another device: no remote copies, remote signals or barrier semaphores. Data moves between devices by JAX's collectives and lax.ppermute only.
A program may use at most 256 MiB of HBM per device.

```python
from functools import partial
import jax
import jax.numpy as jnp
from jax import lax

D = 1536
HEADS = 8
KEY = 64
VAL = 192
NB = 32
FF = 3072
SKIP = 1280
ITEMS = 4
SEQ = 1024
N_HEADS = 2


def with_ends(values, stream_key, least, largest):
    extent = values.shape
    index_at = [jax.random.randint(jax.random.fold_in(stream_key, axis), (), 0, extent[axis]) for axis in range(len(extent))]
    values = values.at[tuple(index_at)].set(least)
    longest = extent.index(max(extent))
    index_at[longest] = (index_at[longest] + 1) % extent[longest]
    return values.at[tuple(index_at)].set(largest)


def shard_levels(stream_key, shape, cuts, smallest, high):
    def one(position, shards_of):
        draws = jax.random.uniform(jax.random.fold_in(jax.random.fold_in(stream_key, 6), position), (shards_of,), jnp.float32, smallest / len(cuts), high / len(cuts))
        return jnp.repeat(jnp.exp(draws), shape[position] // shards_of).reshape((-1,) + (1,) * (len(shape) - position - 1))

    factor_of = one(*cuts[0])
    for cut in cuts[1:]:
        factor_of = factor_of * one(*cut)
    return factor_of


def noise(stream_key, extent, spread, bound, pieces=(), kind=jnp.bfloat16):
    entries = jax.random.normal(stream_key, extent, jnp.float32) * spread
    if len(pieces) > 0:
        entries = shard_levels(stream_key, extent, pieces, -0.22, 0.18) * entries
    return jnp.clip(entries, min=-bound, max=bound).astype(kind)


def setup_inputs(seed: int = 0) -> dict:
    key_of = jax.random.split(jax.random.key(seed), 23)
    return {
        "inputs": noise(key_of[0], (ITEMS, SEQ, D), 1.0, 6.0, ((0, 4), (1, 4), (2, 2))),
        "skip_input": noise(key_of[1], (ITEMS, 2 * SEQ, SKIP), 1.0, 6.0, ((0, 4), (1, 4))),
        "cotangent": noise(key_of[2], (ITEMS, 2 * SEQ, D), 1.0, 6.0, ((0, 4), (1, 4), (2, 2))),
        "track_mask": with_ends((jax.random.randint(key_of[3], (ITEMS, D), 0, 4) < 3).astype(jnp.int32), jax.random.fold_in(key_of[3], 1), 0, 1),
        "norm1_gain": jnp.clip(1.0 + 0.18 * jax.random.normal(key_of[4], (D,), jnp.float32), 0.1, 1.9),
        "norm1_bias": noise(key_of[5], (D,), 0.3, 1.8, ((0, 16),), jnp.float32),
        "query_weight": noise(key_of[6], (D, HEADS * KEY), D ** -0.5, 0.15625, ((0, 16), (1, 2)), jnp.float32),
        "key_weight": noise(key_of[7], (D, HEADS * KEY), D ** -0.5, 0.15625, ((0, 16), (1, 2)), jnp.float32),
        "value_weight": noise(key_of[8], (D, HEADS * VAL), D ** -0.5, 0.15625, ((0, 16), (1, 2)), jnp.float32),
        "rel_weight": noise(key_of[9], (HEADS, NB * KEY), NB ** -0.5, 1.0, ((0, 2), (1, 16)), jnp.float32),
        "out_weight": noise(key_of[10], (HEADS * VAL, D), (HEADS * VAL // 16) ** -0.5, 0.625, ((0, 2), (1, 16)), jnp.float32),
        "norm2_gain": jnp.clip(1.0 + 0.18 * jax.random.normal(key_of[11], (D,), jnp.float32), 0.1, 1.9),
        "norm2_bias": noise(key_of[12], (D,), 0.3, 1.8, ((0, 16),), jnp.float32),
        "up_weight": noise(key_of[13], (D, FF), D ** -0.5, 0.15625, ((0, 16), (1, 2)), jnp.float32),
        "up_bias": noise(key_of[14], (N_HEADS, FF // N_HEADS), 0.3, 1.8, ((0, 2), (1, 16)), jnp.float32),
        "down_weight": noise(key_of[15], (FF, D), FF ** -0.5, 0.109375, ((0, 2), (1, 16)), jnp.float32),
        "down_bias": noise(key_of[16], (D,), 0.3, 1.8, ((0, 16),), jnp.float32),
        "skip_weight": noise(key_of[17], (SKIP, D), SKIP ** -0.5, 0.15625, ((0, 16), (1, 2)), jnp.float32),
        "skip_bias": noise(key_of[18], (N_HEADS, D // N_HEADS), 0.3, 1.8, ((0, 2), (1, 16)), jnp.float32),
        "depth_weight": noise(key_of[19], (3, N_HEADS, D // N_HEADS), 0.6, 3.0, ((1, 2), (2, 16)), jnp.float32),
        "point_weight": noise(key_of[20], (D, D), D ** -0.5, 0.15625, ((0, 16), (1, 2)), jnp.float32),
        "point_bias": noise(key_of[21], (N_HEADS, D // N_HEADS), 0.3, 1.8, ((0, 2), (1, 16)), jnp.float32),
    }


NORM_EPSILON = 1e-05
HIGHEST_PRECISION = lax.Precision.HIGHEST

@jax.custom_vjp
def low(v):
    return lax.optimization_barrier(v.astype(jnp.bfloat16)).astype(jnp.float32)

@jax.custom_vjp
def low_back(v):
    return v

def low_keep(v):
    return (low(v), None)

def low_pass(kept, grad):
    return (grad,)

def back_keep(v):
    return (v, None)

def back_low(kept, grad):
    return (low(grad),)
low.defvjp(low_keep, low_pass)
low_back.defvjp(back_keep, back_low)

def matmul(left, right):
    return jnp.dot(left, right, precision=HIGHEST_PRECISION, preferred_element_type=jnp.float32)

def layer_norm(values, gain_vec, offset_vec):
    centered = values - lax.optimization_barrier(jnp.mean(values, axis=-1, keepdims=True))
    variance = lax.optimization_barrier(jnp.mean(centered * centered, axis=-1, keepdims=True))
    return centered * lax.rsqrt(variance + NORM_EPSILON) * gain_vec + offset_vec

def position_basis(length):
    distance = jnp.arange(2 * length - 1, dtype=jnp.float32) - (length - 1)
    magnitude = jnp.abs(distance)[:, None]
    number = NB // 4
    steps_up = jnp.arange(number, dtype=jnp.float32)
    half_life = 3.0 * (length / 3.0) ** (steps_up / max(number - 1, 1))
    decays = jnp.exp(-0.6931471805599453 * magnitude / half_life)
    widths = 2.0 ** (steps_up + 1.0) - 1.0
    central = (widths > magnitude).astype(jnp.float32)
    even_part = jnp.concatenate([decays, central], axis=1)
    return jnp.concatenate([even_part, jnp.sign(distance)[:, None] * even_part], axis=1)

def skew_rows(rel_table):
    rows_n = rel_table.shape[-2]
    table_width = rel_table.shape[-1]
    flattened = rel_table.reshape(rel_table.shape[:-2] + (rows_n * table_width,))
    flattened = flattened[..., rows_n - 1:rows_n - 1 + rows_n * (table_width - 1)]
    shaped = flattened.reshape(rel_table.shape[:-2] + (rows_n, table_width - 1))
    return shaped[..., :table_width - rows_n + 1]

def item_forward(params, inputs_one, skip_low):
    gain_one, bias_one, w_query, w_key, w_value, w_rel, w_out, gain_two, bias_two, w_up, b_up, w_down, b_down, w_skip, b_skip, w_depth, w_point, b_point = tuple((low(master) for master in params))
    normed = low(layer_norm(inputs_one, gain_one, bias_one))
    queries = low_back(low(KEY ** (-0.5) * matmul(normed, w_query))).reshape(SEQ, HEADS, KEY)
    keys_all = low_back(low(matmul(normed, w_key))).reshape(SEQ, HEADS, KEY)
    values_all = low_back(low(matmul(normed, w_value))).reshape(SEQ, HEADS, VAL)
    rel_basis = low(position_basis(SEQ))
    rel_keys = low(jnp.einsum('tb,hbd->thd', rel_basis, w_rel.reshape(HEADS, NB, KEY), precision=HIGHEST_PRECISION))
    block_rows = min(512, SEQ)

    def attend(block_start):
        query_block = lax.dynamic_slice_in_dim(queries, block_start, block_rows, 0)
        content = jnp.einsum('qhd,khd->hqk', query_block, keys_all, precision=HIGHEST_PRECISION)
        window = lax.dynamic_slice_in_dim(rel_keys, SEQ - block_start - block_rows, SEQ + block_rows - 1, 0)
        rel_table = jnp.einsum('qhd,thd->hqt', query_block, window, precision=HIGHEST_PRECISION)
        logits = low_back(content + skew_rows(rel_table))
        attn_probs = jax.nn.softmax(logits, axis=-1)
        return jnp.einsum('hqk,khv->qhv', low(attn_probs), values_all, precision=HIGHEST_PRECISION)
    starts = jnp.arange(SEQ // block_rows, dtype=jnp.int32) * block_rows
    attended = lax.map(jax.checkpoint(attend), starts)
    attended = low_back(low(attended.reshape(SEQ, HEADS * VAL)))
    hidden_one = inputs_one + low_back(matmul(attended, w_out))
    normed_two = low(layer_norm(hidden_one, gain_two, bias_two))
    pre_act = low_back(matmul(normed_two, w_up) + b_up.reshape(-1))
    activated = low(jax.nn.gelu(pre_act, approximate=True))
    transformed = hidden_one + low_back(matmul(activated, w_down) + b_down)
    upsampled = jnp.repeat(jax.nn.gelu(transformed, approximate=True), 2, axis=0)
    skip_term = low_back(matmul(skip_low, w_skip) + b_skip.reshape(-1))
    summed = upsampled + skip_term
    padded = jnp.pad(summed, ((1, 1), (0, 0)))
    taps = w_depth.reshape(3, D)
    mixed = low(taps[0] * padded[:-2] + taps[1] * padded[1:-1] + taps[2] * padded[2:])
    return low_back(matmul(mixed, w_point) + b_point.reshape(-1))

def reference(inputs, skip_input, cotangent, track_mask, norm1_gain, norm1_bias, query_weight, key_weight, value_weight, rel_weight, out_weight, norm2_gain, norm2_bias, up_weight, up_bias, down_weight, down_bias, skip_weight, skip_bias, depth_weight, point_weight, point_bias):
    params = (norm1_gain, norm1_bias, query_weight, key_weight, value_weight, rel_weight, out_weight, norm2_gain, norm2_bias, up_weight, up_bias, down_weight, down_bias, skip_weight, skip_bias, depth_weight, point_weight, point_bias)
    zero_grads = jax.tree.map(jnp.zeros_like, params)

    def one_item(totals, item_data):
        inputs_one, skip_one, cot_one, mask_one = item_data
        skip_low = low(jax.nn.gelu(skip_one.astype(jnp.float32), approximate=True))
        output, pullback = jax.vjp(partial(item_forward, skip_low=skip_low), params, inputs_one.astype(jnp.float32))
        grad_params, grad_input = pullback(cot_one.astype(jnp.float32) * mask_one.astype(jnp.float32)[None, :])
        totals = jax.tree.map(jnp.add, totals, grad_params)
        return (totals, (output.astype(jnp.bfloat16), grad_input))
    totals, (outputs, grad_inputs) = lax.scan(one_item, zero_grads, (inputs, skip_input, cotangent, track_mask))
    return (outputs, grad_inputs, totals[0], totals[1], totals[2], totals[3], totals[4], totals[5], totals[6], totals[7], totals[8], totals[9], totals[10], totals[11], totals[12], totals[13], totals[14], totals[15], totals[16], totals[17])
```

```python
import functools

import jax
import jax.numpy as jnp
import numpy as np
from jax import lax
from jax.experimental import pallas as pl
from jax.experimental.pallas import tpu as pltpu
from jax.sharding import PartitionSpec as P

KEY = 64
VAL = 192
NB = 32
EPS = 1e-05
IT, HD, RW = "items", "heads", "rows"
LOW = jnp.bfloat16
F32 = jnp.float32
VMEM = pltpu.CompilerParams(vmem_limit_bytes=56 * 2**20)
LANES = 1280


def nn(a, b):
    return lax.dot_general(a, b, (((1,), (0,)), ((), ())), preferred_element_type=F32)


def nt(a, b):
    return lax.dot_general(a, b, (((1,), (1,)), ((), ())), preferred_element_type=F32)


def tn(a, b):
    return lax.dot_general(a, b, (((0,), (0,)), ((), ())), preferred_element_type=F32)


def wide(a):
    return a.astype(F32)


def low(a):
    return lax.reduce_precision(a, 8, 7).astype(LOW)


def to_core(a):
    n = lax.axis_size(IT)
    return lax.ppermute(a, IT, [(i, i ^ 1) for i in range(n)])


def to_pair(a, k):
    n = lax.axis_size(IT)
    return lax.ppermute(a, IT, [(i, (i + 2 * k) % n) for i in range(n)])


def to_row(a, k):
    n = lax.axis_size(RW)
    return lax.ppermute(a, RW, [(i, (i + k) % n) for i in range(n)])


def to_head(a):
    return lax.ppermute(a, HD, [(0, 1), (1, 0)])


def place():
    item = lax.axis_index(IT)
    return item // 2, item % 2, lax.axis_index(RW)


def gather_pieces(piece):
    pairs, rows = lax.axis_size(IT) // 2, lax.axis_size(RW)
    own = [((0, dz), piece if dz == 0 else to_row(piece, dz)) for dz in range(rows)]
    both = own + [
        ((dx, dz), to_pair(got, dx)) for dx in range(1, pairs) for (_, dz), got in own
    ]
    out = [((dx, 0, dz), got) for (dx, dz), got in both]
    return out + [((dx, 1, dz), to_core(got)) for (dx, dz), got in both]


def assemble_kernel(offsets, height, at_ref, *refs):
    pieces, (full_ref, tail_ref, sems) = refs[:-3], refs[-3:]
    copies = []
    for i, piece in enumerate(pieces):
        spot = at_ref[i]
        start = pl.multiple_of(spot * height, 16)
        copies.append(
            pltpu.make_async_copy(
                piece.at[pl.ds(0, height)], full_ref.at[pl.ds(start, height)], sems.at[0, i]
            )
        )
        copies.append(
            pltpu.make_async_copy(
                piece.at[pl.ds(height, piece.shape[0] - height)], tail_ref.at[spot], sems.at[1, i]
            )
        )
    for copy in copies:
        copy.start()
    for copy in copies:
        copy.wait()


def gather_group(piece, height):
    pairs, rows = lax.axis_size(IT) // 2, lax.axis_size(RW)
    group = pairs * 2 * rows
    if group > 16 or height % 16:
        full = lax.all_gather(piece, (IT, RW), axis=0, tiled=False)
        return full[:, :height].reshape(group * height, -1), full[:, height:]
    x, c, z = place()
    pieces = gather_pieces(piece)
    spots = []
    for (dx, dc, dz), _ in pieces:
        spots.append((((x - dx) % pairs) * 2 + (c + dc) % 2) * rows + (z - dz) % rows)
    n = piece.shape[1]
    tail = piece.shape[0] - height
    anywhere = pl.BlockSpec(memory_space=pl.ANY)
    return pl.pallas_call(
        functools.partial(assemble_kernel, None, height),
        in_specs=[pl.BlockSpec(memory_space=pltpu.SMEM)] + [anywhere] * group,
        out_specs=(anywhere, anywhere),
        out_shape=(
            jax.ShapeDtypeStruct((group * height, n), piece.dtype),
            jax.ShapeDtypeStruct((group, tail, n), piece.dtype),
        ),
        scratch_shapes=[pltpu.SemaphoreType.DMA((2, group))],
    )(jnp.stack(spots).astype(jnp.int32), *[got for _, got in pieces])


def scatter_rows(block):
    rows = lax.axis_size(RW)
    z = lax.axis_index(RW)
    w = block.shape[0] // rows
    total = lax.dynamic_slice_in_dim(block, z * w, w, 0)
    for k in range(1, rows):
        part = lax.dynamic_slice_in_dim(block, ((z + k) % rows) * w, w, 0)
        total = total + wide(to_row(low(part), k))
    return total


def scatter_grads(pairs_of):
    pairs = lax.axis_size(IT) // 2
    x, c, _ = place()
    wanted = [(x + k) % pairs for k in range(pairs)]

    def product(side):
        out = []
        for left, right in pairs_of:
            w = left.shape[1] // (2 * pairs)
            part = [
                lax.dynamic_slice_in_dim(left, (xi * 2 + side) * w, w, 1) for xi in wanted
            ]
            out.append(tn(jnp.concatenate(part, axis=1), right))
        return jnp.concatenate(out, axis=1)

    theirs = low(product(1 - c))
    ours = product(c) + wide(to_core(theirs))
    w = ours.shape[0] // pairs
    total = ours[:w]
    for k in range(1, pairs):
        total = total + wide(to_pair(low(ours[k * w : (k + 1) * w]), k))
    return scatter_rows(total)


def scatter_small(parts):
    pairs, rows = lax.axis_size(IT) // 2, lax.axis_size(RW)
    x, c, z = place()
    n = parts.shape[1]
    cube = parts.reshape(pairs, 2, rows, n)
    cube = lax.dynamic_index_in_dim(cube, c, 1, keepdims=False) + to_core(
        lax.dynamic_index_in_dim(cube, 1 - c, 1, keepdims=False)
    )
    plane = lax.dynamic_index_in_dim(cube, x, 0, keepdims=False)
    for k in range(1, pairs):
        plane = plane + to_pair(
            lax.dynamic_index_in_dim(cube, (x + k) % pairs, 0, keepdims=False), k
        )
    total = lax.dynamic_index_in_dim(plane, z, 0, keepdims=True)
    for k in range(1, rows):
        total = total + to_row(
            lax.dynamic_index_in_dim(plane, (z + k) % rows, 0, keepdims=True), k
        )
    return total


def attend_kernel(q_ref, kv_ref, wr_ref, basis_ref, out_ref, p_ref):
    rows, seq, heads = q_ref.shape[0], kv_ref.shape[0], p_ref.shape[0]
    width = heads * KEY
    basis = basis_ref[...]
    outs = []
    for h in range(heads):
        qh = q_ref[:, h * KEY : (h + 1) * KEY]
        kh = kv_ref[:, h * KEY : (h + 1) * KEY]
        vh = kv_ref[:, width + h * VAL : width + (h + 1) * VAL]
        features = nt(qh, wr_ref[h * NB : (h + 1) * NB, :]).astype(LOW)
        table = nt(features, basis)
        rel = [
            pltpu.roll(
                table[:, k * 2 * rows : (k + 1) * 2 * rows], rows + 1, 1, stride=1, stride_axis=0
            )[:, :rows]
            for k in range(seq // rows)
        ]
        logits = nt(qh, kh) + jnp.concatenate(rel, axis=1)
        e = jnp.exp(logits - jnp.max(logits, axis=1, keepdims=True))
        p = (e * (1.0 / jnp.sum(e, axis=1, keepdims=True))).astype(LOW)
        p_ref[h] = p
        outs.append(nn(p, vh))
    out_ref[...] = jnp.concatenate(outs, axis=1).astype(LOW)


def attend_back_kernel(q_ref, kv_ref, wr_ref, basis_ref, p_ref, g_ref, dq_ref, dkv_ref, dwr_ref):
    rows, seq, heads = q_ref.shape[0], kv_ref.shape[0], p_ref.shape[0]
    width = heads * KEY
    basis = basis_ref[...]
    ii = lax.broadcasted_iota(jnp.int32, (rows, rows), 0)
    jj = lax.broadcasted_iota(jnp.int32, (rows, rows), 1)
    flip = (ii + jj == rows - 1).astype(F32).astype(LOW)
    dqs, dks, dvs = [], [], []
    for h in range(heads):
        qh = q_ref[:, h * KEY : (h + 1) * KEY]
        kh = kv_ref[:, h * KEY : (h + 1) * KEY]
        vh = kv_ref[:, width + h * VAL : width + (h + 1) * VAL]
        gh = g_ref[:, h * VAL : (h + 1) * VAL]
        wr = wr_ref[h * NB : (h + 1) * NB, :]
        p = p_ref[h]
        probs = p.astype(F32)
        dp = nt(gh, vh)
        inner = jnp.sum(probs * dp, axis=1, keepdims=True)
        ds = (probs * (dp - inner)).astype(LOW)
        dvs.append(tn(p, gh))
        dks.append(tn(ds, qh))
        rev = nn(flip, ds)
        zeros = jnp.zeros((rows, rows), F32)
        tabs = [
            pltpu.roll(
                jnp.concatenate([rev[:, k * rows : (k + 1) * rows], zeros], axis=1),
                0,
                1,
                stride=1,
                stride_axis=0,
            ).astype(LOW)
            for k in range(seq // rows)
        ]
        features = nn(jnp.concatenate(tabs, axis=1), basis).astype(LOW)
        features = nn(flip, features).astype(LOW)
        dqs.append(nn(ds, kh) + nn(features, wr))
        dwr_ref[h * NB : (h + 1) * NB, :] = tn(features, qh)
    dq = jnp.concatenate(dqs, axis=1).astype(LOW).astype(F32) * (KEY**-0.5)
    dq_ref[...] = dq.astype(LOW)
    dkv_ref[...] = jnp.concatenate(dks + dvs, axis=1).astype(LOW)


def attend(q, kv, wr, basis):
    heads = wr.shape[0] // NB
    return pl.pallas_call(
        attend_kernel,
        out_shape=(
            jax.ShapeDtypeStruct((q.shape[0], heads * VAL), LOW),
            jax.ShapeDtypeStruct((heads, q.shape[0], kv.shape[0]), LOW),
        ),
        compiler_params=VMEM,
    )(q, kv, wr, basis)


def attend_back(q, kv, wr, basis, p, g):
    return pl.pallas_call(
        attend_back_kernel,
        out_shape=(
            jax.ShapeDtypeStruct(q.shape, LOW),
            jax.ShapeDtypeStruct(kv.shape, LOW),
            jax.ShapeDtypeStruct(wr.shape, F32),
        ),
        compiler_params=VMEM,
    )(q, kv, wr, basis, p, g)


def position_windows(z, width, rows):
    seq = width * rows
    block = (z - np.arange(rows)) % rows - z
    t = block[:, None] * width + (np.arange(2 * width) - (width - 1))[None, :]
    distance = t.reshape(-1).astype(F32)
    magnitude = jnp.abs(distance)[:, None]
    number = NB // 4
    steps_up = np.arange(number, dtype=np.float32)
    half_life = (3.0 * (seq / 3.0) ** (steps_up / max(number - 1, 1))).astype(np.float32)
    decays = jnp.exp(-0.6931471805599453 * magnitude / half_life)
    central = (2.0 ** (steps_up + 1.0) - 1.0 > magnitude).astype(F32)
    even = jnp.concatenate([decays, central], axis=1)
    return jnp.concatenate([even, jnp.sign(distance)[:, None] * even], axis=1).astype(LOW)


G0, G1 = 0.7978845608028654, 0.044715


def gelu(u):
    return 0.5 * u * (1.0 + jnp.tanh(G0 * (u + G1 * u * u * u)))


def gelu_slope(u):
    t = jnp.tanh(G0 * (u + G1 * u * u * u))
    return 0.5 * (1.0 + t) + 0.5 * u * (1.0 - t * t) * (G0 * (1.0 + 3.0 * G1 * u * u))


def normalize(values):
    centered = values - jnp.mean(values, axis=-1, keepdims=True)
    scale = lax.rsqrt(jnp.mean(centered * centered, axis=-1, keepdims=True) + EPS)
    return centered * scale, scale


def norm_back(grad, hat, scale, gain):
    gg = grad * gain
    return scale * (
        gg
        - jnp.mean(gg, axis=-1, keepdims=True)
        - hat * jnp.mean(gg * hat, axis=-1, keepdims=True)
    )


def pick(head, own, other):
    return jnp.where(head == 0, own, other), jnp.where(head == 0, other, own)


def both_halves(head, own, other):
    return jnp.concatenate(pick(head, own, other), axis=1)


def half(a, head):
    n = a.shape[1] // 2
    return lax.dynamic_slice_in_dim(a, head * n, n, 1)


def one_hot(select, height, width):
    ii = lax.broadcasted_iota(jnp.int32, (height, width), 0)
    jj = lax.broadcasted_iota(jnp.int32, (height, width), 1)
    return select(ii, jj).astype(LOW)


def halo_down(a):
    n = lax.axis_size(RW)
    edge = lax.ppermute(a[-1:].astype(LOW), RW, [(i, i + 1) for i in range(n - 1)])
    return jnp.concatenate([wide(edge), a[:-1]], axis=0)


def halo_up(a):
    n = lax.axis_size(RW)
    edge = lax.ppermute(a[:1].astype(LOW), RW, [(i + 1, i) for i in range(n - 1)])
    return jnp.concatenate([a[1:], wide(edge)], axis=0)


def fold(values, height):
    k = -(-values.size // height)
    return jnp.pad(values.reshape(-1), (0, k * height - values.size))


def shards(
    inputs,
    skip_input,
    cotangent,
    track_mask,
    norm1_gain,
    norm1_bias,
    query_weight,
    key_weight,
    value_weight,
    rel_weight,
    out_weight,
    norm2_gain,
    norm2_bias,
    up_weight,
    up_bias,
    down_weight,
    down_bias,
    skip_weight,
    skip_bias,
    depth_weight,
    point_weight,
    point_bias,
):
    head = lax.axis_index(HD)
    _, _, z = place()
    rows = lax.axis_size(RW)
    group = lax.axis_size(IT) * rows
    width, chan = inputs.shape[1], inputs.shape[2]
    model = 2 * chan
    heads = rel_weight.shape[0]
    kw = heads * KEY
    shard = norm1_gain.shape[0]
    small = skip_bias.shape[1]
    rel_cols = rel_weight.shape[1]

    flat = jnp.concatenate(
        [norm1_gain, norm1_bias, norm2_gain, norm2_bias, down_bias, up_bias[0]]
        + [skip_bias[0], depth_weight.reshape(-1), point_bias[0], rel_weight.reshape(-1)]
    ).astype(LOW)
    tail_rows = -(-flat.size // (16 * LANES)) * 16
    flat = jnp.pad(flat, (0, tail_rows * LANES - flat.size)).reshape(tail_rows, LANES)
    qkv_piece = jnp.concatenate([query_weight, key_weight, value_weight], axis=1).astype(LOW)
    qkv_piece = jnp.concatenate([qkv_piece, flat], axis=0)
    big_piece = jnp.concatenate(
        [out_weight.T.astype(LOW), up_weight.astype(LOW)]
        + [down_weight.T.astype(LOW), point_weight.astype(LOW)],
        axis=1,
    )
    big = lax.all_gather(big_piece, (IT, RW), axis=0, tiled=True)
    w_skip = lax.all_gather(skip_weight.astype(LOW), (IT, RW), axis=0, tiled=True)
    w_qkv, tails = gather_group(qkv_piece, shard)
    ff = up_weight.shape[1]
    w_out, w_up = big[:, :chan], big[:, chan : chan + ff]
    w_down, w_point = big[:, chan + ff : chan + 2 * ff], big[:, chan + 2 * ff :]
    tails = tails.reshape(group, -1)

    def vector(start, count):
        return wide(tails[:, start : start + count]).reshape(1, -1)

    gain_one, bias_one, gain_two, bias_two, b_down, b_up = (
        vector(i * shard, shard) for i in range(6)
    )
    at = 6 * shard
    b_skip, tap0, tap1, tap2, b_point = (vector(at + i * small, small) for i in range(5))
    at += 5 * small
    w_rel = tails[:, at : at + heads * rel_cols].reshape(group, heads, rel_cols)
    w_rel = w_rel.transpose(1, 0, 2).reshape(heads * NB, KEY)

    own_blocks = [inputs[0]] + [to_row(inputs[0], k) for k in range(1, rows)]
    blocks = [both_halves(head, b, to_head(b)) for b in own_blocks]
    x_own = wide(blocks[0])
    hat_all, scale_all = normalize(wide(jnp.concatenate(blocks, axis=0)))
    normed_all = (hat_all * gain_one + bias_one).astype(LOW)
    normed = normed_all[:width]
    hat_one, scale_one = hat_all[:width], scale_all[:width]
    queries = (nn(normed, w_qkv[:, :kw]) * (KEY**-0.5)).astype(LOW)
    kv = nn(normed_all, w_qkv[:, kw:]).astype(LOW)
    basis = position_windows(z, width, rows)

    attended, probs = attend(queries, kv, w_rel, basis)
    partial_attn = low(nt(attended, w_out))
    hidden = x_own + (wide(partial_attn) + wide(to_head(partial_attn)))
    hat_two, scale_two = normalize(hidden)
    normed_two = (hat_two * gain_two + bias_two).astype(LOW)
    pre_act = nn(normed_two, w_up) + b_up
    activated = gelu(pre_act).astype(LOW)
    partial_ff = nt(activated, w_down)
    ff_local = half(partial_ff, head) + wide(to_head(low(half(partial_ff, 1 - head))))
    trans = half(hidden, head) + ff_local + half(b_down, head)

    even = one_hot(lambda i, j: j == 2 * i, width, 2 * width)
    odd = one_hot(lambda i, j: j == 2 * i + 1, width, 2 * width)
    apart = jnp.concatenate([even, odd], axis=0)
    skip_low = nn(apart, gelu(wide(skip_input[0])).astype(LOW)).astype(LOW)
    grad_out = nn(apart, (wide(cotangent[0]) * wide(track_mask)).astype(LOW)).astype(LOW)

    grad_mixed = nt(grad_out, w_point)
    grad_mixed = half(grad_mixed, head) + wide(to_head(low(half(grad_mixed, 1 - head))))
    gm_even, gm_odd = grad_mixed[:width], grad_mixed[width:]
    gs_even = tap0 * gm_odd + tap1 * gm_even + tap2 * halo_down(gm_odd)
    gs_odd = tap0 * halo_up(gm_even) + tap1 * gm_odd + tap2 * gm_even
    grad_skip_low = jnp.concatenate([gs_even, gs_odd], axis=0).astype(LOW)
    grad_skip = scatter_grads([(skip_low, grad_skip_low)])
    grad_skip_bias = jnp.sum(wide(grad_skip_low), axis=0)
    grad_coarse = gs_even + gs_odd

    skip_term = nn(skip_low, w_skip) + b_skip
    coarse = gelu(trans)
    s_even, s_odd = coarse + skip_term[:width], coarse + skip_term[width:]
    s_before, s_after = halo_down(s_odd), halo_up(s_even)
    mixed = jnp.concatenate(
        [
            tap0 * s_before + tap1 * s_even + tap2 * s_odd,
            tap0 * s_even + tap1 * s_odd + tap2 * s_after,
        ],
        axis=0,
    ).astype(LOW)
    mixed_full = both_halves(head, mixed, to_head(mixed))
    result = (nn(mixed_full, w_point) + b_point).astype(LOW)
    block_output = tn(apart, result).astype(LOW)[None]
    grad_point = scatter_grads([(mixed_full, grad_out)])
    grad_point_bias = jnp.sum(wide(grad_out), axis=0)
    grad_depth = [
        jnp.sum(gm_even * s_before + gm_odd * s_even, axis=0),
        jnp.sum(gm_even * s_even + gm_odd * s_odd, axis=0),
        jnp.sum(gm_even * s_odd + gm_odd * s_after, axis=0),
    ]

    grad_trans = gelu_slope(trans) * grad_coarse
    grad_own = low(grad_trans)
    grad_ff_low = both_halves(head, grad_own, to_head(grad_own))
    grad_act = nn(grad_ff_low, w_down)
    grad_pre_low = (gelu_slope(pre_act) * grad_act).astype(LOW)
    grad_down = scatter_grads([(grad_ff_low, activated)])
    grad_down_bias = jnp.sum(wide(grad_ff_low), axis=0)
    partial_two = low(nt(grad_pre_low, w_up))
    grad_up = scatter_grads([(normed_two, grad_pre_low)])
    grad_up_bias = jnp.sum(wide(grad_pre_low), axis=0)
    grad_normed_two = wide(partial_two) + wide(to_head(partial_two))
    grad_gain_two = jnp.sum(grad_normed_two * hat_two, axis=0)
    grad_bias_two = jnp.sum(grad_normed_two, axis=0)
    grad_norm_two = norm_back(grad_normed_two, hat_two, scale_two, gain_two)
    grad_proj_low = (wide(grad_ff_low) + grad_norm_two).astype(LOW)
    grad_attended = nn(grad_proj_low, w_out).astype(LOW)
    grad_out_w = scatter_grads([(grad_proj_low, attended)])
    dq, dkv, grad_rel = attend_back(queries, kv, w_rel, basis, probs, grad_attended)
    dkv_own = dkv[:width]
    for k in range(1, rows):
        dkv_own = wide(dkv_own) + wide(to_row(dkv[k * width : (k + 1) * width], rows - k))
    grad_qkv = scatter_grads([(normed, dq), (normed_all, dkv)])
    dqkv = jnp.concatenate([dq, dkv_own.astype(LOW)], axis=1)
    partial_one = low(nt(dqkv, w_qkv))
    grad_normed = wide(partial_one) + wide(to_head(partial_one))
    grad_gain_one = jnp.sum(grad_normed * hat_one, axis=0)
    grad_bias_one = jnp.sum(grad_normed, axis=0)
    grad_norm_one = norm_back(grad_normed, hat_one, scale_one, gain_one)
    input_grad = (grad_trans + half(grad_norm_two, head) + half(grad_norm_one, head))[None]

    rel_parts = grad_rel.reshape(heads, group, rel_cols).transpose(1, 0, 2)
    parts = [grad_gain_one, grad_bias_one, grad_gain_two, grad_bias_two, grad_down_bias]
    parts += [grad_up_bias, grad_skip_bias] + grad_depth + [grad_point_bias]
    parts = jnp.concatenate([p.reshape(group, -1) for p in parts] + [rel_parts.reshape(group, -1)], axis=1)
    sums = scatter_small(parts)

    def own(start, count):
        return sums[0, start : start + count]

    at = 6 * shard
    return (
        block_output,
        input_grad,
        own(0, shard),
        own(shard, shard),
        grad_qkv[:, :kw],
        grad_qkv[:, kw : 2 * kw],
        grad_qkv[:, 2 * kw :],
        own(at + 5 * small, heads * rel_cols).reshape(heads, rel_cols),
        grad_out_w.T,
        own(2 * shard, shard),
        own(3 * shard, shard),
        grad_up,
        own(5 * shard, shard)[None],
        grad_down.T,
        own(4 * shard, shard),
        grad_skip,
        own(at, small)[None],
        own(at + small, 3 * small).reshape(3, 1, small),
        grad_point,
        own(at + 4 * small, small)[None],
    )


def solution(mesh):
    gr = (IT, RW)
    vec, cols, rws = P(gr), P(gr, HD), P(HD, gr)
    act = P(IT, RW, HD)
    taps = P(None, HD, gr)
    weights = (vec, vec, cols, cols, cols, rws, rws, vec, vec, cols, rws, rws, vec, cols, rws)
    weights += (taps, cols, rws)
    return jax.shard_map(
        shards,
        mesh=mesh,
        in_specs=(act, P(IT, RW, None), act, P(IT, HD)) + weights,
        out_specs=(act, act) + weights,
        check_vma=False,
    )
```

```python
import functools

import jax
import jax.numpy as jnp
import numpy as np
from jax import lax
from jax.experimental import pallas as pl
from jax.experimental.pallas import tpu as pltpu
from jax.sharding import PartitionSpec as P

KEY = 64
VAL = 192
NB = 32
EPS = 1e-05
IT, HD, RW = "items", "heads", "rows"
LOW = jnp.bfloat16
F32 = jnp.float32
VMEM = pltpu.CompilerParams(vmem_limit_bytes=56 * 2**20)
SHORT = pl.CostEstimate(flops=1, bytes_accessed=1, transcendentals=0)


def nn(a, b):
    return lax.dot_general(a, b, (((1,), (0,)), ((), ())), preferred_element_type=F32)


def nt(a, b):
    return lax.dot_general(a, b, (((1,), (1,)), ((), ())), preferred_element_type=F32)


def tn(a, b):
    return lax.dot_general(a, b, (((0,), (0,)), ((), ())), preferred_element_type=F32)


def wide(a):
    return a.astype(F32)


def low(a):
    return lax.reduce_precision(a, 8, 7).astype(LOW)


def bit_order(n):
    out, bit = [0], n // 2
    while bit:
        out += [i + bit for i in out]
        bit //= 2
    return out


def to_core(a):
    n = lax.axis_size(IT)
    return lax.ppermute(a, IT, [(i, i ^ 1) for i in range(n)])


def to_pair(a, k):
    n = lax.axis_size(IT)
    return lax.ppermute(a, IT, [(i, (i + 2 * k) % n) for i in range(n)])


def to_head(a):
    return lax.ppermute(a, HD, [(0, 1), (1, 0)])


def place():
    item = lax.axis_index(IT)
    return item // 2, item % 2, lax.axis_index(RW)


def to_bit(a, bit):
    n = lax.axis_size(RW)
    return lax.ppermute(a, RW, [(i, i ^ bit) for i in range(n)])


def halve(keep, got, pick_bit, pieces, after=()):
    w, n = keep.shape[0] // pieces, keep.shape[1]
    shape = (pieces // 2, 2, w, n)
    if w % 16:
        total = (keep + wide(jnp.concatenate(got, axis=1))).reshape(shape)
        mine = lax.dynamic_index_in_dim(total, pick_bit, 1, keepdims=False)
        send = lax.dynamic_index_in_dim(total, 1 - pick_bit, 1, keepdims=False)
        return mine.reshape(-1, n), low(send).reshape(-1, n)
    widths = [g.shape[1] for g in got]

    def body(bit_ref, keep_ref, *refs):
        got_refs, (mine_ref, send_ref) = refs[:-2], refs[-2:]

        def write(bit):
            at = 0
            for ref, count in zip(got_refs, widths):
                there = slice(at, at + count)
                at += count
                mine_ref[0, :, there] = keep_ref[0, bit, :, there] + ref[0, bit].astype(F32)
                total = keep_ref[0, 1 - bit, :, there] + ref[0, 1 - bit].astype(F32)
                send_ref[0, :, there] = total.astype(LOW)

        for bit in range(2):
            pl.when(bit_ref[0] == bit)(functools.partial(write, bit))

    def block(count):
        return (1, 2, w, count), lambda i: (i, 0, 0, 0)

    out = (1, w, n), lambda i: (i, 0, 0)
    half_shape = (pieces // 2, w, n)
    mine, send = run(
        body,
        pieces // 2,
        [(pick_bit.reshape(1), None, None), (keep.reshape(shape), *block(n))]
        + [(g.reshape(pieces // 2, 2, w, count), *block(count)) for g, count in zip(got, widths)],
        [(new(half_shape, F32), *out), (new(half_shape, LOW), *out)],
        after=after,
    )
    return mine.reshape(-1, n), send.reshape(-1, n)


def side_product(pairs_of, side, got=None, after=(), groups=None):
    pairs = lax.axis_size(IT) // 2
    x, _, _ = place()
    w = pairs_of[0][0].shape[1] // (2 * pairs)
    spots = [(((x + k) % pairs) * 2 + side) for k in range(pairs)]
    cols = [right.shape[1] for _, right in pairs_of]
    ends = [int(e) for e in np.cumsum([0] + cols)]
    groups = groups or [[k] for k in range(len(cols))]
    bounds = [(ends[g[0]], ends[g[-1] + 1]) for g in groups]
    if w % 128:
        out = []
        for left, right in pairs_of:
            part = [lax.dynamic_slice_in_dim(left, spot * w, w, 1) for spot in spots]
            out.append(tn(jnp.concatenate(part, axis=1)[: right.shape[0]], right))
        out = jnp.concatenate(out, axis=1)
        if got is None:
            return low(out)
        out = out + wide(got)
        return out[:w], [low(out[w:, i:j]) for i, j in bounds]
    n, count, m = sum(cols), len(pairs_of), len(after)

    def body(spot_ref, *refs):
        lefts, rights = refs[:count], refs[count : 2 * count]
        outs = refs[2 * count + (got is not None) + m :]
        step = pl.program_id(0)
        for k in range(count):
            there = slice(ends[k], ends[k + 1])
            to = next(i for i, g in enumerate(groups) if k in g)
            inside = slice(ends[k] - bounds[to][0], ends[k + 1] - bounds[to][0])
            part = tn(lefts[k][...], rights[k][...])
            if got is None:
                outs[0][:, there] = part.astype(LOW)
                continue
            part = part + refs[2 * count][:, there].astype(F32)

            @pl.when(step == 0)
            def _(part=part, there=there):
                outs[0][:, there] = part

            @pl.when(step > 0)
            def _(part=part, to=to, inside=inside):
                outs[1 + to][:, inside] = part.astype(LOW)

    specs = [
        pl.BlockSpec((right.shape[0], w), lambda i, spot: (0, spot[i])) for left, right in pairs_of
    ] + [pl.BlockSpec(right.shape, lambda i, spot: (0, 0)) for _, right in pairs_of]
    operands = [left for left, _ in pairs_of] + [right for _, right in pairs_of]
    by_step = pl.BlockSpec((w, n), lambda i, spot: (i, 0))
    if got is None:
        out_specs, out_shape = [by_step], [new((pairs * w, n), LOW)]
    else:
        specs.append(by_step)
        operands.append(got)
        out_specs, out_shape = [pl.BlockSpec((w, n), lambda i, spot: (0, 0))], [new((w, n), F32)]
        for c in [j - i for i, j in bounds]:
            out_specs.append(pl.BlockSpec((w, c), lambda i, spot: (jnp.maximum(i - 1, 0), 0)))
            out_shape.append(new(((pairs - 1) * w, c), LOW))
    out = pl.pallas_call(
        body,
        grid_spec=pltpu.PrefetchScalarGridSpec(
            num_scalar_prefetch=1,
            grid=(pairs,),
            in_specs=specs + [pl.BlockSpec(memory_space=pl.ANY)] * m,
            out_specs=out_specs,
        ),
        out_shape=out_shape,
        compiler_params=VMEM,
        cost_estimate=SHORT,
    )(jnp.stack(spots).astype(jnp.int32), *operands, *after)
    return out[0] if got is None else (out[0], list(out[1:]))


class Scatter:
    def __init__(self, pairs_of, after=(), after_more=(), groups=None):
        _, c, _ = place()
        theirs = side_product(pairs_of, 1 - c, None, after)
        self.keep, self.send = side_product(
            pairs_of, c, to_core(theirs), after_more, groups
        )
        self.bit = 1

    def across(self, i):
        pairs = lax.axis_size(IT) // 2
        w = self.keep.shape[0]
        return [to_pair(self.send[i][(k - 1) * w : k * w], k) for k in range(1, pairs)]

    def take(self, got):
        for terms in zip(*[g[:-1] for g in got]):
            self.keep = self.keep + wide(jnp.concatenate(terms, axis=1))
        self.got = [g[-1] for g in got]

    def step(self, after=()):
        rows, z = lax.axis_size(RW), lax.axis_index(RW)
        pieces = rows // self.bit
        self.keep, self.sent = halve(self.keep, self.got, (z // self.bit) % 2, pieces, after)
        self.got = [to_bit(self.sent, self.bit)]
        self.bit *= 2
        return self.got

    def finish(self, after=()):
        while self.bit < lax.axis_size(RW):
            self.step(after)
        return self.keep + wide(self.got[0])


def scatter_small(parts):
    pairs, rows = lax.axis_size(IT) // 2, lax.axis_size(RW)
    x, c, z = place()
    n = parts.shape[1]
    cube = parts.reshape(pairs, 2, rows, n)
    cube = lax.dynamic_index_in_dim(cube, c, 1, keepdims=False) + to_core(
        lax.dynamic_index_in_dim(cube, 1 - c, 1, keepdims=False)
    )
    plane = lax.dynamic_index_in_dim(cube, x, 0, keepdims=False)
    for k in range(1, pairs):
        plane = plane + to_pair(
            lax.dynamic_index_in_dim(cube, (x + k) % pairs, 0, keepdims=False), k
        )
    bit = 1
    while bit < rows:
        both = plane.reshape(-1, 2, n)
        mine = (z // bit) % 2
        sent = to_bit(lax.dynamic_index_in_dim(both, 1 - mine, 1, keepdims=False), bit)
        plane = lax.dynamic_index_in_dim(both, mine, 1, keepdims=False) + sent
        bit *= 2
    return plane


def attend_kernel(q_ref, kv_ref, wr_ref, basis_ref, out_ref, p_ref):
    rows, seq, heads = q_ref.shape[0], kv_ref.shape[0], p_ref.shape[0]
    width = heads * KEY
    basis = basis_ref[...]
    outs = []
    for h in range(heads):
        qh = q_ref[:, h * KEY : (h + 1) * KEY]
        kh = kv_ref[:, h * KEY : (h + 1) * KEY]
        vh = kv_ref[:, width + h * VAL : width + (h + 1) * VAL]
        features = nt(qh, wr_ref[h * NB : (h + 1) * NB, :]).astype(LOW)
        table = nt(features, basis)
        rel = [
            pltpu.roll(
                table[:, k * 2 * rows : (k + 1) * 2 * rows], rows + 1, 1, stride=1, stride_axis=0
            )[:, :rows]
            for k in range(seq // rows)
        ]
        logits = nt(qh, kh) + jnp.concatenate(rel, axis=1)
        e = jnp.exp(logits - jnp.max(logits, axis=1, keepdims=True))
        p = (e * (1.0 / jnp.sum(e, axis=1, keepdims=True))).astype(LOW)
        p_ref[h] = p
        outs.append(nn(p, vh))
    out_ref[...] = jnp.concatenate(outs, axis=1).astype(LOW)


def attend_back_kernel(q_ref, kv_ref, wr_ref, basis_ref, p_ref, g_ref, dq_ref, dkv_ref, dwr_ref):
    rows, seq, heads = q_ref.shape[0], kv_ref.shape[0], p_ref.shape[0]
    width = heads * KEY
    basis = basis_ref[...]
    ii = lax.broadcasted_iota(jnp.int32, (rows, rows), 0)
    jj = lax.broadcasted_iota(jnp.int32, (rows, rows), 1)
    flip = (ii + jj == rows - 1).astype(F32).astype(LOW)
    dqs, dks, dvs = [], [], []
    for h in range(heads):
        qh = q_ref[:, h * KEY : (h + 1) * KEY]
        kh = kv_ref[:, h * KEY : (h + 1) * KEY]
        vh = kv_ref[:, width + h * VAL : width + (h + 1) * VAL]
        gh = g_ref[:, h * VAL : (h + 1) * VAL]
        wr = wr_ref[h * NB : (h + 1) * NB, :]
        p = p_ref[h]
        probs = p.astype(F32)
        dp = nt(gh, vh)
        inner = jnp.sum(probs * dp, axis=1, keepdims=True)
        ds = (probs * (dp - inner)).astype(LOW)
        dvs.append(tn(p, gh))
        dks.append(tn(ds, qh))
        rev = nn(flip, ds)
        zeros = jnp.zeros((rows, rows), F32)
        tabs = [
            pltpu.roll(
                jnp.concatenate([rev[:, k * rows : (k + 1) * rows], zeros], axis=1),
                0,
                1,
                stride=1,
                stride_axis=0,
            ).astype(LOW)
            for k in range(seq // rows)
        ]
        features = nn(jnp.concatenate(tabs, axis=1), basis).astype(LOW)
        features = nn(flip, features).astype(LOW)
        dqs.append(nn(ds, kh) + nn(features, wr))
        dwr_ref[h * NB : (h + 1) * NB, :] = tn(features, qh)
    dq = jnp.concatenate(dqs, axis=1).astype(LOW).astype(F32) * (KEY**-0.5)
    dq_ref[...] = dq.astype(LOW)
    dkv_ref[...] = jnp.concatenate(dks + dvs, axis=1).astype(LOW)


def run(body, grid, ins, outs, scratch=(), after=()):
    n, m = len(ins), len(after)

    def kernel(*refs):
        body(*refs[:n], *refs[n + m :])

    def spec(shape, index):
        if index is None:
            return pl.BlockSpec(memory_space=pltpu.SMEM)
        return pl.BlockSpec(shape, index)

    def whole(a):
        return (a, a.shape, lambda i: (0,) * a.ndim)

    full = [entry if isinstance(entry, tuple) else whole(entry) for entry in ins]
    out_full = [entry if isinstance(entry, tuple) else whole(entry) for entry in outs]
    return pl.pallas_call(
        kernel,
        grid=(grid,),
        in_specs=[spec(shape, index) for _, shape, index in full]
        + [pl.BlockSpec(memory_space=pl.ANY)] * m,
        out_specs=tuple(spec(shape, index) for _, shape, index in out_full),
        out_shape=tuple(a for a, _, _ in out_full),
        scratch_shapes=scratch,
        compiler_params=VMEM,
        cost_estimate=SHORT,
    )(*[a for a, _, _ in full], *after)


def new(shape, dtype):
    return jax.ShapeDtypeStruct(shape, dtype)


def ordered(head_ref, own, other):
    first = head_ref[0] == 0
    return jnp.concatenate([jnp.where(first, own, other), jnp.where(first, other, own)], axis=1)


def my_half(head_ref, a):
    n = a.shape[1] // 2
    first = head_ref[0] == 0
    return jnp.where(first, a[:, :n], a[:, n:]), jnp.where(first, a[:, n:], a[:, :n])


def project_kernel(rows, head_ref, *refs):
    own, other = refs[:rows], refs[rows : 2 * rows]
    gain_ref, bias_ref, qk_ref, v_ref, q_ref, kv_ref, normed_ref = refs[2 * rows :]
    width, kw = q_ref.shape
    for k in range(rows):
        x = ordered(head_ref, own[k][...].astype(F32), other[k][...].astype(F32))
        normed = (normalize(x)[0] * gain_ref[...] + bias_ref[...]).astype(LOW)
        at = slice(k * width, (k + 1) * width)
        normed_ref[at, :] = normed
        kv_ref[at, :kw] = nn(normed, qk_ref[:, kw:]).astype(LOW)
        kv_ref[at, kw:] = nn(normed, v_ref[...]).astype(LOW)
        if k == 0:
            q_ref[...] = (nn(normed, qk_ref[:, :kw]) * (KEY**-0.5)).astype(LOW)


def attend_out_kernel(q_ref, kv_ref, wr_ref, basis_ref, out_w_ref, out_ref, p_ref, part_ref):
    attend_kernel(q_ref, kv_ref, wr_ref, basis_ref, out_ref, p_ref)
    part_ref[...] = nt(out_ref[...], out_w_ref[...]).astype(LOW)


def ff_kernel(
    head_ref, own_ref, other_ref, p_ref, po_ref, gain_ref, bias_ref, b_up_ref, b_down_ref, up_ref, down_ref,
    hidden_ref, normed_ref, act_ref, slope_ref, mine_ref, send_ref, acc,
):
    step = pl.program_id(0)

    @pl.when(step == 0)
    def _():
        x = ordered(head_ref, own_ref[...].astype(F32), other_ref[...].astype(F32))
        hidden = x + (p_ref[...].astype(F32) + po_ref[...].astype(F32))
        hidden_ref[...] = hidden
        normed_ref[...] = (normalize(hidden)[0] * gain_ref[...] + bias_ref[...]).astype(LOW)
        acc[...] = hidden + b_down_ref[...]

    u = nn(normed_ref[...], up_ref[...]) + b_up_ref[...]
    t = jnp.tanh(G0 * (u + G1 * u * u * u))
    act = (0.5 * u * (1.0 + t)).astype(LOW)
    slope = 0.5 * (1.0 + t) + 0.5 * u * (1.0 - t * t) * (G0 * (1.0 + 3.0 * G1 * u * u))
    act_ref[...] = act
    slope_ref[...] = slope.astype(LOW)
    n = acc.shape[1] // 2
    part = nt(act, down_ref[...])
    mine, theirs = my_half(head_ref, part)

    @pl.when(step == 0)
    def _():
        mine_ref[...] = my_half(head_ref, acc[...])[0] + mine
        acc[:, :n] = theirs

    @pl.when(step > 0)
    def _():
        mine_ref[...] += mine
        acc[:, :n] += theirs

    @pl.when(step == pl.num_programs(0) - 1)
    def _():
        send_ref[...] = acc[:, :n].astype(LOW)


def ff_back_kernel(
    head_ref, own_ref, other_ref, slope_ref, up_ref, down_ref,
    grad_ref, pre_ref, part_ref, b_up_ref, b_down_ref, acc,
):
    step = pl.program_id(0)

    @pl.when(step == 0)
    def _():
        grad = ordered(head_ref, own_ref[...], other_ref[...])
        grad_ref[...] = grad
        b_down_ref[...] = jnp.sum(grad.astype(F32), axis=0, keepdims=True)
        acc[...] = jnp.zeros_like(acc)

    pre = (slope_ref[...].astype(F32) * nn(grad_ref[...], down_ref[...])).astype(LOW)
    pre_ref[...] = pre
    b_up_ref[...] = jnp.sum(pre.astype(F32), axis=0, keepdims=True)
    acc[...] += nt(pre, up_ref[...])

    @pl.when(step == pl.num_programs(0) - 1)
    def _():
        part_ref[...] = acc[...].astype(LOW)


def inner_back_kernel(
    head_ref, p_ref, po_ref, hidden_ref, grad_ref, trans_ref, gain_ref, out_w_ref,
    q_ref, kv_ref, wr_ref, basis_ref, probs_ref,
    proj_ref, resid_ref, gain_sum_ref, bias_sum_ref, dq_ref, dkv_ref, dwr_ref, attended,
):
    grad_normed = p_ref[...].astype(F32) + po_ref[...].astype(F32)
    hat, scale = normalize(hidden_ref[...])
    gain_sum_ref[...] = jnp.sum(grad_normed * hat, axis=0, keepdims=True)
    bias_sum_ref[...] = jnp.sum(grad_normed, axis=0, keepdims=True)
    through = norm_back(grad_normed, hat, scale, gain_ref[...])
    resid_ref[...] = trans_ref[...] + my_half(head_ref, through)[0]
    proj = (grad_ref[...].astype(F32) + through).astype(LOW)
    proj_ref[...] = proj
    attended[...] = nn(proj, out_w_ref[...]).astype(LOW)
    attend_back_kernel(
        q_ref, kv_ref, wr_ref, basis_ref, probs_ref, attended, dq_ref, dkv_ref, dwr_ref
    )


def point_back_kernel(head_ref, grad_ref, point_ref, mine_ref, send_ref, bias_ref):
    grad = grad_ref[...]
    bias_ref[...] = jnp.sum(grad[: grad.shape[0] - 16].astype(F32), axis=0, keepdims=True)
    mine, theirs = my_half(head_ref, nt(grad, point_ref[...]))
    mine_ref[...] = mine
    send_ref[...] = theirs.astype(LOW)


def before(a, edge):
    row = lax.broadcasted_iota(jnp.int32, a.shape, 0)
    return jnp.where(row == 0, edge, pltpu.roll(a, 1, 0))


def behind(a, edge):
    row = lax.broadcasted_iota(jnp.int32, a.shape, 0)
    return jnp.where(row == a.shape[0] - 1, edge, pltpu.roll(a, a.shape[0] - 1, 0))


def section_back_kernel(mine_ref, got_ref, tap0, tap1, tap2, gm_ref, low_ref, coarse_ref, bias_ref):
    n = coarse_ref.shape[0]
    gm = mine_ref[...] + got_ref[...].astype(F32)
    gm_ref[...] = gm[: 2 * n]
    even, odd = gm[:n], gm[n : 2 * n]
    prev, later = gm[2 * n : 2 * n + 1], gm[2 * n + 1 : 2 * n + 2]
    gs_even = tap0[...] * odd + tap1[...] * even + tap2[...] * before(odd, prev)
    gs_odd = tap0[...] * behind(even, later) + tap1[...] * odd + tap2[...] * even
    coarse_ref[...] = gs_even + gs_odd
    gs = jnp.concatenate([gs_even, gs_odd], axis=0).astype(LOW)
    low_ref[...] = gs
    bias_ref[...] = jnp.sum(gs.astype(F32), axis=0, keepdims=True)


def section_kernel(trans_ref, skip_ref, prev_ref, later_ref, gm_ref, tap0, tap1, tap2, mixed_ref, depth_ref):
    n = trans_ref.shape[0]
    coarse = gelu(trans_ref[...])
    s_even, s_odd = coarse + skip_ref[:n], coarse + skip_ref[n:]
    s_before, s_after = before(s_odd, prev_ref[...]), behind(s_even, later_ref[...])
    mixed_ref[:n] = (tap0[...] * s_before + tap1[...] * s_even + tap2[...] * s_odd).astype(LOW)
    mixed_ref[n:] = (tap0[...] * s_even + tap1[...] * s_odd + tap2[...] * s_after).astype(LOW)
    even, odd = gm_ref[:n], gm_ref[n:]
    for k, a, b in ((0, s_before, s_even), (1, s_even, s_odd), (2, s_odd, s_after)):
        depth_ref[k : k + 1] = jnp.sum(even * a + odd * b, axis=0, keepdims=True)


def project_back_kernel(rows, dq_ref, *refs):
    parts, (qk_ref, v_ref, out_ref) = refs[:rows], refs[rows:]
    kw = dq_ref.shape[1]
    dkv = parts[0][...].astype(F32)
    for k in range(1, rows):
        dkv = dkv + parts[k][...].astype(F32)
    dkv = dkv.astype(LOW)
    dqk = jnp.concatenate([dq_ref[...], dkv[:, :kw]], axis=1)
    out_ref[...] = (nt(dqk, qk_ref[...]) + nt(dkv[:, kw:], v_ref[...])).astype(LOW)


def outer_back_kernel(
    head_ref, own_ref, other_ref, p_ref, po_ref, gain_ref, resid_ref, grad_ref, gain_sum_ref, bias_sum_ref
):
    hat, scale = normalize(
        ordered(head_ref, own_ref[...].astype(F32), other_ref[...].astype(F32))
    )
    grad_normed = p_ref[...].astype(F32) + po_ref[...].astype(F32)
    gain_sum_ref[...] = jnp.sum(grad_normed * hat, axis=0, keepdims=True)
    bias_sum_ref[...] = jnp.sum(grad_normed, axis=0, keepdims=True)
    through = norm_back(grad_normed, hat, scale, gain_ref[...])
    grad_ref[...] = resid_ref[...] + my_half(head_ref, through)[0]


def position_windows(z, width, rows):
    seq = width * rows
    block = jnp.bitwise_xor(z, np.array(bit_order(rows), np.int32)) - z
    t = block[:, None] * width + (np.arange(2 * width) - (width - 1))[None, :]
    distance = t.reshape(-1).astype(F32)
    magnitude = jnp.abs(distance)[:, None]
    number = NB // 4
    steps_up = np.arange(number, dtype=np.float32)
    half_life = (3.0 * (seq / 3.0) ** (steps_up / max(number - 1, 1))).astype(np.float32)
    decays = jnp.exp(-0.6931471805599453 * magnitude / half_life)
    central = (2.0 ** (steps_up + 1.0) - 1.0 > magnitude).astype(F32)
    even = jnp.concatenate([decays, central], axis=1)
    return jnp.concatenate([even, jnp.sign(distance)[:, None] * even], axis=1).astype(LOW)


G0, G1 = 0.7978845608028654, 0.044715


def gelu(u):
    return 0.5 * u * (1.0 + jnp.tanh(G0 * (u + G1 * u * u * u)))


def gelu_slope(u):
    t = jnp.tanh(G0 * (u + G1 * u * u * u))
    return 0.5 * (1.0 + t) + 0.5 * u * (1.0 - t * t) * (G0 * (1.0 + 3.0 * G1 * u * u))


def normalize(values):
    centered = values - jnp.mean(values, axis=-1, keepdims=True)
    scale = lax.rsqrt(jnp.mean(centered * centered, axis=-1, keepdims=True) + EPS)
    return centered * scale, scale


def norm_back(grad, hat, scale, gain):
    gg = grad * gain
    return scale * (
        gg
        - jnp.mean(gg, axis=-1, keepdims=True)
        - hat * jnp.mean(gg * hat, axis=-1, keepdims=True)
    )


def pick(head, own, other):
    return jnp.where(head == 0, own, other), jnp.where(head == 0, other, own)


def both_halves(head, own, other):
    return jnp.concatenate(pick(head, own, other), axis=1)


def half(a, head):
    n = a.shape[1] // 2
    return lax.dynamic_slice_in_dim(a, head * n, n, 1)


def one_hot(select, height, width):
    ii = lax.broadcasted_iota(jnp.int32, (height, width), 0)
    jj = lax.broadcasted_iota(jnp.int32, (height, width), 1)
    return select(ii, jj).astype(LOW)


def from_before(row):
    n = lax.axis_size(RW)
    return lax.ppermute(row, RW, [(i, i + 1) for i in range(n - 1)])


def from_behind(row):
    n = lax.axis_size(RW)
    return lax.ppermute(row, RW, [(i + 1, i) for i in range(n - 1)])


def shards(
    inputs,
    skip_input,
    cotangent,
    track_mask,
    norm1_gain,
    norm1_bias,
    query_weight,
    key_weight,
    value_weight,
    rel_weight,
    out_weight,
    norm2_gain,
    norm2_bias,
    up_weight,
    up_bias,
    down_weight,
    down_bias,
    skip_weight,
    skip_bias,
    depth_weight,
    point_weight,
    point_bias,
):
    head = lax.axis_index(HD)
    _, _, z = place()
    rows = lax.axis_size(RW)
    group = lax.axis_size(IT) * rows
    width, chan = inputs.shape[1], inputs.shape[2]
    model = 2 * chan
    heads = rel_weight.shape[0]
    kw = heads * KEY
    shard = norm1_gain.shape[0]
    small = skip_bias.shape[1]
    rel_cols = rel_weight.shape[1]

    skip_rows = skip_weight.shape[0]
    flat = jnp.concatenate(
        [norm1_gain, norm1_bias, norm2_gain, norm2_bias, down_bias, up_bias[0]]
        + [skip_bias[0], depth_weight.reshape(-1), point_bias[0], rel_weight.reshape(-1)]
    ).astype(LOW)
    spare = shard - skip_rows
    flat = jnp.pad(flat, (0, spare * chan - flat.size)).reshape(spare, chan)
    ff = up_weight.shape[1]
    order = [up_weight, down_weight.T, out_weight.T, point_weight]
    order += [jnp.concatenate([skip_weight.astype(LOW), flat], axis=0)]
    order += [value_weight, query_weight, key_weight]
    piece = jnp.concatenate([w.astype(LOW) for w in order], axis=1)
    big = lax.all_gather(piece, (IT, RW), axis=0, tiled=True)
    at = 2 * ff

    def columns(start, count):
        return (big, (model, count), lambda i: (0, start // count))

    w_out, w_value = columns(at, chan), columns(at + 3 * chan, heads * VAL)
    w_qk = columns(at + 3 * chan + heads * VAL, 2 * kw)
    w_point = columns(at + chan, chan)
    steps = 3
    cut = ff // steps
    w_up = (big, (model, cut), lambda i: (0, i))
    w_down = (big, (model, cut), lambda i: (0, steps + i))
    last = big[:, at + 2 * chan : at + 3 * chan].reshape(group, shard, chan)
    w_skip = last[:, :skip_rows].reshape(group * skip_rows, chan)
    tails = last[:, skip_rows:].reshape(group, -1)

    def vector(start, count):
        return wide(tails[:, start : start + count]).reshape(1, -1)

    gain_one, bias_one, gain_two, bias_two, b_down, b_up = (
        vector(i * shard, shard) for i in range(6)
    )
    at = 6 * shard
    b_skip, tap0, tap1, tap2, b_point = (vector(at + i * small, small) for i in range(5))
    at += 5 * small
    w_rel = tails[:, at : at + heads * rel_cols].reshape(group, heads, rel_cols)
    w_rel = w_rel.transpose(1, 0, 2).reshape(heads * NB, KEY)

    at_head = (head.reshape(1).astype(jnp.int32), None, None)
    even = one_hot(lambda i, j: j == 2 * i, width, 2 * width)
    odd = one_hot(lambda i, j: j == 2 * i + 1, width, 2 * width)
    apart = jnp.concatenate([even, odd], axis=0)
    masked = (wide(cotangent[0]) * wide(track_mask)).astype(LOW)
    edges = [from_before(masked[-1:]), from_behind(masked[:1]), jnp.zeros((14, chan), LOW)]
    grad_out = nn(apart, masked).astype(LOW)
    grad_rows = jnp.concatenate([grad_out] + edges, axis=0)
    skip_low = nn(apart, gelu(wide(skip_input[0])).astype(LOW)).astype(LOW)

    own_blocks = [to_bit(inputs[0], k) if k else inputs[0] for k in bit_order(rows)]
    other_blocks = [to_head(b) for b in own_blocks]
    basis = position_windows(z, width, rows)
    queries, kv, normed_all = run(
        functools.partial(project_kernel, rows),
        1,
        [at_head] + own_blocks + other_blocks + [gain_one, bias_one, w_qk, w_value],
        [new((width, kw), LOW), new((rows * width, kw + heads * VAL), LOW)]
        + [new((rows * width, model), LOW)],
        after=[skip_low, grad_rows, basis],
    )
    attended, probs, partial_attn = run(
        attend_out_kernel,
        1,
        [queries, kv, w_rel, basis, w_out],
        [new((width, heads * VAL), LOW), new((heads, width, rows * width), LOW)]
        + [new((width, model), LOW)],
    )
    skip_term = nn(skip_low, w_skip) + b_skip
    gm_mine, gm_send, grad_point_bias = run(
        point_back_kernel,
        1,
        [at_head, grad_rows, w_point],
        [new((2 * width + 16, chan), F32), new((2 * width + 16, chan), LOW), new((1, chan), F32)],
        after=[partial_attn],
    )
    grad_mixed, grad_skip_low, grad_coarse, grad_skip_bias = run(
        section_back_kernel,
        1,
        [gm_mine, to_head(gm_send), tap0, tap1, tap2],
        [new((2 * width, chan), F32), new((2 * width, chan), LOW)]
        + [new((width, chan), F32), new((1, chan), F32)],
    )

    by_cut = (width, cut), lambda i: (0, i)
    hidden, normed_two, activated, slope, trans, send = run(
        ff_kernel,
        steps,
        [at_head, own_blocks[0], other_blocks[0], partial_attn, to_head(partial_attn)]
        + [gain_two, bias_two, (b_up, (1, cut), lambda i: (0, i)), b_down, w_up, w_down],
        [new((width, model), F32), new((width, model), LOW), (new((width, ff), LOW), *by_cut)]
        + [(new((width, ff), LOW), *by_cut), new((width, chan), F32), new((width, chan), LOW)],
        [pltpu.VMEM((width, model), F32)],
        after=[skip_term],
    )
    trans = trans + wide(to_head(send))

    for_skip = Scatter([(skip_low, grad_skip_low)])

    s_first = gelu(trans[:1]) + skip_term[:1]
    s_last = gelu(trans[-1:]) + skip_term[-1:]
    prev, later = wide(from_before(low(s_last))), wide(from_behind(low(s_first)))

    grad_trans = gelu_slope(trans) * grad_coarse
    grad_own = low(grad_trans)
    grad_ff_low, grad_pre_low, partial_two, grad_up_bias, grad_down_bias = run(
        ff_back_kernel,
        steps,
        [at_head, grad_own, to_head(grad_own), (slope, *by_cut), w_up, w_down],
        [new((width, model), LOW), (new((width, ff), LOW), *by_cut), new((width, model), LOW)]
        + [(new((1, ff), F32), (1, cut), lambda i: (0, i)), new((1, model), F32)],
        [pltpu.VMEM((width, model), F32)],
        after=[prev, later],
    )
    for_ff = Scatter([(grad_ff_low, activated), (normed_two, grad_pre_low)])
    grad_proj_low, resid, grad_gain_two, grad_bias_two, dq, dkv, grad_rel = run(
        inner_back_kernel,
        1,
        [at_head, partial_two, to_head(partial_two), hidden, grad_ff_low, grad_trans, gain_two]
        + [w_out, queries, kv, w_rel, basis, probs],
        [new((width, model), LOW), new((width, chan), F32)]
        + [new((1, model), F32), new((1, model), F32)]
        + [new(queries.shape, LOW), new(kv.shape, LOW), new(w_rel.shape, F32)],
        [pltpu.VMEM((width, heads * VAL), LOW)],
        after=for_ff.send + for_skip.send,
    )
    dkv_parts, rest, bit, arrived = [dkv[:width]], dkv, 1, []
    while bit < rows:
        n = rest.shape[0] // 2
        got = to_bit(rest[n:], bit)
        dkv_parts.append(got[:width])
        arrived.append(got)
        if n > width:
            rest = low(wide(rest[:n]) + wide(got))
            dkv_parts = [rest[:width]]
        bit *= 2
    ff_across, skip_across = [for_ff.across(0), for_ff.across(1)], [for_skip.across(0)]
    mixed, grad_depth = run(
        section_kernel,
        1,
        [trans, skip_term, prev, later, grad_mixed, tap0, tap1, tap2],
        [new((2 * width, chan), LOW), new((3, chan), F32)],
    )
    mixed_other = to_head(mixed)
    for_attn = Scatter(
        [(grad_proj_low, attended), (normed_all, dq), (normed_all, dkv)],
        arrived[:1] + ff_across[0] + ff_across[1] + [mixed_other],
        (),
        [[0], [1, 2]],
    )
    for_ff.take(ff_across)
    ff_along = for_ff.step(arrived[1:] + for_attn.send)
    (partial_one,) = run(
        functools.partial(project_back_kernel, len(dkv_parts)),
        1,
        [dq] + dkv_parts + [w_qk, w_value],
        [new((width, model), LOW)],
        after=skip_across[0] + for_attn.send + [mixed_other, for_ff.sent],
    )
    mixed_full = both_halves(head, mixed, mixed_other)
    for_point = Scatter([(mixed_full, grad_out)], [partial_one])
    for_skip.take(skip_across)
    attn_across = [for_attn.across(i) for i in range(2)]
    input_grad, grad_gain_one, grad_bias_one = run(
        outer_back_kernel,
        1,
        [at_head, own_blocks[0], other_blocks[0], partial_one, to_head(partial_one)]
        + [gain_one, resid],
        [new((width, chan), F32), new((1, model), F32), new((1, model), F32)],
        after=for_point.send + ff_along + attn_across[0] + attn_across[1],
    )
    input_grad = input_grad[None]
    for_attn.take(attn_across)
    for_point.take([for_point.across(0)])
    for_ff.step([partial_one])
    for_attn.step([for_ff.sent])
    for_skip.step([for_attn.sent])
    for_point.step([for_attn.sent])
    for_attn.step([for_ff.sent])
    for_skip.step([for_attn.sent])
    for_point.step([for_attn.sent])
    grad_skip, grad_ff = for_skip.finish(), for_ff.finish()
    grad_attn, grad_point = for_attn.finish(), for_point.finish()
    grad_out_w, grad_qkv = grad_attn[:, : heads * VAL], grad_attn[:, heads * VAL :]
    result = (nn(mixed_full, w_point[0][:, 2 * ff + chan : 2 * ff + 2 * chan]) + b_point).astype(LOW)
    block_output = tn(apart, result).astype(LOW)[None]
    grad_depth = [grad_depth[k] for k in range(3)]

    rel_parts = grad_rel.reshape(heads, group, rel_cols).transpose(1, 0, 2)
    parts = [grad_gain_one, grad_bias_one, grad_gain_two, grad_bias_two, grad_down_bias]
    parts += [grad_up_bias, grad_skip_bias] + grad_depth + [grad_point_bias]
    parts = jnp.concatenate([p.reshape(group, -1) for p in parts] + [rel_parts.reshape(group, -1)], axis=1)
    sums = scatter_small(parts)

    def own(start, count):
        return sums[0, start : start + count]

    at = 6 * shard
    return (
        block_output,
        input_grad,
        own(0, shard),
        own(shard, shard),
        grad_qkv[:, :kw],
        grad_qkv[:, kw : 2 * kw],
        grad_qkv[:, 2 * kw :],
        own(at + 5 * small, heads * rel_cols).reshape(heads, rel_cols),
        grad_out_w.T,
        own(2 * shard, shard),
        own(3 * shard, shard),
        grad_ff[:, ff:],
        own(5 * shard, shard)[None],
        grad_ff[:, :ff].T,
        own(4 * shard, shard),
        grad_skip,
        own(at, small)[None],
        own(at + small, 3 * small).reshape(3, 1, small),
        grad_point,
        own(at + 4 * small, small)[None],
    )


def solution(mesh):
    gr = (IT, RW)
    vec, cols, rws = P(gr), P(gr, HD), P(HD, gr)
    act = P(IT, RW, HD)
    taps = P(None, HD, gr)
    weights = (vec, vec, cols, cols, cols, rws, rws, vec, vec, cols, rws, rws, vec, cols, rws)
    weights += (taps, cols, rws)
    return jax.shard_map(
        shards,
        mesh=mesh,
        in_specs=(act, P(IT, RW, None), act, P(IT, HD)) + weights,
        out_specs=(act, act) + weights,
        check_vma=False,
    )
```

```python
import functools

import jax
import jax.numpy as jnp
import numpy as np
from jax import lax
from jax.experimental import pallas as pl
from jax.experimental.pallas import tpu as pltpu
from jax.sharding import PartitionSpec as P

KEY = 64
VAL = 192
NB = 32
EPS = 1e-05
IT, HD, RW = "items", "heads", "rows"
LOW = jnp.bfloat16
F32 = jnp.float32
VMEM = pltpu.CompilerParams(vmem_limit_bytes=56 * 2**20)
SHORT = pl.CostEstimate(flops=1, bytes_accessed=1, transcendentals=0)


def nn(a, b):
    return lax.dot_general(a, b, (((1,), (0,)), ((), ())), preferred_element_type=F32)


def nt(a, b):
    return lax.dot_general(a, b, (((1,), (1,)), ((), ())), preferred_element_type=F32)


def tn(a, b):
    return lax.dot_general(a, b, (((0,), (0,)), ((), ())), preferred_element_type=F32)


def wide(a):
    return a.astype(F32)


def low(a):
    return lax.reduce_precision(a, 8, 7).astype(LOW)


def bit_order(n):
    out, bit = [0], n // 2
    while bit:
        out += [i + bit for i in out]
        bit //= 2
    return out


def to_core(a):
    n = lax.axis_size(IT)
    return lax.ppermute(a, IT, [(i, i ^ 1) for i in range(n)])


def to_pair(a, k):
    n = lax.axis_size(IT)
    return lax.ppermute(a, IT, [(i, (i + 2 * k) % n) for i in range(n)])


def to_head(a):
    return lax.ppermute(a, HD, [(0, 1), (1, 0)])


def place():
    item = lax.axis_index(IT)
    return item // 2, item % 2, lax.axis_index(RW)


def to_bit(a, bit):
    n = lax.axis_size(RW)
    return lax.ppermute(a, RW, [(i, i ^ bit) for i in range(n)])


def halve(keep, got, pick_bit, pieces, after=()):
    w, n = keep.shape[0] // pieces, keep.shape[1]
    shape = (pieces // 2, 2, w, n)
    if w % 16:
        total = (keep + wide(jnp.concatenate(got, axis=1))).reshape(shape)
        mine = lax.dynamic_index_in_dim(total, pick_bit, 1, keepdims=False)
        send = lax.dynamic_index_in_dim(total, 1 - pick_bit, 1, keepdims=False)
        return mine.reshape(-1, n), low(send).reshape(-1, n)
    widths = [g.shape[1] for g in got]

    def body(bit_ref, keep_ref, *refs):
        got_refs, (mine_ref, send_ref) = refs[:-2], refs[-2:]

        def write(bit):
            at = 0
            for ref, count in zip(got_refs, widths):
                there = slice(at, at + count)
                at += count
                mine_ref[0, :, there] = keep_ref[0, bit, :, there] + ref[0, bit].astype(F32)
                total = keep_ref[0, 1 - bit, :, there] + ref[0, 1 - bit].astype(F32)
                send_ref[0, :, there] = total.astype(LOW)

        for bit in range(2):
            pl.when(bit_ref[0] == bit)(functools.partial(write, bit))

    def block(count):
        return (1, 2, w, count), lambda i: (i, 0, 0, 0)

    out = (1, w, n), lambda i: (i, 0, 0)
    half_shape = (pieces // 2, w, n)
    mine, send = run(
        body,
        pieces // 2,
        [(pick_bit.reshape(1), None, None), (keep.reshape(shape), *block(n))]
        + [(g.reshape(pieces // 2, 2, w, count), *block(count)) for g, count in zip(got, widths)],
        [(new(half_shape, F32), *out), (new(half_shape, LOW), *out)],
        after=after,
    )
    return mine.reshape(-1, n), send.reshape(-1, n)


def find(bounds, start, end):
    at = next(i for i, (a, b) in enumerate(bounds) if a <= start and end <= b)
    return at, slice(start - bounds[at][0], end - bounds[at][0])


def bounds_of(arrays):
    ends = [int(e) for e in np.cumsum([0] + [a.shape[1] for a in arrays])]
    return list(zip(ends, ends[1:]))


def spots_of(side, w):
    pairs = lax.axis_size(IT) // 2
    x, _, _ = place()
    return [(((x + k) % pairs) * 2 + side) for k in range(pairs)]


def fits(w):
    rows = lax.axis_size(RW)
    return lax.axis_size(IT) == 4 and w % 128 == 0 and (w // rows) % 16 == 0


def columns_product(spots_ref, left_ref, right, out_ref, there):
    count = spots_ref.shape[0]
    w = out_ref.shape[0] // count
    for k in range(count):
        start = pl.multiple_of(spots_ref[k] * w, 128)
        left = left_ref[pl.ds(0, right.shape[0]), pl.ds(start, w)]
        out_ref[k * w : (k + 1) * w, there] = tn(left, right).astype(LOW)


def side_product(pairs_of, side, got=None, after=(), groups=None, others=False):
    pairs = lax.axis_size(IT) // 2
    w = pairs_of[0][0].shape[1] // (2 * pairs)
    spots = spots_of(side, w)
    cols = [right.shape[1] for _, right in pairs_of]
    ends = [int(e) for e in np.cumsum([0] + cols)]
    groups = groups or [[k] for k in range(len(cols))]
    bounds = [(ends[g[0]], ends[g[-1] + 1]) for g in groups]
    if w % 128:
        out = []
        for left, right in pairs_of:
            part = [lax.dynamic_slice_in_dim(left, spot * w, w, 1) for spot in spots]
            out.append(tn(jnp.concatenate(part, axis=1)[: right.shape[0]], right))
        out = jnp.concatenate(out, axis=1)
        if got is None:
            return low(out)
        out = out + wide(jnp.concatenate(got, axis=1))
        return out[:w], [low(out[w:, i:j]) for i, j in bounds]
    n, count, m = sum(cols), len(pairs_of), len(after)
    first = int(others)
    got = got or []
    got_bounds = bounds_of(got)

    def body(spot_ref, *refs):
        lefts, rights = refs[:count], refs[count : 2 * count]
        gots = refs[2 * count : 2 * count + len(got)]
        outs = refs[2 * count + len(got) + m :]
        if others:
            outs = (None,) + tuple(outs)
        step = pl.program_id(0)
        for k in range(count):
            there = slice(ends[k], ends[k + 1])
            to = next(i for i, g in enumerate(groups) if k in g)
            inside = slice(ends[k] - bounds[to][0], ends[k + 1] - bounds[to][0])
            part = tn(lefts[k][...], rights[k][...])
            if not got:
                outs[0][:, there] = part.astype(LOW)
                continue
            which, where = find(got_bounds, ends[k], ends[k + 1])
            part = part + gots[which][:, where].astype(F32)

            if others:
                outs[1 + to][:, inside] = part.astype(LOW)
                continue

            @pl.when(step == 0)
            def _(part=part, there=there):
                outs[0][:, there] = part

            @pl.when(step > 0)
            def _(part=part, to=to, inside=inside):
                outs[1 + to][:, inside] = part.astype(LOW)

    specs = [
        pl.BlockSpec((right.shape[0], w), lambda i, spot: (0, spot[i])) for left, right in pairs_of
    ] + [pl.BlockSpec(right.shape, lambda i, spot: (0, 0)) for _, right in pairs_of]
    operands = [left for left, _ in pairs_of] + [right for _, right in pairs_of]
    specs += [pl.BlockSpec((w, g.shape[1]), lambda i, spot: (i + first, 0)) for g in got]
    operands += got
    if not got:
        out_specs = [pl.BlockSpec((w, n), lambda i, spot: (i, 0))]
        out_shape = [new((pairs * w, n), LOW)]
    else:
        out_specs, out_shape = [pl.BlockSpec((w, n), lambda i, spot: (0, 0))], [new((w, n), F32)]
        for c in [j - i for i, j in bounds]:
            out_specs.append(
                pl.BlockSpec((w, c), lambda i, spot: (jnp.maximum(i - 1 + first, 0), 0))
            )
            out_shape.append(new(((pairs - 1) * w, c), LOW))
        out_specs, out_shape = out_specs[first:], out_shape[first:]
    out = pl.pallas_call(
        body,
        grid_spec=pltpu.PrefetchScalarGridSpec(
            num_scalar_prefetch=1,
            grid=(pairs - first,),
            in_specs=specs + [pl.BlockSpec(memory_space=pl.ANY)] * m,
            out_specs=out_specs,
        ),
        out_shape=out_shape,
        compiler_params=VMEM,
        cost_estimate=SHORT,
    )(jnp.stack(spots[first:]).astype(jnp.int32), *operands, *after)
    if others:
        return list(out)
    return (out[0], list(out[1:])) if got else out[0]


def product_halve(pairs_of, spot, core, terms, pick_bit, pieces, after=()):
    w = pairs_of[0][0].shape[1] // (2 * (lax.axis_size(IT) // 2))
    cols = [right.shape[1] for _, right in pairs_of]
    ends = [int(e) for e in np.cumsum([0] + cols)]
    n, count, m = ends[-1], len(pairs_of), len(after)
    widths = [g.shape[1] for g in terms]
    piece = w // pieces
    core_bounds = bounds_of(core)

    def body(at_ref, *refs):
        lefts, rights = refs[:count], refs[count : 2 * count]
        at = 2 * count + len(core)
        core_refs, term_refs = refs[2 * count : at], refs[at : at + len(terms)]
        mine_ref, send_ref, total = refs[at + len(terms) + m :]
        for k in range(count):
            there = slice(ends[k], ends[k + 1])
            which, where = find(core_bounds, ends[k], ends[k + 1])
            part = core_refs[which][:, where].astype(F32)
            total[:, there] = tn(lefts[k][...], rights[k][...]) + part
        at = 0
        for ref, wide_n in zip(term_refs, widths):
            there = slice(at, at + wide_n)
            at += wide_n
            total[:, there] += ref[...].astype(F32)
        for i in range(pieces // 2):
            out = slice(i * piece, (i + 1) * piece)
            for bit in range(2):

                @pl.when(at_ref[1] == bit)
                def _(i=i, bit=bit, out=out):
                    mine = (2 * i + bit) * piece
                    send = (2 * i + 1 - bit) * piece
                    mine_ref[out] = total[mine : mine + piece]
                    send_ref[out] = total[send : send + piece].astype(LOW)

    in_specs = [
        pl.BlockSpec((right.shape[0], w), lambda i, at: (0, at[0])) for _, right in pairs_of
    ] + [pl.BlockSpec(right.shape, lambda i, at: (0, 0)) for _, right in pairs_of]
    in_specs += [pl.BlockSpec((w, g.shape[1]), lambda i, at: (0, 0)) for g in core]
    in_specs += [pl.BlockSpec(t.shape, lambda i, at: (0, 0)) for t in terms]
    out_spec = pl.BlockSpec((w // 2, n), lambda i, at: (0, 0))
    return pl.pallas_call(
        body,
        grid_spec=pltpu.PrefetchScalarGridSpec(
            num_scalar_prefetch=1,
            grid=(1,),
            in_specs=in_specs + [pl.BlockSpec(memory_space=pl.ANY)] * m,
            out_specs=[out_spec, out_spec],
            scratch_shapes=[pltpu.VMEM((w, n), F32)],
        ),
        out_shape=[new((w // 2, n), F32), new((w // 2, n), LOW)],
        compiler_params=VMEM,
        cost_estimate=SHORT,
    )(
        jnp.stack([spot, pick_bit]).astype(jnp.int32),
        *[left for left, _ in pairs_of],
        *[right for _, right in pairs_of],
        *core,
        *terms,
        *after,
    )


class Scatter:
    def __init__(self, pairs_of, theirs=None, after=(), after_more=(), groups=None):
        pairs = lax.axis_size(IT) // 2
        self.x, self.c, self.z = place()
        self.pairs_of, self.groups = pairs_of, groups
        self.plain = not fits(pairs_of[0][0].shape[1] // (2 * pairs))
        if theirs is None:
            theirs = [side_product(pairs_of, 1 - self.c, None, after)]
        self.theirs = theirs
        self.core = [to_core(t) for t in theirs]
        if self.plain:
            self.keep, self.send = side_product(pairs_of, self.c, self.core, after_more, groups)
        else:
            self.send = side_product(
                pairs_of, self.c, self.core, after_more, groups, others=True
            )
        self.bit = 1

    def across(self, i):
        pairs = lax.axis_size(IT) // 2
        w = self.send[i].shape[0] // (pairs - 1)
        return [to_pair(self.send[i][(k - 1) * w : k * w], k) for k in range(1, pairs)]

    def take(self, got):
        if self.plain:
            for terms in zip(*[g[:-1] for g in got]):
                self.keep = self.keep + wide(jnp.concatenate(terms, axis=1))
        self.got = [g[-1] for g in got]

    def step(self, after=()):
        pieces = lax.axis_size(RW) // self.bit
        pick_bit = (self.z // self.bit) % 2
        if self.bit == 1 and not self.plain:
            self.keep, self.sent = product_halve(
                self.pairs_of, self.x * 2 + self.c, self.core, self.got, pick_bit, pieces, after
            )
        else:
            self.keep, self.sent = halve(self.keep, self.got, pick_bit, pieces, after)
        self.got = [to_bit(self.sent, self.bit)]
        self.bit *= 2
        return self.got

    def finish(self, after=()):
        while self.bit < lax.axis_size(RW):
            self.step(after)
        return self.keep + wide(self.got[0])


def scatter_small(parts):
    pairs, rows = lax.axis_size(IT) // 2, lax.axis_size(RW)
    x, c, z = place()
    n = parts.shape[1]
    cube = parts.reshape(pairs, 2, rows, n)
    cube = lax.dynamic_index_in_dim(cube, c, 1, keepdims=False) + to_core(
        lax.dynamic_index_in_dim(cube, 1 - c, 1, keepdims=False)
    )
    plane = lax.dynamic_index_in_dim(cube, x, 0, keepdims=False)
    for k in range(1, pairs):
        plane = plane + to_pair(
            lax.dynamic_index_in_dim(cube, (x + k) % pairs, 0, keepdims=False), k
        )
    total = lax.dynamic_index_in_dim(plane, z, 0, keepdims=True)
    for k in range(1, rows):
        spot = jnp.bitwise_xor(z, k)
        total = total + to_bit(lax.dynamic_index_in_dim(plane, spot, 0, keepdims=True), k)
    return total


def attend_kernel(q_ref, kv_ref, wr_ref, basis_ref, out_ref, p_ref):
    rows, seq, heads = q_ref.shape[0], kv_ref.shape[0], p_ref.shape[0]
    width = heads * KEY
    basis = basis_ref[...]
    outs = []
    for h in range(heads):
        qh = q_ref[:, h * KEY : (h + 1) * KEY]
        kh = kv_ref[:, h * KEY : (h + 1) * KEY]
        vh = kv_ref[:, width + h * VAL : width + (h + 1) * VAL]
        features = nt(qh, wr_ref[h * NB : (h + 1) * NB, :].astype(LOW)).astype(LOW)
        table = nt(features, basis)
        rel = [
            pltpu.roll(
                table[:, k * 2 * rows : (k + 1) * 2 * rows], rows + 1, 1, stride=1, stride_axis=0
            )[:, :rows]
            for k in range(seq // rows)
        ]
        logits = nt(qh, kh) + jnp.concatenate(rel, axis=1)
        e = jnp.exp(logits - jnp.max(logits, axis=1, keepdims=True))
        p = (e * (1.0 / jnp.sum(e, axis=1, keepdims=True))).astype(LOW)
        p_ref[h] = p
        outs.append(nn(p, vh))
    out_ref[...] = jnp.concatenate(outs, axis=1).astype(LOW)


def attend_back_kernel(q_ref, kv_ref, wr_ref, basis_ref, p_ref, g_ref, dq_ref, dkv_ref, dwr_ref):
    rows, seq, heads = q_ref.shape[0], kv_ref.shape[0], p_ref.shape[0]
    width = heads * KEY
    basis = basis_ref[...]
    ii = lax.broadcasted_iota(jnp.int32, (rows, rows), 0)
    jj = lax.broadcasted_iota(jnp.int32, (rows, rows), 1)
    flip = (ii + jj == rows - 1).astype(F32).astype(LOW)
    dqs, dks, dvs = [], [], []
    for h in range(heads):
        qh = q_ref[:, h * KEY : (h + 1) * KEY]
        kh = kv_ref[:, h * KEY : (h + 1) * KEY]
        vh = kv_ref[:, width + h * VAL : width + (h + 1) * VAL]
        gh = g_ref[:, h * VAL : (h + 1) * VAL]
        wr = wr_ref[h * NB : (h + 1) * NB, :].astype(LOW)
        p = p_ref[h]
        probs = p.astype(F32)
        dp = nt(gh, vh)
        inner = jnp.sum(probs * dp, axis=1, keepdims=True)
        ds = (probs * (dp - inner)).astype(LOW)
        dvs.append(tn(p, gh))
        dks.append(tn(ds, qh))
        rev = nn(flip, ds)
        zeros = jnp.zeros((rows, rows), F32)
        tabs = [
            pltpu.roll(
                jnp.concatenate([rev[:, k * rows : (k + 1) * rows], zeros], axis=1),
                0,
                1,
                stride=1,
                stride_axis=0,
            ).astype(LOW)
            for k in range(seq // rows)
        ]
        features = nn(jnp.concatenate(tabs, axis=1), basis).astype(LOW)
        features = nn(flip, features).astype(LOW)
        dqs.append(nn(ds, kh) + nn(features, wr))
        dwr_ref[h * NB : (h + 1) * NB, :] = tn(features, qh)
    dq = jnp.concatenate(dqs, axis=1).astype(LOW).astype(F32) * (KEY**-0.5)
    dq_ref[...] = dq.astype(LOW)
    dkv_ref[...] = jnp.concatenate(dks + dvs, axis=1).astype(LOW)


def run(body, grid, ins, outs, scratch=(), after=()):
    n, m = len(ins), len(after)

    def kernel(*refs):
        body(*refs[:n], *refs[n + m :])

    def spec(shape, index):
        if index is None:
            return pl.BlockSpec(memory_space=pltpu.SMEM)
        return pl.BlockSpec(shape, index)

    def whole(a):
        return (a, a.shape, lambda i: (0,) * a.ndim)

    full = [entry if isinstance(entry, tuple) else whole(entry) for entry in ins]
    out_full = [entry if isinstance(entry, tuple) else whole(entry) for entry in outs]
    return pl.pallas_call(
        kernel,
        grid=(grid,),
        in_specs=[spec(shape, index) for _, shape, index in full]
        + [pl.BlockSpec(memory_space=pl.ANY)] * m,
        out_specs=tuple(spec(shape, index) for _, shape, index in out_full),
        out_shape=tuple(a for a, _, _ in out_full),
        scratch_shapes=scratch,
        compiler_params=VMEM,
        cost_estimate=SHORT,
    )(*[a for a, _, _ in full], *after)


def new(shape, dtype):
    return jax.ShapeDtypeStruct(shape, dtype)


def ordered(head_ref, own, other):
    first = head_ref[0] == 0
    return jnp.concatenate([jnp.where(first, own, other), jnp.where(first, other, own)], axis=1)


def my_half(head_ref, a):
    n = a.shape[1] // 2
    first = head_ref[0] == 0
    return jnp.where(first, a[:, :n], a[:, n:]), jnp.where(first, a[:, n:], a[:, :n])


def pack_kernel(count, *refs):
    out_ref, rows_ref = refs[-2:]
    rows, height = rows_ref.shape[0], out_ref.shape[0]
    at = 0
    for ref in refs[:count]:
        there = slice(at, at + ref.shape[1])
        at += ref.shape[1]
        out_ref[: ref.shape[0], there] = ref[...].astype(LOW)
        if ref.shape[0] < height:
            below = there
    rows_ref[...] = jnp.zeros_like(rows_ref)
    spot, width = 0, rows_ref.shape[1]
    for ref in refs[count:-2]:
        for i in range(ref.shape[0]):
            done, n = 0, ref.shape[1]
            while done < n:
                row, col = divmod(spot, width)
                part = min(n - done, width - col)
                rows_ref[row : row + 1, col : col + part] = ref[i : i + 1, done : done + part]
                done, spot = done + part, spot + part
    out_ref[height - rows :, below] = rows_ref[...].astype(LOW)


def unpack_kernel(shard, skip_rows, lengths, last_ref, skip_ref, rel_ref, *outs):
    group = last_ref.shape[0] // shard
    heads = rel_ref.shape[0] // NB
    width = last_ref.shape[1]
    for g in range(group):
        start = g * shard
        skip_ref[g * skip_rows : (g + 1) * skip_rows] = last_ref[start : start + skip_rows]
        rows = last_ref[start + skip_rows : start + shard].astype(F32)

        def piece(spot, n):
            parts, done = [], 0
            while done < n:
                row, col = divmod(spot + done, width)
                part = min(n - done, width - col)
                parts.append(rows[row : row + 1, col : col + part])
                done += part
            return parts[0] if len(parts) == 1 else jnp.concatenate(parts, axis=1)

        spot = 0
        for n, out in zip(lengths, outs):
            out[:, g * n : (g + 1) * n] = piece(spot, n)
            spot += n
        each = NB // group
        for h in range(heads):
            for j in range(each):
                row = h * NB + g * each + j
                rel_ref[row : row + 1] = piece(spot, KEY)
                spot += KEY


def project_kernel(rows, head_ref, *refs):
    own, other = refs[:rows], refs[rows : 2 * rows]
    gain_ref, bias_ref, qk_ref, v_ref, q_ref, kv_ref, normed_ref = refs[2 * rows :]
    width, kw = q_ref.shape
    for k in range(rows):
        x = ordered(head_ref, own[k][...].astype(F32), other[k][...].astype(F32))
        normed = (normalize(x)[0] * gain_ref[...] + bias_ref[...]).astype(LOW)
        at = slice(k * width, (k + 1) * width)
        normed_ref[at, :] = normed
        kv_ref[at, :kw] = nn(normed, qk_ref[:, kw:]).astype(LOW)
        kv_ref[at, kw:] = nn(normed, v_ref[...]).astype(LOW)
        if k == 0:
            q_ref[...] = (nn(normed, qk_ref[:, :kw]) * (KEY**-0.5)).astype(LOW)


def attend_out_kernel(q_ref, kv_ref, wr_ref, basis_ref, out_w_ref, out_ref, p_ref, part_ref):
    attend_kernel(q_ref, kv_ref, wr_ref, basis_ref, out_ref, p_ref)
    part_ref[...] = nt(out_ref[...], out_w_ref[...]).astype(LOW)


def ff_kernel(
    head_ref, own_ref, other_ref, p_ref, po_ref, gain_ref, bias_ref, b_up_ref, b_down_ref, up_ref, down_ref,
    hidden_ref, normed_ref, act_ref, slope_ref, mine_ref, send_ref, acc,
):
    step = pl.program_id(0)

    @pl.when(step == 0)
    def _():
        x = ordered(head_ref, own_ref[...].astype(F32), other_ref[...].astype(F32))
        hidden = x + (p_ref[...].astype(F32) + po_ref[...].astype(F32))
        hidden_ref[...] = hidden
        normed_ref[...] = (normalize(hidden)[0] * gain_ref[...] + bias_ref[...]).astype(LOW)
        acc[...] = hidden + b_down_ref[...]

    u = nn(normed_ref[...], up_ref[...]) + b_up_ref[...]
    t = jnp.tanh(G0 * (u + G1 * u * u * u))
    act = (0.5 * u * (1.0 + t)).astype(LOW)
    slope = 0.5 * (1.0 + t) + 0.5 * u * (1.0 - t * t) * (G0 * (1.0 + 3.0 * G1 * u * u))
    act_ref[...] = act
    slope_ref[...] = slope.astype(LOW)
    n = acc.shape[1] // 2
    part = nt(act, down_ref[...])
    mine, theirs = my_half(head_ref, part)

    @pl.when(step == 0)
    def _():
        mine_ref[...] = my_half(head_ref, acc[...])[0] + mine
        acc[:, :n] = theirs

    @pl.when(step > 0)
    def _():
        mine_ref[...] += mine
        acc[:, :n] += theirs

    @pl.when(step == pl.num_programs(0) - 1)
    def _():
        send_ref[...] = acc[:, :n].astype(LOW)


def ff_back_kernel(
    head_ref, own_ref, other_ref, slope_ref, up_ref, down_ref, *refs
):
    normed_ref, act_ref = refs[:2]
    grad_ref, pre_ref, part_ref, b_up_ref, b_down_ref = refs[2:7]
    step, acc = pl.program_id(0), refs[-1]

    @pl.when(step == 0)
    def _():
        grad = ordered(head_ref, own_ref[...], other_ref[...])
        grad_ref[...] = grad
        b_down_ref[...] = jnp.sum(grad.astype(F32), axis=0, keepdims=True)
        acc[...] = jnp.zeros_like(acc)

    pre = (slope_ref[...].astype(F32) * nn(grad_ref[...], down_ref[...])).astype(LOW)
    pre_ref[...] = pre
    b_up_ref[...] = jnp.sum(pre.astype(F32), axis=0, keepdims=True)
    acc[...] += nt(pre, up_ref[...])
    refs[7][...] = tn(grad_ref[...], act_ref[...]).astype(LOW)
    refs[8][...] = tn(normed_ref[...], pre).astype(LOW)

    @pl.when(step == pl.num_programs(0) - 1)
    def _():
        part_ref[...] = acc[...].astype(LOW)


def inner_back_kernel(
    fused, head_ref, p_ref, po_ref, hidden_ref, grad_ref, trans_ref, gain_ref, out_w_ref,
    q_ref, kv_ref, wr_ref, basis_ref, probs_ref, *refs
):
    spots_ref, normed_ref, out_ref = refs[:3] if fused else (None, None, None)
    outs = refs[3 * fused :]
    proj_ref, resid_ref, gain_sum_ref, bias_sum_ref, dq_ref, dkv_ref, dwr_ref = outs[:7]
    attended = outs[-1]
    grad_normed = p_ref[...].astype(F32) + po_ref[...].astype(F32)
    hat, scale = normalize(hidden_ref[...])
    gain_sum_ref[...] = jnp.sum(grad_normed * hat, axis=0, keepdims=True)
    bias_sum_ref[...] = jnp.sum(grad_normed, axis=0, keepdims=True)
    through = norm_back(grad_normed, hat, scale, gain_ref[...])
    resid_ref[...] = trans_ref[...] + my_half(head_ref, through)[0]
    proj = (grad_ref[...].astype(F32) + through).astype(LOW)
    proj_ref[...] = proj
    attended[...] = nn(proj, out_w_ref[...]).astype(LOW)
    attend_back_kernel(
        q_ref, kv_ref, wr_ref, basis_ref, probs_ref, attended, dq_ref, dkv_ref, dwr_ref
    )
    if fused:
        kw = dq_ref.shape[1]
        columns_product(spots_ref, proj_ref, out_ref[...], outs[7], slice(None))
        columns_product(spots_ref, normed_ref, dq_ref[...], outs[8], slice(0, kw))
        columns_product(spots_ref, normed_ref, dkv_ref[...], outs[8], slice(kw, None))


def point_back_kernel(head_ref, grad_ref, point_ref, mine_ref, send_ref, bias_ref):
    grad = grad_ref[...]
    bias_ref[...] = jnp.sum(grad[: grad.shape[0] - 16].astype(F32), axis=0, keepdims=True)
    mine, theirs = my_half(head_ref, nt(grad, point_ref[...]))
    mine_ref[...] = mine
    send_ref[...] = theirs.astype(LOW)


def before(a, edge):
    row = lax.broadcasted_iota(jnp.int32, a.shape, 0)
    return jnp.where(row == 0, edge, pltpu.roll(a, 1, 0))


def behind(a, edge):
    row = lax.broadcasted_iota(jnp.int32, a.shape, 0)
    return jnp.where(row == a.shape[0] - 1, edge, pltpu.roll(a, a.shape[0] - 1, 0))


def section_back_kernel(mine_ref, got_ref, tap0, tap1, tap2, gm_ref, low_ref, coarse_ref, bias_ref):
    n = coarse_ref.shape[0]
    gm = mine_ref[...] + got_ref[...].astype(F32)
    gm_ref[...] = gm[: 2 * n]
    even, odd = gm[:n], gm[n : 2 * n]
    prev, later = gm[2 * n : 2 * n + 1], gm[2 * n + 1 : 2 * n + 2]
    gs_even = tap0[...] * odd + tap1[...] * even + tap2[...] * before(odd, prev)
    gs_odd = tap0[...] * behind(even, later) + tap1[...] * odd + tap2[...] * even
    coarse_ref[...] = gs_even + gs_odd
    gs = jnp.concatenate([gs_even, gs_odd], axis=0).astype(LOW)
    low_ref[...] = gs
    bias_ref[...] = jnp.sum(gs.astype(F32), axis=0, keepdims=True)


def section_kernel(trans_ref, skip_ref, prev_ref, later_ref, gm_ref, tap0, tap1, tap2, mixed_ref, depth_ref):
    n = trans_ref.shape[0]
    coarse = gelu(trans_ref[...])
    s_even, s_odd = coarse + skip_ref[:n], coarse + skip_ref[n:]
    s_before, s_after = before(s_odd, prev_ref[...]), behind(s_even, later_ref[...])
    mixed_ref[:n] = (tap0[...] * s_before + tap1[...] * s_even + tap2[...] * s_odd).astype(LOW)
    mixed_ref[n:] = (tap0[...] * s_even + tap1[...] * s_odd + tap2[...] * s_after).astype(LOW)
    even, odd = gm_ref[:n], gm_ref[n:]
    for k, a, b in ((0, s_before, s_even), (1, s_even, s_odd), (2, s_odd, s_after)):
        depth_ref[k : k + 1] = jnp.sum(even * a + odd * b, axis=0, keepdims=True)


def project_back_kernel(rows, dq_ref, *refs):
    parts, (qk_ref, v_ref, out_ref) = refs[:rows], refs[rows:]
    kw = dq_ref.shape[1]
    dkv = parts[0][...].astype(F32)
    for k in range(1, rows):
        dkv = dkv + parts[k][...].astype(F32)
    dkv = dkv.astype(LOW)
    dqk = jnp.concatenate([dq_ref[...], dkv[:, :kw]], axis=1)
    out_ref[...] = (nt(dqk, qk_ref[...]) + nt(dkv[:, kw:], v_ref[...])).astype(LOW)


def outer_back_kernel(
    head_ref, own_ref, other_ref, p_ref, po_ref, gain_ref, resid_ref, grad_ref, gain_sum_ref, bias_sum_ref
):
    hat, scale = normalize(
        ordered(head_ref, own_ref[...].astype(F32), other_ref[...].astype(F32))
    )
    grad_normed = p_ref[...].astype(F32) + po_ref[...].astype(F32)
    gain_sum_ref[...] = jnp.sum(grad_normed * hat, axis=0, keepdims=True)
    bias_sum_ref[...] = jnp.sum(grad_normed, axis=0, keepdims=True)
    through = norm_back(grad_normed, hat, scale, gain_ref[...])
    grad_ref[...] = resid_ref[...] + my_half(head_ref, through)[0]


def position_windows(z, width, rows):
    seq = width * rows
    block = jnp.bitwise_xor(z, np.array(bit_order(rows), np.int32)) - z
    t = block[:, None] * width + (np.arange(2 * width) - (width - 1))[None, :]
    distance = t.reshape(-1).astype(F32)
    magnitude = jnp.abs(distance)[:, None]
    number = NB // 4
    steps_up = np.arange(number, dtype=np.float32)
    half_life = (3.0 * (seq / 3.0) ** (steps_up / max(number - 1, 1))).astype(np.float32)
    decays = jnp.exp(-0.6931471805599453 * magnitude / half_life)
    central = (2.0 ** (steps_up + 1.0) - 1.0 > magnitude).astype(F32)
    even = jnp.concatenate([decays, central], axis=1)
    return jnp.concatenate([even, jnp.sign(distance)[:, None] * even], axis=1).astype(LOW)


G0, G1 = 0.7978845608028654, 0.044715


def gelu(u):
    return 0.5 * u * (1.0 + jnp.tanh(G0 * (u + G1 * u * u * u)))


def gelu_slope(u):
    t = jnp.tanh(G0 * (u + G1 * u * u * u))
    return 0.5 * (1.0 + t) + 0.5 * u * (1.0 - t * t) * (G0 * (1.0 + 3.0 * G1 * u * u))


def normalize(values):
    centered = values - jnp.mean(values, axis=-1, keepdims=True)
    scale = lax.rsqrt(jnp.mean(centered * centered, axis=-1, keepdims=True) + EPS)
    return centered * scale, scale


def norm_back(grad, hat, scale, gain):
    gg = grad * gain
    return scale * (
        gg
        - jnp.mean(gg, axis=-1, keepdims=True)
        - hat * jnp.mean(gg * hat, axis=-1, keepdims=True)
    )


def pick(head, own, other):
    return jnp.where(head == 0, own, other), jnp.where(head == 0, other, own)


def both_halves(head, own, other):
    return jnp.concatenate(pick(head, own, other), axis=1)


def half(a, head):
    n = a.shape[1] // 2
    return lax.dynamic_slice_in_dim(a, head * n, n, 1)


def one_hot(select, height, width):
    ii = lax.broadcasted_iota(jnp.int32, (height, width), 0)
    jj = lax.broadcasted_iota(jnp.int32, (height, width), 1)
    return select(ii, jj).astype(LOW)


def from_before(row):
    n = lax.axis_size(RW)
    return lax.ppermute(row, RW, [(i, i + 1) for i in range(n - 1)])


def from_behind(row):
    n = lax.axis_size(RW)
    return lax.ppermute(row, RW, [(i + 1, i) for i in range(n - 1)])


def shards(
    inputs,
    skip_input,
    cotangent,
    track_mask,
    norm1_gain,
    norm1_bias,
    query_weight,
    key_weight,
    value_weight,
    rel_weight,
    out_weight,
    norm2_gain,
    norm2_bias,
    up_weight,
    up_bias,
    down_weight,
    down_bias,
    skip_weight,
    skip_bias,
    depth_weight,
    point_weight,
    point_bias,
):
    head = lax.axis_index(HD)
    _, _, z = place()
    rows = lax.axis_size(RW)
    group = lax.axis_size(IT) * rows
    width, chan = inputs.shape[1], inputs.shape[2]
    model = 2 * chan
    heads = rel_weight.shape[0]
    kw = heads * KEY
    shard = norm1_gain.shape[0]
    small = skip_bias.shape[1]
    rel_cols = rel_weight.shape[1]

    skip_rows = skip_weight.shape[0]
    flat = jnp.concatenate(
        [norm1_gain, norm1_bias, norm2_gain, norm2_bias, down_bias, up_bias[0]]
        + [skip_bias[0], depth_weight.reshape(-1), point_bias[0], rel_weight.reshape(-1)]
    ).astype(LOW)
    spare = shard - skip_rows
    singles = [norm1_gain, norm1_bias, norm2_gain, norm2_bias, down_bias, up_bias]
    singles += [skip_bias, depth_weight, point_bias, rel_weight]
    flat = jnp.pad(flat, (0, spare * chan - flat.size)).reshape(spare, chan)
    ff = up_weight.shape[1]
    order = [up_weight, down_weight.T, out_weight.T, point_weight]
    order += [jnp.concatenate([skip_weight.astype(LOW), flat], axis=0)]
    order += [value_weight, query_weight, key_weight]
    if shard % 16 == 0 and skip_rows % 16 == 0 and spare == 16:
        order[4] = skip_weight
        singles = [v.reshape(-1, v.shape[-1]) for v in singles]
        (piece,) = run(
            functools.partial(pack_kernel, len(order)),
            1,
            order + singles,
            [new((shard, sum(w.shape[1] for w in order)), LOW)],
            [pltpu.VMEM((spare, chan), F32)],
        )
    else:
        piece = jnp.concatenate([w.astype(LOW) for w in order], axis=1)
    big = lax.all_gather(piece, (IT, RW), axis=0, tiled=True)
    at = 2 * ff

    def columns(start, count):
        return (big, (model, count), lambda i: (0, start // count))

    w_out, w_value = columns(at, chan), columns(at + 3 * chan, heads * VAL)
    w_qk = columns(at + 3 * chan + heads * VAL, 2 * kw)
    w_point = columns(at + chan, chan)
    steps = 3
    cut = ff // steps
    w_up = (big, (model, cut), lambda i: (0, i))
    w_down = (big, (model, cut), lambda i: (0, steps + i))
    if shard % 16 == 0 and skip_rows % 16 == 0 and spare == 16 and NB % group == 0:
        lengths = [shard] * 6 + [small] * 5
        w_skip, w_rel, *singles = run(
            functools.partial(unpack_kernel, shard, skip_rows, lengths),
            1,
            [columns(at + 2 * chan, chan)],
            [new((group * skip_rows, chan), LOW), new((heads * NB, KEY), F32)]
            + [new((1, group * n), F32) for n in lengths],
        )
        gain_one, bias_one, gain_two, bias_two, b_down, b_up = singles[:6]
        b_skip, tap0, tap1, tap2, b_point = singles[6:]
    else:
        last = big[:, at + 2 * chan : at + 3 * chan].reshape(group, shard, chan)
        w_skip = last[:, :skip_rows].reshape(group * skip_rows, chan)
        tails = last[:, skip_rows:].reshape(group, -1)

        def vector(start, count):
            return wide(tails[:, start : start + count]).reshape(1, -1)

        gain_one, bias_one, gain_two, bias_two, b_down, b_up = (
            vector(i * shard, shard) for i in range(6)
        )
        at = 6 * shard
        b_skip, tap0, tap1, tap2, b_point = (vector(at + i * small, small) for i in range(5))
        at += 5 * small
        w_rel = tails[:, at : at + heads * rel_cols].reshape(group, heads, rel_cols)
        w_rel = w_rel.transpose(1, 0, 2).reshape(heads * NB, KEY)

    at_head = (head.reshape(1).astype(jnp.int32), None, None)
    even = one_hot(lambda i, j: j == 2 * i, width, 2 * width)
    odd = one_hot(lambda i, j: j == 2 * i + 1, width, 2 * width)
    apart = jnp.concatenate([even, odd], axis=0)
    masked = (wide(cotangent[0]) * wide(track_mask)).astype(LOW)
    edges = [from_before(masked[-1:]), from_behind(masked[:1]), jnp.zeros((14, chan), LOW)]
    grad_out = nn(apart, masked).astype(LOW)
    grad_rows = jnp.concatenate([grad_out] + edges, axis=0)
    skip_low = nn(apart, gelu(wide(skip_input[0])).astype(LOW)).astype(LOW)

    own_blocks = [to_bit(inputs[0], k) if k else inputs[0] for k in bit_order(rows)]
    other_blocks = [to_head(b) for b in own_blocks]
    basis = position_windows(z, width, rows)
    queries, kv, normed_all = run(
        functools.partial(project_kernel, rows),
        1,
        [at_head] + own_blocks + other_blocks + [gain_one, bias_one, w_qk, w_value],
        [new((width, kw), LOW), new((rows * width, kw + heads * VAL), LOW)]
        + [new((rows * width, model), LOW)],
        after=[skip_low, grad_rows, basis],
    )
    attended, probs, partial_attn = run(
        attend_out_kernel,
        1,
        [queries, kv, w_rel, basis, w_out],
        [new((width, heads * VAL), LOW), new((heads, width, rows * width), LOW)]
        + [new((width, model), LOW)],
    )
    skip_term = nn(skip_low, w_skip) + b_skip
    gm_mine, gm_send, grad_point_bias = run(
        point_back_kernel,
        1,
        [at_head, grad_rows, w_point],
        [new((2 * width + 16, chan), F32), new((2 * width + 16, chan), LOW), new((1, chan), F32)],
        after=[partial_attn],
    )
    grad_mixed, grad_skip_low, grad_coarse, grad_skip_bias = run(
        section_back_kernel,
        1,
        [gm_mine, to_head(gm_send), tap0, tap1, tap2],
        [new((2 * width, chan), F32), new((2 * width, chan), LOW)]
        + [new((width, chan), F32), new((1, chan), F32)],
    )

    by_cut = (width, cut), lambda i: (0, i)
    hidden, normed_two, activated, slope, trans, send = run(
        ff_kernel,
        steps,
        [at_head, own_blocks[0], other_blocks[0], partial_attn, to_head(partial_attn)]
        + [gain_two, bias_two, (b_up, (1, cut), lambda i: (0, i)), b_down, w_up, w_down],
        [new((width, model), F32), new((width, model), LOW), (new((width, ff), LOW), *by_cut)]
        + [(new((width, ff), LOW), *by_cut), new((width, chan), F32), new((width, chan), LOW)],
        [pltpu.VMEM((width, model), F32)],
        after=[skip_term],
    )
    trans = trans + wide(to_head(send))

    for_skip = Scatter([(skip_low, grad_skip_low)])

    s_first = gelu(trans[:1]) + skip_term[:1]
    s_last = gelu(trans[-1:]) + skip_term[-1:]
    prev, later = wide(from_before(low(s_last))), wide(from_behind(low(s_first)))

    grad_trans = gelu_slope(trans) * grad_coarse
    grad_own = low(grad_trans)
    owned = model // lax.axis_size(IT)
    fused = fits(owned)
    core_rows = model // 2
    spots = jnp.stack(spots_of(1 - place()[1], owned)).astype(jnp.int32), None, None
    extra = new((model, ff), LOW), (model, cut), lambda i: (0, i)
    grad_ff_low, grad_pre_low, partial_two, grad_up_bias, grad_down_bias, *theirs = run(
        ff_back_kernel,
        steps,
        [at_head, grad_own, to_head(grad_own), (slope, *by_cut), w_up, w_down]
        + [normed_two, (activated, *by_cut)],
        [new((width, model), LOW), (new((width, ff), LOW), *by_cut), new((width, model), LOW)]
        + [(new((1, ff), F32), (1, cut), lambda i: (0, i)), new((1, model), F32)]
        + [extra, extra],
        [pltpu.VMEM((width, model), F32)],
        after=[prev, later],
    )
    grad_down, grad_up = (
        lax.psum_scatter(t, (IT, RW), scatter_dimension=0, tiled=True) for t in theirs
    )
    mixed, grad_depth = run(
        section_kernel,
        1,
        [trans, skip_term, prev, later, grad_mixed, tap0, tap1, tap2],
        [new((2 * width, chan), LOW), new((3, chan), F32)],
    )
    grad_proj_low, resid, grad_gain_two, grad_bias_two, dq, dkv, grad_rel, *theirs = run(
        functools.partial(inner_back_kernel, fused),
        1,
        [at_head, partial_two, to_head(partial_two), hidden, grad_ff_low, grad_trans, gain_two]
        + [w_out, queries, kv, w_rel, basis, probs]
        + [spots, normed_all, attended][: 3 * fused],
        [new((width, model), LOW), new((width, chan), F32)]
        + [new((1, model), F32), new((1, model), F32)]
        + [new(queries.shape, LOW), new(kv.shape, LOW), new(w_rel.shape, F32)]
        + [new((core_rows, heads * VAL), LOW), new((core_rows, kw + kv.shape[1]), LOW)][: 2 * fused],
        [pltpu.VMEM((width, heads * VAL), LOW)],
        after=for_skip.send + [mixed],
    )
    dkv_parts, rest, bit, arrived = [dkv[:width]], dkv, 1, []
    summed = []
    while bit < rows:
        n = rest.shape[0] // 2
        got = to_bit(rest[n:], bit)
        dkv_parts.append(got[:width])
        arrived.append(got)
        if n > width:
            rest = low(wide(rest[:n]) + wide(got))
            dkv_parts = [rest[:width]]
            summed.append(rest)
        bit *= 2
    skip_across = [for_skip.across(0)]
    mixed_other = to_head(mixed)
    for_attn = Scatter(
        [(grad_proj_low, attended), (normed_all, dq), (normed_all, dkv)],
        theirs or None,
        [],
        [],
        [[0], [1, 2]],
    )
    attn_across = [for_attn.across(i) for i in range(2)]
    mixed_full = both_halves(head, mixed, mixed_other)
    for_point = Scatter([(mixed_full, grad_out)], None, for_attn.send)
    for_skip.take(skip_across)
    (partial_one,) = run(
        functools.partial(project_back_kernel, len(dkv_parts)),
        1,
        [dq] + dkv_parts + [w_qk, w_value],
        [new((width, model), LOW)],
        after=skip_across[0] + attn_across[0] + for_attn.send + for_point.theirs,
    )
    for_skip.step([partial_one])
    point_across = for_point.across(0)
    for_attn.take(attn_across)
    for_attn.step(for_point.send)
    input_grad, grad_gain_one, grad_bias_one = run(
        outer_back_kernel,
        1,
        [at_head, own_blocks[0], other_blocks[0], partial_one, to_head(partial_one)]
        + [gain_one, resid],
        [new((width, chan), F32), new((1, model), F32), new((1, model), F32)],
        after=point_across + for_skip.got + for_attn.got,
    )
    input_grad = input_grad[None]
    for_point.take([point_across])
    for_attn.step()
    for_point.step([for_attn.sent])
    for_skip.step([for_attn.sent])
    for_point.step([for_attn.sent])
    grad_skip = for_skip.finish()
    grad_attn, grad_point = for_attn.finish(), for_point.finish()
    grad_out_w, grad_qkv = grad_attn[:, : heads * VAL], grad_attn[:, heads * VAL :]
    result = (nn(mixed_full, w_point[0][:, 2 * ff + chan : 2 * ff + 2 * chan]) + b_point).astype(LOW)
    block_output = tn(apart, result).astype(LOW)[None]
    grad_depth = [grad_depth[k] for k in range(3)]

    rel_parts = grad_rel.reshape(heads, group, rel_cols).transpose(1, 0, 2)
    parts = [grad_gain_one, grad_bias_one, grad_gain_two, grad_bias_two, grad_down_bias]
    parts += [grad_up_bias, grad_skip_bias] + grad_depth + [grad_point_bias]
    parts = jnp.concatenate([p.reshape(group, -1) for p in parts] + [rel_parts.reshape(group, -1)], axis=1)
    sums = scatter_small(parts)

    def own(start, count):
        return sums[0, start : start + count]

    at = 6 * shard
    return (
        block_output,
        input_grad,
        own(0, shard),
        own(shard, shard),
        grad_qkv[:, :kw],
        grad_qkv[:, kw : 2 * kw],
        grad_qkv[:, 2 * kw :],
        own(at + 5 * small, heads * rel_cols).reshape(heads, rel_cols),
        grad_out_w.T,
        own(2 * shard, shard),
        own(3 * shard, shard),
        wide(grad_up),
        own(5 * shard, shard)[None],
        wide(grad_down).T,
        own(4 * shard, shard),
        grad_skip,
        own(at, small)[None],
        own(at + small, 3 * small).reshape(3, 1, small),
        grad_point,
        own(at + 4 * small, small)[None],
    )


def solution(mesh):
    gr = (IT, RW)
    vec, cols, rws = P(gr), P(gr, HD), P(HD, gr)
    act = P(IT, RW, HD)
    taps = P(None, HD, gr)
    weights = (vec, vec, cols, cols, cols, rws, rws, vec, vec, cols, rws, rws, vec, cols, rws)
    weights += (taps, cols, rws)
    return jax.shard_map(
        shards,
        mesh=mesh,
        in_specs=(act, P(IT, RW, None), act, P(IT, HD)) + weights,
        out_specs=(act, act) + weights,
        check_vma=False,
    )
```

```python
import functools

import jax
import jax.numpy as jnp
import numpy as np
from jax import lax
from jax.experimental import pallas as pl
from jax.experimental.pallas import tpu as pltpu
from jax.sharding import PartitionSpec as P

KEY = 64
VAL = 192
NB = 32
EPS = 1e-05
IT, HD, RW = "items", "heads", "rows"
LOW = jnp.bfloat16
F32 = jnp.float32
VMEM = pltpu.CompilerParams(vmem_limit_bytes=56 * 2**20)
SHORT = pl.CostEstimate(flops=1, bytes_accessed=1, transcendentals=0)


def nn(a, b):
    return lax.dot_general(a, b, (((1,), (0,)), ((), ())), preferred_element_type=F32)


def nt(a, b):
    return lax.dot_general(a, b, (((1,), (1,)), ((), ())), preferred_element_type=F32)


def tn(a, b):
    return lax.dot_general(a, b, (((0,), (0,)), ((), ())), preferred_element_type=F32)


def wide(a):
    return a.astype(F32)


def low(a):
    return lax.reduce_precision(a, 8, 7).astype(LOW)


def bit_order(n):
    out, bit = [0], n // 2
    while bit:
        out += [i + bit for i in out]
        bit //= 2
    return out


def to_core(a):
    n = lax.axis_size(IT)
    return lax.ppermute(a, IT, [(i, i ^ 1) for i in range(n)])


def to_pair(a, k):
    n = lax.axis_size(IT)
    return lax.ppermute(a, IT, [(i, (i + 2 * k) % n) for i in range(n)])


def to_head(a):
    return lax.ppermute(a, HD, [(0, 1), (1, 0)])


def place():
    item = lax.axis_index(IT)
    return item // 2, item % 2, lax.axis_index(RW)


def to_bit(a, bit):
    n = lax.axis_size(RW)
    return lax.ppermute(a, RW, [(i, i ^ bit) for i in range(n)])


def halve(keep, got, pick_bit, pieces, after=()):
    w, n = keep.shape[0] // pieces, keep.shape[1]
    shape = (pieces // 2, 2, w, n)
    if w % 16:
        total = wide(keep)
        if got:
            total = total + wide(jnp.concatenate(got, axis=1))
        total = total.reshape(shape)
        mine = lax.dynamic_index_in_dim(total, pick_bit, 1, keepdims=False)
        send = lax.dynamic_index_in_dim(total, 1 - pick_bit, 1, keepdims=False)
        return mine.reshape(-1, n), low(send).reshape(-1, n)
    widths = [g.shape[1] for g in got]

    def body(bit_ref, keep_ref, *refs):
        got_refs, (mine_ref, send_ref) = refs[:-2], refs[-2:]

        def write(bit):
            if not got:
                mine_ref[0] = keep_ref[0, bit].astype(F32)
                send_ref[0] = keep_ref[0, 1 - bit].astype(LOW)
            at = 0
            for ref, count in zip(got_refs, widths):
                there = slice(at, at + count)
                at += count
                mine_ref[0, :, there] = keep_ref[0, bit, :, there] + ref[0, bit].astype(F32)
                total = keep_ref[0, 1 - bit, :, there] + ref[0, 1 - bit].astype(F32)
                send_ref[0, :, there] = total.astype(LOW)

        for bit in range(2):
            pl.when(bit_ref[0] == bit)(functools.partial(write, bit))

    def block(count):
        return (1, 2, w, count), lambda i: (i, 0, 0, 0)

    out = (1, w, n), lambda i: (i, 0, 0)
    half_shape = (pieces // 2, w, n)
    mine, send = run(
        body,
        pieces // 2,
        [(pick_bit.reshape(1), None, None), (keep.reshape(shape), *block(n))]
        + [(g.reshape(pieces // 2, 2, w, count), *block(count)) for g, count in zip(got, widths)],
        [(new(half_shape, F32), *out), (new(half_shape, LOW), *out)],
        after=after,
    )
    return mine.reshape(-1, n), send.reshape(-1, n)


def find(bounds, start, end):
    at = next(i for i, (a, b) in enumerate(bounds) if a <= start and end <= b)
    return at, slice(start - bounds[at][0], end - bounds[at][0])


def bounds_of(arrays):
    ends = [int(e) for e in np.cumsum([0] + [a.shape[1] for a in arrays])]
    return list(zip(ends, ends[1:]))


def spots_of(side, w):
    pairs = lax.axis_size(IT) // 2
    x, _, _ = place()
    return [(((x + k) % pairs) * 2 + side) for k in range(pairs)]


def fits(w):
    rows = lax.axis_size(RW)
    return lax.axis_size(IT) == 4 and w % 128 == 0 and (w // rows) % 16 == 0


def columns_product(spots_ref, left_ref, right, out_ref, there):
    count = spots_ref.shape[0]
    w = out_ref.shape[0] // count
    for k in range(count):
        start = pl.multiple_of(spots_ref[k] * w, 128)
        left = left_ref[pl.ds(0, right.shape[0]), pl.ds(start, w)]
        out_ref[k * w : (k + 1) * w, there] = tn(left, right).astype(LOW)


def add_last(keep, got, after):
    if keep.shape[0] % 16:
        return keep + wide(got)

    def body(keep_ref, got_ref, out_ref):
        out_ref[...] = keep_ref[...] + got_ref[...].astype(F32)

    return run(body, 1, [keep, got], [new(keep.shape, F32)], after=after)[0]


def side_product(pairs_of, side, got=None, after=(), groups=None, others=False):
    pairs = lax.axis_size(IT) // 2
    w = pairs_of[0][0].shape[1] // (2 * pairs)
    spots = spots_of(side, w)
    cols = [right.shape[1] for _, right in pairs_of]
    ends = [int(e) for e in np.cumsum([0] + cols)]
    groups = groups or [[k] for k in range(len(cols))]
    bounds = [(ends[g[0]], ends[g[-1] + 1]) for g in groups]
    if w % 128:
        out = []
        for left, right in pairs_of:
            part = [lax.dynamic_slice_in_dim(left, spot * w, w, 1) for spot in spots]
            out.append(tn(jnp.concatenate(part, axis=1)[: right.shape[0]], right))
        out = jnp.concatenate(out, axis=1)
        if got is None:
            return low(out)
        out = out + wide(jnp.concatenate(got, axis=1))
        return out[:w], [low(out[w:, i:j]) for i, j in bounds]
    n, count, m = sum(cols), len(pairs_of), len(after)
    first = int(others)
    got = got or []
    got_bounds = bounds_of(got)

    def body(spot_ref, *refs):
        lefts, rights = refs[:count], refs[count : 2 * count]
        gots = refs[2 * count : 2 * count + len(got)]
        outs = refs[2 * count + len(got) + m :]
        if others:
            outs = (None,) + tuple(outs)
        step = pl.program_id(0)
        for k in range(count):
            there = slice(ends[k], ends[k + 1])
            to = next(i for i, g in enumerate(groups) if k in g)
            inside = slice(ends[k] - bounds[to][0], ends[k + 1] - bounds[to][0])
            part = tn(lefts[k][...], rights[k][...])
            if not got:
                outs[0][:, there] = part.astype(LOW)
                continue
            which, where = find(got_bounds, ends[k], ends[k + 1])
            part = part + gots[which][:, where].astype(F32)

            if others:
                outs[1 + to][:, inside] = part.astype(LOW)
                continue

            @pl.when(step == 0)
            def _(part=part, there=there):
                outs[0][:, there] = part

            @pl.when(step > 0)
            def _(part=part, to=to, inside=inside):
                outs[1 + to][:, inside] = part.astype(LOW)

    specs = [
        pl.BlockSpec((right.shape[0], w), lambda i, spot: (0, spot[i])) for left, right in pairs_of
    ] + [pl.BlockSpec(right.shape, lambda i, spot: (0, 0)) for _, right in pairs_of]
    operands = [left for left, _ in pairs_of] + [right for _, right in pairs_of]
    specs += [pl.BlockSpec((w, g.shape[1]), lambda i, spot: (i + first, 0)) for g in got]
    operands += got
    if not got:
        out_specs = [pl.BlockSpec((w, n), lambda i, spot: (i, 0))]
        out_shape = [new((pairs * w, n), LOW)]
    else:
        out_specs, out_shape = [pl.BlockSpec((w, n), lambda i, spot: (0, 0))], [new((w, n), F32)]
        for c in [j - i for i, j in bounds]:
            out_specs.append(
                pl.BlockSpec((w, c), lambda i, spot: (jnp.maximum(i - 1 + first, 0), 0))
            )
            out_shape.append(new(((pairs - 1) * w, c), LOW))
        out_specs, out_shape = out_specs[first:], out_shape[first:]
    out = pl.pallas_call(
        body,
        grid_spec=pltpu.PrefetchScalarGridSpec(
            num_scalar_prefetch=1,
            grid=(pairs - first,),
            in_specs=specs + [pl.BlockSpec(memory_space=pl.ANY)] * m,
            out_specs=out_specs,
        ),
        out_shape=out_shape,
        compiler_params=VMEM,
        cost_estimate=SHORT,
    )(jnp.stack(spots[first:]).astype(jnp.int32), *operands, *after)
    if others:
        return list(out)
    return (out[0], list(out[1:])) if got else out[0]


def product_halve(pairs_of, spot, core, terms, pick_bit, pieces, after=()):
    w = pairs_of[0][0].shape[1] // (2 * (lax.axis_size(IT) // 2))
    cols = [right.shape[1] for _, right in pairs_of]
    ends = [int(e) for e in np.cumsum([0] + cols)]
    n, count, m = ends[-1], len(pairs_of), len(after)
    widths = [g.shape[1] for g in terms]
    piece = w // pieces
    core_bounds = bounds_of(core)

    def body(at_ref, *refs):
        lefts, rights = refs[:count], refs[count : 2 * count]
        at = 2 * count + len(core)
        core_refs, term_refs = refs[2 * count : at], refs[at : at + len(terms)]
        mine_ref, send_ref, total = refs[at + len(terms) + m :]
        for k in range(count):
            there = slice(ends[k], ends[k + 1])
            which, where = find(core_bounds, ends[k], ends[k + 1])
            part = core_refs[which][:, where].astype(F32)
            total[:, there] = tn(lefts[k][...], rights[k][...]) + part
        at = 0
        for ref, wide_n in zip(term_refs, widths):
            there = slice(at, at + wide_n)
            at += wide_n
            total[:, there] += ref[...].astype(F32)
        for i in range(pieces // 2):
            out = slice(i * piece, (i + 1) * piece)
            for bit in range(2):

                @pl.when(at_ref[1] == bit)
                def _(i=i, bit=bit, out=out):
                    mine = (2 * i + bit) * piece
                    send = (2 * i + 1 - bit) * piece
                    mine_ref[out] = total[mine : mine + piece]
                    send_ref[out] = total[send : send + piece].astype(LOW)

    in_specs = [
        pl.BlockSpec((right.shape[0], w), lambda i, at: (0, at[0])) for _, right in pairs_of
    ] + [pl.BlockSpec(right.shape, lambda i, at: (0, 0)) for _, right in pairs_of]
    in_specs += [pl.BlockSpec((w, g.shape[1]), lambda i, at: (0, 0)) for g in core]
    in_specs += [pl.BlockSpec(t.shape, lambda i, at: (0, 0)) for t in terms]
    out_spec = pl.BlockSpec((w // 2, n), lambda i, at: (0, 0))
    return pl.pallas_call(
        body,
        grid_spec=pltpu.PrefetchScalarGridSpec(
            num_scalar_prefetch=1,
            grid=(1,),
            in_specs=in_specs + [pl.BlockSpec(memory_space=pl.ANY)] * m,
            out_specs=[out_spec, out_spec],
            scratch_shapes=[pltpu.VMEM((w, n), F32)],
        ),
        out_shape=[new((w // 2, n), F32), new((w // 2, n), LOW)],
        compiler_params=VMEM,
        cost_estimate=SHORT,
    )(
        jnp.stack([spot, pick_bit]).astype(jnp.int32),
        *[left for left, _ in pairs_of],
        *[right for _, right in pairs_of],
        *core,
        *terms,
        *after,
    )


class Scatter:
    def __init__(self, pairs_of, theirs=None, after=(), after_more=(), groups=None):
        pairs = lax.axis_size(IT) // 2
        self.x, self.c, self.z = place()
        self.pairs_of, self.groups = pairs_of, groups
        self.plain = not fits(pairs_of[0][0].shape[1] // (2 * pairs))
        if theirs is None:
            theirs = [side_product(pairs_of, 1 - self.c, None, after)]
        self.theirs = theirs
        self.core = [to_core(t) for t in theirs]
        if self.plain:
            self.keep, self.send = side_product(pairs_of, self.c, self.core, after_more, groups)
        else:
            self.send = side_product(
                pairs_of, self.c, self.core, after_more, groups, others=True
            )
        self.bit = 1

    def across(self, i):
        pairs = lax.axis_size(IT) // 2
        w = self.send[i].shape[0] // (pairs - 1)
        return [to_pair(self.send[i][(k - 1) * w : k * w], k) for k in range(1, pairs)]

    def take(self, got):
        if self.plain:
            for terms in zip(*[g[:-1] for g in got]):
                self.keep = self.keep + wide(jnp.concatenate(terms, axis=1))
        self.got = [g[-1] for g in got]

    def step(self, after=()):
        pieces = lax.axis_size(RW) // self.bit
        pick_bit = (self.z // self.bit) % 2
        if self.bit == 1 and not self.plain:
            self.keep, self.sent = product_halve(
                self.pairs_of, self.x * 2 + self.c, self.core, self.got, pick_bit, pieces, after
            )
        else:
            self.keep, self.sent = halve(self.keep, self.got, pick_bit, pieces, after)
        self.got = [to_bit(self.sent, self.bit)]
        self.bit *= 2
        return self.got

    def finish(self, after=()):
        while self.bit < lax.axis_size(RW):
            self.step(after)
        return add_last(self.keep, self.got[0], after)


class RowSum:
    def __init__(self, keep):
        self.keep, self.got, self.bit = keep, [], 1
        self.z = lax.axis_index(RW)

    def step(self, after=()):
        pieces = lax.axis_size(RW) // self.bit
        pick_bit = (self.z // self.bit) % 2
        self.keep, self.sent = halve(self.keep, self.got, pick_bit, pieces, after)
        self.got = [to_bit(self.sent, self.bit)]
        self.bit *= 2
        return self.got

    def finish(self, after=()):
        while self.bit < lax.axis_size(RW):
            self.step(after)
        return add_last(self.keep, self.got[0], after)


def scatter_small(parts, after):
    pairs, rows = lax.axis_size(IT) // 2, lax.axis_size(RW)
    x, c, z = place()
    n = parts.shape[1]
    cube = parts.reshape(pairs, 2, rows, n)
    cube = lax.dynamic_index_in_dim(cube, c, 1, keepdims=False) + to_core(
        lax.dynamic_index_in_dim(cube, 1 - c, 1, keepdims=False)
    )
    plane = lax.dynamic_index_in_dim(cube, x, 0, keepdims=False)
    for k in range(1, pairs):
        plane = plane + to_pair(
            lax.dynamic_index_in_dim(cube, (x + k) % pairs, 0, keepdims=False), k
        )
    terms = [lax.dynamic_index_in_dim(plane, z, 0, keepdims=True)]
    for k in range(1, rows):
        spot = jnp.bitwise_xor(z, k)
        terms.append(to_bit(lax.dynamic_index_in_dim(plane, spot, 0, keepdims=True), k))

    def body(*refs):
        refs[-1][...] = sum(ref[...] for ref in refs[1:-1]) + refs[0][...]

    return run(body, 1, terms, [new(terms[0].shape, F32)], after=after)[0]


def attend_kernel(q_ref, kv_ref, wr_ref, basis_ref, out_ref, p_ref):
    rows, seq, heads = q_ref.shape[0], kv_ref.shape[0], p_ref.shape[0]
    width = heads * KEY
    basis = basis_ref[...]
    outs = []
    for h in range(heads):
        qh = q_ref[:, h * KEY : (h + 1) * KEY]
        kh = kv_ref[:, h * KEY : (h + 1) * KEY]
        vh = kv_ref[:, width + h * VAL : width + (h + 1) * VAL]
        features = nt(qh, wr_ref[h * NB : (h + 1) * NB, :].astype(LOW)).astype(LOW)
        table = nt(features, basis)
        rel = [
            pltpu.roll(
                table[:, k * 2 * rows : (k + 1) * 2 * rows], rows + 1, 1, stride=1, stride_axis=0
            )[:, :rows]
            for k in range(seq // rows)
        ]
        logits = nt(qh, kh) + jnp.concatenate(rel, axis=1)
        e = jnp.exp(logits - jnp.max(logits, axis=1, keepdims=True))
        p = (e * (1.0 / jnp.sum(e, axis=1, keepdims=True))).astype(LOW)
        p_ref[h] = p
        outs.append(nn(p, vh))
    out_ref[...] = jnp.concatenate(outs, axis=1).astype(LOW)


def attend_back_kernel(q_ref, kv_ref, wr_ref, basis_ref, p_ref, g_ref, dq_ref, dkv_ref, dwr_ref):
    rows, seq, heads = q_ref.shape[0], kv_ref.shape[0], p_ref.shape[0]
    width = heads * KEY
    basis = basis_ref[...]
    ii = lax.broadcasted_iota(jnp.int32, (rows, rows), 0)
    jj = lax.broadcasted_iota(jnp.int32, (rows, rows), 1)
    flip = (ii + jj == rows - 1).astype(F32).astype(LOW)
    dqs, dks, dvs = [], [], []
    for h in range(heads):
        qh = q_ref[:, h * KEY : (h + 1) * KEY]
        kh = kv_ref[:, h * KEY : (h + 1) * KEY]
        vh = kv_ref[:, width + h * VAL : width + (h + 1) * VAL]
        gh = g_ref[:, h * VAL : (h + 1) * VAL]
        wr = wr_ref[h * NB : (h + 1) * NB, :].astype(LOW)
        p = p_ref[h]
        probs = p.astype(F32)
        dp = nt(gh, vh)
        inner = jnp.sum(probs * dp, axis=1, keepdims=True)
        ds = (probs * (dp - inner)).astype(LOW)
        dvs.append(tn(p, gh))
        dks.append(tn(ds, qh))
        rev = nn(flip, ds)
        zeros = jnp.zeros((rows, rows), F32)
        tabs = [
            pltpu.roll(
                jnp.concatenate([rev[:, k * rows : (k + 1) * rows], zeros], axis=1),
                0,
                1,
                stride=1,
                stride_axis=0,
            ).astype(LOW)
            for k in range(seq // rows)
        ]
        features = nn(jnp.concatenate(tabs, axis=1), basis).astype(LOW)
        features = nn(flip, features).astype(LOW)
        dqs.append(nn(ds, kh) + nn(features, wr))
        dwr_ref[h * NB : (h + 1) * NB, :] = tn(features, qh)
    dq = jnp.concatenate(dqs, axis=1).astype(LOW).astype(F32) * (KEY**-0.5)
    dq_ref[...] = dq.astype(LOW)
    dkv_ref[...] = jnp.concatenate(dks + dvs, axis=1).astype(LOW)


def run(body, grid, ins, outs, scratch=(), after=()):
    n, m = len(ins), len(after)

    def kernel(*refs):
        body(*refs[:n], *refs[n + m :])

    def spec(shape, index):
        if index is None:
            return pl.BlockSpec(memory_space=pltpu.SMEM)
        return pl.BlockSpec(shape, index)

    def whole(a):
        return (a, a.shape, lambda i: (0,) * a.ndim)

    full = [entry if isinstance(entry, tuple) else whole(entry) for entry in ins]
    out_full = [entry if isinstance(entry, tuple) else whole(entry) for entry in outs]
    return pl.pallas_call(
        kernel,
        grid=(grid,),
        in_specs=[spec(shape, index) for _, shape, index in full]
        + [pl.BlockSpec(memory_space=pl.ANY)] * m,
        out_specs=tuple(spec(shape, index) for _, shape, index in out_full),
        out_shape=tuple(a for a, _, _ in out_full),
        scratch_shapes=scratch,
        compiler_params=VMEM,
        cost_estimate=SHORT,
    )(*[a for a, _, _ in full], *after)


def new(shape, dtype):
    return jax.ShapeDtypeStruct(shape, dtype)


def ordered(head_ref, own, other):
    first = head_ref[0] == 0
    return jnp.concatenate([jnp.where(first, own, other), jnp.where(first, other, own)], axis=1)


def my_half(head_ref, a):
    n = a.shape[1] // 2
    first = head_ref[0] == 0
    return jnp.where(first, a[:, :n], a[:, n:]), jnp.where(first, a[:, n:], a[:, :n])


def pack_kernel(count, *refs):
    out_ref, rows_ref = refs[-2:]
    rows, height = rows_ref.shape[0], out_ref.shape[0]
    at = 0
    for ref in refs[:count]:
        there = slice(at, at + ref.shape[1])
        at += ref.shape[1]
        out_ref[: ref.shape[0], there] = ref[...].astype(LOW)
        if ref.shape[0] < height:
            below = there
    rows_ref[...] = jnp.zeros_like(rows_ref)
    spot, width = 0, rows_ref.shape[1]
    for ref in refs[count:-2]:
        for i in range(ref.shape[0]):
            done, n = 0, ref.shape[1]
            while done < n:
                row, col = divmod(spot, width)
                part = min(n - done, width - col)
                rows_ref[row : row + 1, col : col + part] = ref[i : i + 1, done : done + part]
                done, spot = done + part, spot + part
    out_ref[height - rows :, below] = rows_ref[...].astype(LOW)


def unpack_kernel(shard, skip_rows, lengths, last_ref, skip_ref, rel_ref, *outs):
    group = last_ref.shape[0] // shard
    heads = rel_ref.shape[0] // NB
    width = last_ref.shape[1]
    for g in range(group):
        start = g * shard
        skip_ref[g * skip_rows : (g + 1) * skip_rows] = last_ref[start : start + skip_rows]
        rows = last_ref[start + skip_rows : start + shard].astype(F32)

        def piece(spot, n):
            parts, done = [], 0
            while done < n:
                row, col = divmod(spot + done, width)
                part = min(n - done, width - col)
                parts.append(rows[row : row + 1, col : col + part])
                done += part
            return parts[0] if len(parts) == 1 else jnp.concatenate(parts, axis=1)

        spot = 0
        for n, out in zip(lengths, outs):
            out[:, g * n : (g + 1) * n] = piece(spot, n)
            spot += n
        each = NB // group
        for h in range(heads):
            for j in range(each):
                row = h * NB + g * each + j
                rel_ref[row : row + 1] = piece(spot, KEY)
                spot += KEY


def pack_sums_kernel(shares, *refs):
    rel_ref, out_ref = refs[-2:]
    group = out_ref.shape[0]
    heads, each = rel_ref.shape[0] // NB, NB // group
    for g in range(group):
        spot = 0
        for (i, n), ref in zip(shares, refs):
            out_ref[g : g + 1, spot : spot + n] = ref[i : i + 1, g * n : (g + 1) * n]
            spot += n
        for h in range(heads):
            for j in range(each):
                row = h * NB + g * each + j
                out_ref[g : g + 1, spot : spot + KEY] = rel_ref[row : row + 1]
                spot += KEY


def project_kernel(rows, head_ref, *refs):
    own, other = refs[:rows], refs[rows : 2 * rows]
    gain_ref, bias_ref, qk_ref, v_ref, q_ref, kv_ref, normed_ref = refs[2 * rows :]
    width, kw = q_ref.shape
    for k in range(rows):
        x = ordered(head_ref, own[k][...].astype(F32), other[k][...].astype(F32))
        normed = (normalize(x)[0] * gain_ref[...] + bias_ref[...]).astype(LOW)
        at = slice(k * width, (k + 1) * width)
        normed_ref[at, :] = normed
        kv_ref[at, :kw] = nn(normed, qk_ref[:, kw:]).astype(LOW)
        kv_ref[at, kw:] = nn(normed, v_ref[...]).astype(LOW)
        if k == 0:
            q_ref[...] = (nn(normed, qk_ref[:, :kw]) * (KEY**-0.5)).astype(LOW)


def attend_out_kernel(q_ref, kv_ref, wr_ref, basis_ref, out_w_ref, out_ref, p_ref, part_ref):
    attend_kernel(q_ref, kv_ref, wr_ref, basis_ref, out_ref, p_ref)
    part_ref[...] = nt(out_ref[...], out_w_ref[...]).astype(LOW)


def ff_kernel(
    head_ref, own_ref, other_ref, p_ref, po_ref, gain_ref, bias_ref, b_up_ref, b_down_ref, up_ref, down_ref,
    hidden_ref, normed_ref, act_ref, slope_ref, mine_ref, send_ref, acc,
):
    step = pl.program_id(0)

    @pl.when(step == 0)
    def _():
        x = ordered(head_ref, own_ref[...].astype(F32), other_ref[...].astype(F32))
        hidden = x + (p_ref[...].astype(F32) + po_ref[...].astype(F32))
        hidden_ref[...] = hidden
        normed_ref[...] = (normalize(hidden)[0] * gain_ref[...] + bias_ref[...]).astype(LOW)
        acc[...] = hidden + b_down_ref[...]

    u = nn(normed_ref[...], up_ref[...]) + b_up_ref[...]
    t = jnp.tanh(G0 * (u + G1 * u * u * u))
    act = (0.5 * u * (1.0 + t)).astype(LOW)
    slope = 0.5 * (1.0 + t) + 0.5 * u * (1.0 - t * t) * (G0 * (1.0 + 3.0 * G1 * u * u))
    act_ref[...] = act
    slope_ref[...] = slope.astype(LOW)
    n = acc.shape[1] // 2
    part = nt(act, down_ref[...])
    mine, theirs = my_half(head_ref, part)

    @pl.when(step == 0)
    def _():
        mine_ref[...] = my_half(head_ref, acc[...])[0] + mine
        acc[:, :n] = theirs

    @pl.when(step > 0)
    def _():
        mine_ref[...] += mine
        acc[:, :n] += theirs

    @pl.when(step == pl.num_programs(0) - 1)
    def _():
        send_ref[...] = acc[:, :n].astype(LOW)


def ff_back_kernel(
    head_ref, own_ref, other_ref, slope_ref, up_ref, down_ref, *refs
):
    normed_ref, act_ref = refs[:2]
    grad_ref, pre_ref, part_ref, b_up_ref, b_down_ref = refs[2:7]
    step, acc = pl.program_id(0), refs[-1]

    @pl.when(step == 0)
    def _():
        grad = ordered(head_ref, own_ref[...], other_ref[...])
        grad_ref[...] = grad
        b_down_ref[...] = jnp.sum(grad.astype(F32), axis=0, keepdims=True)
        acc[...] = jnp.zeros_like(acc)

    pre = (slope_ref[...].astype(F32) * nn(grad_ref[...], down_ref[...])).astype(LOW)
    pre_ref[...] = pre
    b_up_ref[...] = jnp.sum(pre.astype(F32), axis=0, keepdims=True)
    acc[...] += nt(pre, up_ref[...])
    refs[7][...] = tn(grad_ref[...], act_ref[...]).astype(LOW)
    refs[8][...] = tn(normed_ref[...], pre).astype(LOW)

    @pl.when(step == pl.num_programs(0) - 1)
    def _():
        part_ref[...] = acc[...].astype(LOW)


def inner_back_kernel(
    fused, head_ref, p_ref, po_ref, hidden_ref, grad_ref, trans_ref, gain_ref, out_w_ref,
    q_ref, kv_ref, wr_ref, basis_ref, probs_ref, *refs
):
    spots_ref, normed_ref, out_ref = refs[:3] if fused else (None, None, None)
    outs = refs[3 * fused :]
    proj_ref, resid_ref, gain_sum_ref, bias_sum_ref, dq_ref, dkv_ref, dwr_ref = outs[:7]
    attended = outs[-1]
    grad_normed = p_ref[...].astype(F32) + po_ref[...].astype(F32)
    hat, scale = normalize(hidden_ref[...])
    gain_sum_ref[...] = jnp.sum(grad_normed * hat, axis=0, keepdims=True)
    bias_sum_ref[...] = jnp.sum(grad_normed, axis=0, keepdims=True)
    through = norm_back(grad_normed, hat, scale, gain_ref[...])
    resid_ref[...] = trans_ref[...] + my_half(head_ref, through)[0]
    proj = (grad_ref[...].astype(F32) + through).astype(LOW)
    proj_ref[...] = proj
    attended[...] = nn(proj, out_w_ref[...]).astype(LOW)
    attend_back_kernel(
        q_ref, kv_ref, wr_ref, basis_ref, probs_ref, attended, dq_ref, dkv_ref, dwr_ref
    )
    if fused:
        kw = dq_ref.shape[1]
        columns_product(spots_ref, proj_ref, out_ref[...], outs[7], slice(None))
        columns_product(spots_ref, normed_ref, dq_ref[...], outs[8], slice(0, kw))
        columns_product(spots_ref, normed_ref, dkv_ref[...], outs[8], slice(kw, None))


def point_back_kernel(head_ref, grad_ref, point_ref, mine_ref, send_ref, bias_ref):
    grad = grad_ref[...]
    bias_ref[...] = jnp.sum(grad[: grad.shape[0] - 16].astype(F32), axis=0, keepdims=True)
    mine, theirs = my_half(head_ref, nt(grad, point_ref[...]))
    mine_ref[...] = mine
    send_ref[...] = theirs.astype(LOW)


def before(a, edge):
    row = lax.broadcasted_iota(jnp.int32, a.shape, 0)
    return jnp.where(row == 0, edge, pltpu.roll(a, 1, 0))


def behind(a, edge):
    row = lax.broadcasted_iota(jnp.int32, a.shape, 0)
    return jnp.where(row == a.shape[0] - 1, edge, pltpu.roll(a, a.shape[0] - 1, 0))


def section_back_kernel(mine_ref, got_ref, tap0, tap1, tap2, gm_ref, low_ref, coarse_ref, bias_ref):
    n = coarse_ref.shape[0]
    gm = mine_ref[...] + got_ref[...].astype(F32)
    gm_ref[...] = gm[: 2 * n]
    even, odd = gm[:n], gm[n : 2 * n]
    prev, later = gm[2 * n : 2 * n + 1], gm[2 * n + 1 : 2 * n + 2]
    gs_even = tap0[...] * odd + tap1[...] * even + tap2[...] * before(odd, prev)
    gs_odd = tap0[...] * behind(even, later) + tap1[...] * odd + tap2[...] * even
    coarse_ref[...] = gs_even + gs_odd
    gs = jnp.concatenate([gs_even, gs_odd], axis=0).astype(LOW)
    low_ref[...] = gs
    bias_ref[...] = jnp.sum(gs.astype(F32), axis=0, keepdims=True)


def section_kernel(trans_ref, skip_ref, prev_ref, later_ref, gm_ref, tap0, tap1, tap2, mixed_ref, depth_ref):
    n = trans_ref.shape[0]
    coarse = gelu(trans_ref[...])
    s_even, s_odd = coarse + skip_ref[:n], coarse + skip_ref[n:]
    s_before, s_after = before(s_odd, prev_ref[...]), behind(s_even, later_ref[...])
    mixed_ref[:n] = (tap0[...] * s_before + tap1[...] * s_even + tap2[...] * s_odd).astype(LOW)
    mixed_ref[n:] = (tap0[...] * s_even + tap1[...] * s_odd + tap2[...] * s_after).astype(LOW)
    even, odd = gm_ref[:n], gm_ref[n:]
    for k, a, b in ((0, s_before, s_even), (1, s_even, s_odd), (2, s_odd, s_after)):
        depth_ref[k : k + 1] = jnp.sum(even * a + odd * b, axis=0, keepdims=True)


def project_back_kernel(rows, dq_ref, *refs):
    parts, (qk_ref, v_ref, out_ref) = refs[:rows], refs[rows:]
    kw = dq_ref.shape[1]
    dkv = parts[0][...].astype(F32)
    for k in range(1, rows):
        dkv = dkv + parts[k][...].astype(F32)
    dkv = dkv.astype(LOW)
    dqk = jnp.concatenate([dq_ref[...], dkv[:, :kw]], axis=1)
    out_ref[...] = (nt(dqk, qk_ref[...]) + nt(dkv[:, kw:], v_ref[...])).astype(LOW)


def outer_back_kernel(
    head_ref, own_ref, other_ref, p_ref, po_ref, gain_ref, resid_ref, grad_ref, gain_sum_ref, bias_sum_ref
):
    hat, scale = normalize(
        ordered(head_ref, own_ref[...].astype(F32), other_ref[...].astype(F32))
    )
    grad_normed = p_ref[...].astype(F32) + po_ref[...].astype(F32)
    gain_sum_ref[...] = jnp.sum(grad_normed * hat, axis=0, keepdims=True)
    bias_sum_ref[...] = jnp.sum(grad_normed, axis=0, keepdims=True)
    through = norm_back(grad_normed, hat, scale, gain_ref[...])
    grad_ref[...] = resid_ref[...] + my_half(head_ref, through)[0]


def position_windows(z, width, rows):
    seq = width * rows
    block = jnp.bitwise_xor(z, np.array(bit_order(rows), np.int32)) - z
    t = block[:, None] * width + (np.arange(2 * width) - (width - 1))[None, :]
    distance = t.reshape(-1).astype(F32)
    magnitude = jnp.abs(distance)[:, None]
    number = NB // 4
    steps_up = np.arange(number, dtype=np.float32)
    half_life = (3.0 * (seq / 3.0) ** (steps_up / max(number - 1, 1))).astype(np.float32)
    decays = jnp.exp(-0.6931471805599453 * magnitude / half_life)
    central = (2.0 ** (steps_up + 1.0) - 1.0 > magnitude).astype(F32)
    even = jnp.concatenate([decays, central], axis=1)
    return jnp.concatenate([even, jnp.sign(distance)[:, None] * even], axis=1).astype(LOW)


G0, G1 = 0.7978845608028654, 0.044715


def gelu(u):
    return 0.5 * u * (1.0 + jnp.tanh(G0 * (u + G1 * u * u * u)))


def gelu_slope(u):
    t = jnp.tanh(G0 * (u + G1 * u * u * u))
    return 0.5 * (1.0 + t) + 0.5 * u * (1.0 - t * t) * (G0 * (1.0 + 3.0 * G1 * u * u))


def normalize(values):
    centered = values - jnp.mean(values, axis=-1, keepdims=True)
    scale = lax.rsqrt(jnp.mean(centered * centered, axis=-1, keepdims=True) + EPS)
    return centered * scale, scale


def norm_back(grad, hat, scale, gain):
    gg = grad * gain
    return scale * (
        gg
        - jnp.mean(gg, axis=-1, keepdims=True)
        - hat * jnp.mean(gg * hat, axis=-1, keepdims=True)
    )


def pick(head, own, other):
    return jnp.where(head == 0, own, other), jnp.where(head == 0, other, own)


def both_halves(head, own, other):
    return jnp.concatenate(pick(head, own, other), axis=1)


def half(a, head):
    n = a.shape[1] // 2
    return lax.dynamic_slice_in_dim(a, head * n, n, 1)


def one_hot(select, height, width):
    ii = lax.broadcasted_iota(jnp.int32, (height, width), 0)
    jj = lax.broadcasted_iota(jnp.int32, (height, width), 1)
    return select(ii, jj).astype(LOW)


def from_before(row):
    n = lax.axis_size(RW)
    return lax.ppermute(row, RW, [(i, i + 1) for i in range(n - 1)])


def from_behind(row):
    n = lax.axis_size(RW)
    return lax.ppermute(row, RW, [(i + 1, i) for i in range(n - 1)])


def shards(
    inputs,
    skip_input,
    cotangent,
    track_mask,
    norm1_gain,
    norm1_bias,
    query_weight,
    key_weight,
    value_weight,
    rel_weight,
    out_weight,
    norm2_gain,
    norm2_bias,
    up_weight,
    up_bias,
    down_weight,
    down_bias,
    skip_weight,
    skip_bias,
    depth_weight,
    point_weight,
    point_bias,
):
    head = lax.axis_index(HD)
    _, _, z = place()
    rows = lax.axis_size(RW)
    group = lax.axis_size(IT) * rows
    width, chan = inputs.shape[1], inputs.shape[2]
    model = 2 * chan
    heads = rel_weight.shape[0]
    kw = heads * KEY
    shard = norm1_gain.shape[0]
    small = skip_bias.shape[1]
    rel_cols = rel_weight.shape[1]

    skip_rows = skip_weight.shape[0]
    flat = jnp.concatenate(
        [norm1_gain, norm1_bias, norm2_gain, norm2_bias, down_bias, up_bias[0]]
        + [skip_bias[0], depth_weight.reshape(-1), point_bias[0], rel_weight.reshape(-1)]
    ).astype(LOW)
    spare = shard - skip_rows
    singles = [norm1_gain, norm1_bias, norm2_gain, norm2_bias, down_bias, up_bias]
    singles += [skip_bias, depth_weight, point_bias, rel_weight]
    flat = jnp.pad(flat, (0, spare * chan - flat.size)).reshape(spare, chan)
    ff = up_weight.shape[1]
    order = [up_weight, down_weight.T, out_weight.T, point_weight]
    order += [jnp.concatenate([skip_weight.astype(LOW), flat], axis=0)]
    order += [value_weight, query_weight, key_weight]
    if shard % 16 == 0 and skip_rows % 16 == 0 and spare == 16:
        order[4] = skip_weight
        singles = [v.reshape(-1, v.shape[-1]) for v in singles]
        (piece,) = run(
            functools.partial(pack_kernel, len(order)),
            1,
            order + singles,
            [new((shard, sum(w.shape[1] for w in order)), LOW)],
            [pltpu.VMEM((spare, chan), F32)],
        )
    else:
        piece = jnp.concatenate([w.astype(LOW) for w in order], axis=1)
    big = lax.all_gather(piece, (IT, RW), axis=0, tiled=True)
    at = 2 * ff

    def columns(start, count):
        return (big, (model, count), lambda i: (0, start // count))

    w_out, w_value = columns(at, chan), columns(at + 3 * chan, heads * VAL)
    w_qk = columns(at + 3 * chan + heads * VAL, 2 * kw)
    w_point = columns(at + chan, chan)
    steps = 3
    cut = ff // steps
    w_up = (big, (model, cut), lambda i: (0, i))
    w_down = (big, (model, cut), lambda i: (0, steps + i))
    if shard % 16 == 0 and skip_rows % 16 == 0 and spare == 16 and NB % group == 0:
        lengths = [shard] * 6 + [small] * 5
        w_skip, w_rel, *singles = run(
            functools.partial(unpack_kernel, shard, skip_rows, lengths),
            1,
            [columns(at + 2 * chan, chan)],
            [new((group * skip_rows, chan), LOW), new((heads * NB, KEY), F32)]
            + [new((1, group * n), F32) for n in lengths],
        )
        gain_one, bias_one, gain_two, bias_two, b_down, b_up = singles[:6]
        b_skip, tap0, tap1, tap2, b_point = singles[6:]
    else:
        last = big[:, at + 2 * chan : at + 3 * chan].reshape(group, shard, chan)
        w_skip = last[:, :skip_rows].reshape(group * skip_rows, chan)
        tails = last[:, skip_rows:].reshape(group, -1)

        def vector(start, count):
            return wide(tails[:, start : start + count]).reshape(1, -1)

        gain_one, bias_one, gain_two, bias_two, b_down, b_up = (
            vector(i * shard, shard) for i in range(6)
        )
        at = 6 * shard
        b_skip, tap0, tap1, tap2, b_point = (vector(at + i * small, small) for i in range(5))
        at += 5 * small
        w_rel = tails[:, at : at + heads * rel_cols].reshape(group, heads, rel_cols)
        w_rel = w_rel.transpose(1, 0, 2).reshape(heads * NB, KEY)

    at_head = (head.reshape(1).astype(jnp.int32), None, None)
    even = one_hot(lambda i, j: j == 2 * i, width, 2 * width)
    odd = one_hot(lambda i, j: j == 2 * i + 1, width, 2 * width)
    apart = jnp.concatenate([even, odd], axis=0)
    masked = (wide(cotangent[0]) * wide(track_mask)).astype(LOW)
    edges = [from_before(masked[-1:]), from_behind(masked[:1]), jnp.zeros((14, chan), LOW)]
    grad_out = nn(apart, masked).astype(LOW)
    grad_rows = jnp.concatenate([grad_out] + edges, axis=0)
    skip_low = nn(apart, gelu(wide(skip_input[0])).astype(LOW)).astype(LOW)

    own_blocks = [to_bit(inputs[0], k) if k else inputs[0] for k in bit_order(rows)]
    other_blocks = [to_head(b) for b in own_blocks]
    basis = position_windows(z, width, rows)
    queries, kv, normed_all = run(
        functools.partial(project_kernel, rows),
        1,
        [at_head] + own_blocks + other_blocks + [gain_one, bias_one, w_qk, w_value],
        [new((width, kw), LOW), new((rows * width, kw + heads * VAL), LOW)]
        + [new((rows * width, model), LOW)],
        after=[skip_low, grad_rows, basis],
    )
    attended, probs, partial_attn = run(
        attend_out_kernel,
        1,
        [queries, kv, w_rel, basis, w_out],
        [new((width, heads * VAL), LOW), new((heads, width, rows * width), LOW)]
        + [new((width, model), LOW)],
    )
    skip_term = nn(skip_low, w_skip) + b_skip
    gm_mine, gm_send, grad_point_bias = run(
        point_back_kernel,
        1,
        [at_head, grad_rows, w_point],
        [new((2 * width + 16, chan), F32), new((2 * width + 16, chan), LOW), new((1, chan), F32)],
        after=[partial_attn],
    )
    grad_mixed, grad_skip_low, grad_coarse, grad_skip_bias = run(
        section_back_kernel,
        1,
        [gm_mine, to_head(gm_send), tap0, tap1, tap2],
        [new((2 * width, chan), F32), new((2 * width, chan), LOW)]
        + [new((width, chan), F32), new((1, chan), F32)],
    )

    by_cut = (width, cut), lambda i: (0, i)
    hidden, normed_two, activated, slope, trans, send = run(
        ff_kernel,
        steps,
        [at_head, own_blocks[0], other_blocks[0], partial_attn, to_head(partial_attn)]
        + [gain_two, bias_two, (b_up, (1, cut), lambda i: (0, i)), b_down, w_up, w_down],
        [new((width, model), F32), new((width, model), LOW), (new((width, ff), LOW), *by_cut)]
        + [(new((width, ff), LOW), *by_cut), new((width, chan), F32), new((width, chan), LOW)],
        [pltpu.VMEM((width, model), F32)],
        after=[skip_term],
    )
    trans = trans + wide(to_head(send))

    for_skip = Scatter([(skip_low, grad_skip_low)])

    s_first = gelu(trans[:1]) + skip_term[:1]
    s_last = gelu(trans[-1:]) + skip_term[-1:]
    prev, later = wide(from_before(low(s_last))), wide(from_behind(low(s_first)))

    grad_trans = gelu_slope(trans) * grad_coarse
    grad_own = low(grad_trans)
    owned = model // lax.axis_size(IT)
    fused = fits(owned)
    core_rows = model // 2
    spots = jnp.stack(spots_of(1 - place()[1], owned)).astype(jnp.int32), None, None
    extra = new((model, ff), LOW), (model, cut), lambda i: (0, i)
    grad_ff_low, grad_pre_low, partial_two, grad_up_bias, grad_down_bias, *theirs = run(
        ff_back_kernel,
        steps,
        [at_head, grad_own, to_head(grad_own), (slope, *by_cut), w_up, w_down]
        + [normed_two, (activated, *by_cut)],
        [new((width, model), LOW), (new((width, ff), LOW), *by_cut), new((width, model), LOW)]
        + [(new((1, ff), F32), (1, cut), lambda i: (0, i)), new((1, model), F32)]
        + [extra, extra],
        [pltpu.VMEM((width, model), F32)],
        after=[prev, later],
    )
    for_down, for_up = (
        RowSum(lax.psum_scatter(t, IT, scatter_dimension=0, tiled=True)) for t in theirs
    )
    mixed, grad_depth = run(
        section_kernel,
        1,
        [trans, skip_term, prev, later, grad_mixed, tap0, tap1, tap2],
        [new((2 * width, chan), LOW), new((3, chan), F32)],
    )
    grad_proj_low, resid, grad_gain_two, grad_bias_two, dq, dkv, grad_rel, *theirs = run(
        functools.partial(inner_back_kernel, fused),
        1,
        [at_head, partial_two, to_head(partial_two), hidden, grad_ff_low, grad_trans, gain_two]
        + [w_out, queries, kv, w_rel, basis, probs]
        + [spots, normed_all, attended][: 3 * fused],
        [new((width, model), LOW), new((width, chan), F32)]
        + [new((1, model), F32), new((1, model), F32)]
        + [new(queries.shape, LOW), new(kv.shape, LOW), new(w_rel.shape, F32)]
        + [new((core_rows, heads * VAL), LOW), new((core_rows, kw + kv.shape[1]), LOW)][: 2 * fused],
        [pltpu.VMEM((width, heads * VAL), LOW)],
        after=for_skip.send + [mixed],
    )
    dkv_parts, rest, bit, arrived = [dkv[:width]], dkv, 1, []
    summed = []
    while bit < rows:
        n = rest.shape[0] // 2
        got = to_bit(rest[n:], bit)
        dkv_parts.append(got[:width])
        arrived.append(got)
        if n > width:
            rest = low(wide(rest[:n]) + wide(got))
            dkv_parts = [rest[:width]]
            summed.append(rest)
        bit *= 2
    skip_across = [for_skip.across(0)]
    mixed_other = to_head(mixed)
    skip_across = [for_skip.across(0)]
    for_skip.take(skip_across)
    for_attn = Scatter(
        [(grad_proj_low, attended), (normed_all, dq), (normed_all, dkv)],
        theirs or None,
        [],
        summed[:1] + skip_across[0],
        [[0, 1, 2]],
    )
    mixed_full = both_halves(head, mixed, mixed_other)
    for_point = Scatter([(mixed_full, grad_out)], None, for_attn.send, for_attn.send)
    for_down.step(for_point.theirs)
    attn_across = [for_attn.across(0)]
    for_attn.take(attn_across)
    point_across = for_point.across(0)
    for_point.take([point_across])
    (partial_one,) = run(
        functools.partial(project_back_kernel, len(dkv_parts)),
        1,
        [dq] + dkv_parts + [w_qk, w_value],
        [new((width, model), LOW)],
        after=for_point.send + [for_down.sent],
    )
    for_down.step([partial_one])
    for_up.step([for_down.sent])
    for_attn.step([for_up.sent])
    for_skip.step([for_attn.sent])
    input_grad, grad_gain_one, grad_bias_one = run(
        outer_back_kernel,
        1,
        [at_head, own_blocks[0], other_blocks[0], partial_one, to_head(partial_one)]
        + [gain_one, resid],
        [new((width, chan), F32), new((1, model), F32), new((1, model), F32)],
        after=[for_skip.sent] + point_across + for_up.got + for_down.got,
    )
    input_grad = input_grad[None]
    for_attn.step([grad_gain_one])
    for_up.step([for_attn.sent] + for_skip.got)
    for_point.step([for_up.sent])
    for_skip.step([for_point.sent])
    for_point.step([for_skip.sent] + for_attn.got)
    last = [for_point.sent]
    grad_down, grad_up, grad_skip = (part.finish(last) for part in (for_down, for_up, for_skip))
    grad_attn, grad_point = for_attn.finish(last), for_point.finish(last)
    grad_out_w, grad_qkv = grad_attn[:, : heads * VAL], grad_attn[:, heads * VAL :]
    result = (nn(mixed_full, w_point[0][:, 2 * ff + chan : 2 * ff + 2 * chan]) + b_point).astype(LOW)
    block_output = tn(apart, result).astype(LOW)[None]
    parts = [grad_gain_one, grad_bias_one, grad_gain_two, grad_bias_two, grad_down_bias]
    parts += [grad_up_bias, grad_skip_bias] + [grad_depth] * 3 + [grad_point_bias]
    which = [0] * 7 + [0, 1, 2] + [0]
    if NB % group == 0:
        shares = [(i, p.shape[-1] // group) for i, p in zip(which, parts)]
        total = sum(n for _, n in shares) + heads * rel_cols
        (parts,) = run(
            functools.partial(pack_sums_kernel, shares),
            1,
            [p.reshape(-1, p.shape[-1]) for p in parts] + [grad_rel],
            [new((group, total), F32)],
        )
    else:
        parts = [p.reshape(-1, p.shape[-1])[i] for i, p in zip(which, parts)]
        rel_parts = grad_rel.reshape(heads, group, rel_cols).transpose(1, 0, 2)
        parts = [p.reshape(group, -1) for p in parts + [rel_parts]]
        parts = jnp.concatenate(parts, axis=1)
    sums = scatter_small(parts, last)

    def own(start, count):
        return sums[0, start : start + count]

    at = 6 * shard
    return (
        block_output,
        input_grad,
        own(0, shard),
        own(shard, shard),
        grad_qkv[:, :kw],
        grad_qkv[:, kw : 2 * kw],
        grad_qkv[:, 2 * kw :],
        own(at + 5 * small, heads * rel_cols).reshape(heads, rel_cols),
        grad_out_w.T,
        own(2 * shard, shard),
        own(3 * shard, shard),
        grad_up,
        own(5 * shard, shard)[None],
        grad_down.T,
        own(4 * shard, shard),
        grad_skip,
        own(at, small)[None],
        own(at + small, 3 * small).reshape(3, 1, small),
        grad_point,
        own(at + 4 * small, small)[None],
    )


def solution(mesh):
    gr = (IT, RW)
    vec, cols, rws = P(gr), P(gr, HD), P(HD, gr)
    act = P(IT, RW, HD)
    taps = P(None, HD, gr)
    weights = (vec, vec, cols, cols, cols, rws, rws, vec, vec, cols, rws, rws, vec, cols, rws)
    weights += (taps, cols, rws)
    return jax.shard_map(
        shards,
        mesh=mesh,
        in_specs=(act, P(IT, RW, None), act, P(IT, HD)) + weights,
        out_specs=(act, act) + weights,
        check_vma=False,
    )
```

```python
import functools

import jax
import jax.numpy as jnp
import numpy as np
from jax import lax
from jax.experimental import pallas as pl
from jax.experimental.pallas import tpu as pltpu
from jax.sharding import PartitionSpec as P

KEY = 64
VAL = 192
NB = 32
EPS = 1e-05
IT, HD, RW = "items", "heads", "rows"
LOW = jnp.bfloat16
F32 = jnp.float32
VMEM = pltpu.CompilerParams(vmem_limit_bytes=56 * 2**20)
SHORT = pl.CostEstimate(flops=1, bytes_accessed=1, transcendentals=0)


def nn(a, b):
    return lax.dot_general(a, b, (((1,), (0,)), ((), ())), preferred_element_type=F32)


def nt(a, b):
    return lax.dot_general(a, b, (((1,), (1,)), ((), ())), preferred_element_type=F32)


def tn(a, b):
    return lax.dot_general(a, b, (((0,), (0,)), ((), ())), preferred_element_type=F32)


def wide(a):
    return a.astype(F32)


def low(a):
    return lax.reduce_precision(a, 8, 7).astype(LOW)


def bit_order(n):
    out, bit = [0], n // 2
    while bit:
        out += [i + bit for i in out]
        bit //= 2
    return out


def to_core(a):
    n = lax.axis_size(IT)
    return lax.ppermute(a, IT, [(i, i ^ 1) for i in range(n)])


def to_pair(a, k):
    n = lax.axis_size(IT)
    return lax.ppermute(a, IT, [(i, (i + 2 * k) % n) for i in range(n)])


def to_head(a):
    return lax.ppermute(a, HD, [(0, 1), (1, 0)])


def place():
    item = lax.axis_index(IT)
    return item // 2, item % 2, lax.axis_index(RW)


def to_bit(a, bit):
    n = lax.axis_size(RW)
    return lax.ppermute(a, RW, [(i, i ^ bit) for i in range(n)])


def halve(keep, got, pick_bit, pieces, after=()):
    w, n = keep.shape[0] // pieces, keep.shape[1]
    shape = (pieces // 2, 2, w, n)
    if w % 16:
        total = wide(keep)
        if got:
            total = total + wide(jnp.concatenate(got, axis=1))
        total = total.reshape(shape)
        mine = lax.dynamic_index_in_dim(total, pick_bit, 1, keepdims=False)
        send = lax.dynamic_index_in_dim(total, 1 - pick_bit, 1, keepdims=False)
        return mine.reshape(-1, n), low(send).reshape(-1, n)
    widths = [g.shape[1] for g in got]

    def body(bit_ref, keep_ref, *refs):
        got_refs, (mine_ref, send_ref) = refs[:-2], refs[-2:]

        def write(bit):
            if not got:
                mine_ref[0] = keep_ref[0, bit].astype(F32)
                send_ref[0] = keep_ref[0, 1 - bit].astype(LOW)
            at = 0
            for ref, count in zip(got_refs, widths):
                there = slice(at, at + count)
                at += count
                mine_ref[0, :, there] = keep_ref[0, bit, :, there] + ref[0, bit].astype(F32)
                total = keep_ref[0, 1 - bit, :, there] + ref[0, 1 - bit].astype(F32)
                send_ref[0, :, there] = total.astype(LOW)

        for bit in range(2):
            pl.when(bit_ref[0] == bit)(functools.partial(write, bit))

    def block(count):
        return (1, 2, w, count), lambda i: (i, 0, 0, 0)

    out = (1, w, n), lambda i: (i, 0, 0)
    half_shape = (pieces // 2, w, n)
    mine, send = run(
        body,
        pieces // 2,
        [(pick_bit.reshape(1), None, None), (keep.reshape(shape), *block(n))]
        + [(g.reshape(pieces // 2, 2, w, count), *block(count)) for g, count in zip(got, widths)],
        [(new(half_shape, F32), *out), (new(half_shape, LOW), *out)],
        after=after,
    )
    return mine.reshape(-1, n), send.reshape(-1, n)


def find(bounds, start, end):
    at = next(i for i, (a, b) in enumerate(bounds) if a <= start and end <= b)
    return at, slice(start - bounds[at][0], end - bounds[at][0])


def bounds_of(arrays):
    ends = [int(e) for e in np.cumsum([0] + [a.shape[1] for a in arrays])]
    return list(zip(ends, ends[1:]))


def spots_of(side, w):
    pairs = lax.axis_size(IT) // 2
    x, _, _ = place()
    return [(((x + k) % pairs) * 2 + side) for k in range(pairs)]


def fits(w):
    rows = lax.axis_size(RW)
    return lax.axis_size(IT) == 4 and w % 128 == 0 and (w // rows) % 16 == 0


def columns_product(spots_ref, left_ref, right, out_ref, there):
    count = spots_ref.shape[0]
    w = out_ref.shape[0] // count
    for k in range(count):
        start = pl.multiple_of(spots_ref[k] * w, 128)
        left = left_ref[pl.ds(0, right.shape[0]), pl.ds(start, w)]
        out_ref[k * w : (k + 1) * w, there] = tn(left, right).astype(LOW)


def add_last(keep, got, after, widths):
    ends = [int(e) for e in np.cumsum([0] + widths)]
    cuts = [slice(i, j) for i, j in zip(ends, ends[1:])]
    if keep.shape[0] % 16:
        return [(keep + wide(got))[:, cut] for cut in cuts]

    def body(keep_ref, got_ref, *outs):
        for cut, out_ref in zip(cuts, outs):
            out_ref[...] = keep_ref[:, cut] + got_ref[:, cut].astype(F32)

    outs = [new((keep.shape[0], n), F32) for n in widths]
    return list(run(body, 1, [keep, got], outs, after=after))


def side_product(pairs_of, side, got=None, after=(), groups=None, others=False):
    pairs = lax.axis_size(IT) // 2
    w = pairs_of[0][0].shape[1] // (2 * pairs)
    spots = spots_of(side, w)
    cols = [right.shape[1] for _, right in pairs_of]
    ends = [int(e) for e in np.cumsum([0] + cols)]
    groups = groups or [[k] for k in range(len(cols))]
    bounds = [(ends[g[0]], ends[g[-1] + 1]) for g in groups]
    if w % 128:
        out = []
        for left, right in pairs_of:
            part = [lax.dynamic_slice_in_dim(left, spot * w, w, 1) for spot in spots]
            out.append(tn(jnp.concatenate(part, axis=1)[: right.shape[0]], right))
        out = jnp.concatenate(out, axis=1)
        if got is None:
            return low(out)
        out = out + wide(jnp.concatenate(got, axis=1))
        return out[:w], [low(out[w:, i:j]) for i, j in bounds]
    n, count, m = sum(cols), len(pairs_of), len(after)
    first = int(others)
    got = got or []
    got_bounds = bounds_of(got)

    def body(spot_ref, *refs):
        lefts, rights = refs[:count], refs[count : 2 * count]
        gots = refs[2 * count : 2 * count + len(got)]
        outs = refs[2 * count + len(got) + m :]
        if others:
            outs = (None,) + tuple(outs)
        step = pl.program_id(0)
        for k in range(count):
            there = slice(ends[k], ends[k + 1])
            to = next(i for i, g in enumerate(groups) if k in g)
            inside = slice(ends[k] - bounds[to][0], ends[k + 1] - bounds[to][0])
            part = tn(lefts[k][...], rights[k][...])
            if not got:
                outs[0][:, there] = part.astype(LOW)
                continue
            which, where = find(got_bounds, ends[k], ends[k + 1])
            part = part + gots[which][:, where].astype(F32)

            if others:
                outs[1 + to][:, inside] = part.astype(LOW)
                continue

            @pl.when(step == 0)
            def _(part=part, there=there):
                outs[0][:, there] = part

            @pl.when(step > 0)
            def _(part=part, to=to, inside=inside):
                outs[1 + to][:, inside] = part.astype(LOW)

    specs = [
        pl.BlockSpec((right.shape[0], w), lambda i, spot: (0, spot[i])) for left, right in pairs_of
    ] + [pl.BlockSpec(right.shape, lambda i, spot: (0, 0)) for _, right in pairs_of]
    operands = [left for left, _ in pairs_of] + [right for _, right in pairs_of]
    specs += [pl.BlockSpec((w, g.shape[1]), lambda i, spot: (i + first, 0)) for g in got]
    operands += got
    if not got:
        out_specs = [pl.BlockSpec((w, n), lambda i, spot: (i, 0))]
        out_shape = [new((pairs * w, n), LOW)]
    else:
        out_specs, out_shape = [pl.BlockSpec((w, n), lambda i, spot: (0, 0))], [new((w, n), F32)]
        for c in [j - i for i, j in bounds]:
            out_specs.append(
                pl.BlockSpec((w, c), lambda i, spot: (jnp.maximum(i - 1 + first, 0), 0))
            )
            out_shape.append(new(((pairs - 1) * w, c), LOW))
        out_specs, out_shape = out_specs[first:], out_shape[first:]
    out = pl.pallas_call(
        body,
        grid_spec=pltpu.PrefetchScalarGridSpec(
            num_scalar_prefetch=1,
            grid=(pairs - first,),
            in_specs=specs + [pl.BlockSpec(memory_space=pl.ANY)] * m,
            out_specs=out_specs,
        ),
        out_shape=out_shape,
        compiler_params=VMEM,
        cost_estimate=SHORT,
    )(jnp.stack(spots[first:]).astype(jnp.int32), *operands, *after)
    if others:
        return list(out)
    return (out[0], list(out[1:])) if got else out[0]


def product_halve(pairs_of, spot, core, terms, pick_bit, pieces, after=()):
    w = pairs_of[0][0].shape[1] // (2 * (lax.axis_size(IT) // 2))
    cols = [right.shape[1] for _, right in pairs_of]
    ends = [int(e) for e in np.cumsum([0] + cols)]
    n, count, m = ends[-1], len(pairs_of), len(after)
    widths = [g.shape[1] for g in terms]
    piece = w // pieces
    core_bounds = bounds_of(core)

    def body(at_ref, *refs):
        lefts, rights = refs[:count], refs[count : 2 * count]
        at = 2 * count + len(core)
        core_refs, term_refs = refs[2 * count : at], refs[at : at + len(terms)]
        mine_ref, send_ref, total = refs[at + len(terms) + m :]
        for k in range(count):
            there = slice(ends[k], ends[k + 1])
            which, where = find(core_bounds, ends[k], ends[k + 1])
            part = core_refs[which][:, where].astype(F32)
            total[:, there] = tn(lefts[k][...], rights[k][...]) + part
        at = 0
        for ref, wide_n in zip(term_refs, widths):
            there = slice(at, at + wide_n)
            at += wide_n
            total[:, there] += ref[...].astype(F32)
        for i in range(pieces // 2):
            out = slice(i * piece, (i + 1) * piece)
            for bit in range(2):

                @pl.when(at_ref[1] == bit)
                def _(i=i, bit=bit, out=out):
                    mine = (2 * i + bit) * piece
                    send = (2 * i + 1 - bit) * piece
                    mine_ref[out] = total[mine : mine + piece]
                    send_ref[out] = total[send : send + piece].astype(LOW)

    in_specs = [
        pl.BlockSpec((right.shape[0], w), lambda i, at: (0, at[0])) for _, right in pairs_of
    ] + [pl.BlockSpec(right.shape, lambda i, at: (0, 0)) for _, right in pairs_of]
    in_specs += [pl.BlockSpec((w, g.shape[1]), lambda i, at: (0, 0)) for g in core]
    in_specs += [pl.BlockSpec(t.shape, lambda i, at: (0, 0)) for t in terms]
    out_spec = pl.BlockSpec((w // 2, n), lambda i, at: (0, 0))
    return pl.pallas_call(
        body,
        grid_spec=pltpu.PrefetchScalarGridSpec(
            num_scalar_prefetch=1,
            grid=(1,),
            in_specs=in_specs + [pl.BlockSpec(memory_space=pl.ANY)] * m,
            out_specs=[out_spec, out_spec],
            scratch_shapes=[pltpu.VMEM((w, n), F32)],
        ),
        out_shape=[new((w // 2, n), F32), new((w // 2, n), LOW)],
        compiler_params=VMEM,
        cost_estimate=SHORT,
    )(
        jnp.stack([spot, pick_bit]).astype(jnp.int32),
        *[left for left, _ in pairs_of],
        *[right for _, right in pairs_of],
        *core,
        *terms,
        *after,
    )


class Scatter:
    def __init__(self, pairs_of, theirs=None, after=(), after_more=(), groups=None):
        pairs = lax.axis_size(IT) // 2
        self.x, self.c, self.z = place()
        self.pairs_of, self.groups = pairs_of, groups
        self.plain = not fits(pairs_of[0][0].shape[1] // (2 * pairs))
        if theirs is None:
            theirs = [side_product(pairs_of, 1 - self.c, None, after)]
        self.theirs = theirs
        self.core = [to_core(t) for t in theirs]
        if self.plain:
            self.keep, self.send = side_product(pairs_of, self.c, self.core, after_more, groups)
        else:
            self.send = side_product(
                pairs_of, self.c, self.core, after_more, groups, others=True
            )
        self.bit = 1

    def across(self, i):
        pairs = lax.axis_size(IT) // 2
        w = self.send[i].shape[0] // (pairs - 1)
        return [to_pair(self.send[i][(k - 1) * w : k * w], k) for k in range(1, pairs)]

    def take(self, got):
        if self.plain:
            for terms in zip(*[g[:-1] for g in got]):
                self.keep = self.keep + wide(jnp.concatenate(terms, axis=1))
        self.got = [g[-1] for g in got]

    def step(self, after=()):
        pieces = lax.axis_size(RW) // self.bit
        pick_bit = (self.z // self.bit) % 2
        if self.bit == 1 and not self.plain:
            self.keep, self.sent = product_halve(
                self.pairs_of, self.x * 2 + self.c, self.core, self.got, pick_bit, pieces, after
            )
        else:
            self.keep, self.sent = halve(self.keep, self.got, pick_bit, pieces, after)
        self.got = [to_bit(self.sent, self.bit)]
        self.bit *= 2
        return self.got

    def finish(self, after=(), widths=None):
        while self.bit < lax.axis_size(RW):
            self.step(after)
        return add_last(self.keep, self.got[0], after, widths or [self.keep.shape[1]])


class RowSum:
    def __init__(self, keep):
        self.keep, self.got, self.bit = keep, [], 1
        self.z = lax.axis_index(RW)

    def step(self, after=()):
        pieces = lax.axis_size(RW) // self.bit
        pick_bit = (self.z // self.bit) % 2
        self.keep, self.sent = halve(self.keep, self.got, pick_bit, pieces, after)
        self.got = [to_bit(self.sent, self.bit)]
        self.bit *= 2
        return self.got

    def finish(self, after=(), widths=None):
        while self.bit < lax.axis_size(RW):
            self.step(after)
        return add_last(self.keep, self.got[0], after, widths or [self.keep.shape[1]])


def scatter_small(parts, after):
    pairs, rows = lax.axis_size(IT) // 2, lax.axis_size(RW)
    x, c, z = place()
    n = parts.shape[1]
    cube = parts.reshape(pairs, 2, rows, n)
    cube = lax.dynamic_index_in_dim(cube, c, 1, keepdims=False) + to_core(
        lax.dynamic_index_in_dim(cube, 1 - c, 1, keepdims=False)
    )
    plane = lax.dynamic_index_in_dim(cube, x, 0, keepdims=False)
    for k in range(1, pairs):
        plane = plane + to_pair(
            lax.dynamic_index_in_dim(cube, (x + k) % pairs, 0, keepdims=False), k
        )
    terms = [lax.dynamic_index_in_dim(plane, z, 0, keepdims=True)]
    for k in range(1, rows):
        spot = jnp.bitwise_xor(z, k)
        terms.append(to_bit(lax.dynamic_index_in_dim(plane, spot, 0, keepdims=True), k))

    def body(*refs):
        refs[-1][...] = sum(ref[...] for ref in refs[1:-1]) + refs[0][...]

    return run(body, 1, terms, [new(terms[0].shape, F32)], after=after)[0]


def attend_kernel(q_ref, kv_ref, wr_ref, basis_ref, out_ref, p_ref):
    rows, seq, heads = q_ref.shape[0], kv_ref.shape[0], p_ref.shape[0]
    width = heads * KEY
    basis = basis_ref[...]
    outs = []
    for h in range(heads):
        qh = q_ref[:, h * KEY : (h + 1) * KEY]
        kh = kv_ref[:, h * KEY : (h + 1) * KEY]
        vh = kv_ref[:, width + h * VAL : width + (h + 1) * VAL]
        features = nt(qh, wr_ref[h * NB : (h + 1) * NB, :].astype(LOW)).astype(LOW)
        table = nt(features, basis)
        rel = [
            pltpu.roll(
                table[:, k * 2 * rows : (k + 1) * 2 * rows], rows + 1, 1, stride=1, stride_axis=0
            )[:, :rows]
            for k in range(seq // rows)
        ]
        logits = nt(qh, kh) + jnp.concatenate(rel, axis=1)
        e = jnp.exp(logits - jnp.max(logits, axis=1, keepdims=True))
        p = (e * (1.0 / jnp.sum(e, axis=1, keepdims=True))).astype(LOW)
        p_ref[h] = p
        outs.append(nn(p, vh))
    out_ref[...] = jnp.concatenate(outs, axis=1).astype(LOW)


def attend_back_kernel(q_ref, kv_ref, wr_ref, basis_ref, p_ref, g_ref, dq_ref, dkv_ref, dwr_ref):
    rows, seq, heads = q_ref.shape[0], kv_ref.shape[0], p_ref.shape[0]
    width = heads * KEY
    basis = basis_ref[...]
    ii = lax.broadcasted_iota(jnp.int32, (rows, rows), 0)
    jj = lax.broadcasted_iota(jnp.int32, (rows, rows), 1)
    flip = (ii + jj == rows - 1).astype(F32).astype(LOW)
    dqs, dks, dvs = [], [], []
    for h in range(heads):
        qh = q_ref[:, h * KEY : (h + 1) * KEY]
        kh = kv_ref[:, h * KEY : (h + 1) * KEY]
        vh = kv_ref[:, width + h * VAL : width + (h + 1) * VAL]
        gh = g_ref[:, h * VAL : (h + 1) * VAL]
        wr = wr_ref[h * NB : (h + 1) * NB, :].astype(LOW)
        p = p_ref[h]
        probs = p.astype(F32)
        dp = nt(gh, vh)
        inner = jnp.sum(probs * dp, axis=1, keepdims=True)
        ds = (probs * (dp - inner)).astype(LOW)
        dvs.append(tn(p, gh))
        dks.append(tn(ds, qh))
        rev = nn(flip, ds)
        zeros = jnp.zeros((rows, rows), F32)
        tabs = [
            pltpu.roll(
                jnp.concatenate([rev[:, k * rows : (k + 1) * rows], zeros], axis=1),
                0,
                1,
                stride=1,
                stride_axis=0,
            ).astype(LOW)
            for k in range(seq // rows)
        ]
        features = nn(jnp.concatenate(tabs, axis=1), basis).astype(LOW)
        features = nn(flip, features).astype(LOW)
        dqs.append(nn(ds, kh) + nn(features, wr))
        dwr_ref[h * NB : (h + 1) * NB, :] = tn(features, qh)
    dq = jnp.concatenate(dqs, axis=1).astype(LOW).astype(F32) * (KEY**-0.5)
    dq_ref[...] = dq.astype(LOW)
    dkv_ref[...] = jnp.concatenate(dks + dvs, axis=1).astype(LOW)


def run(body, grid, ins, outs, scratch=(), after=()):
    n, m = len(ins), len(after)

    def kernel(*refs):
        body(*refs[:n], *refs[n + m :])

    def spec(shape, index):
        if index is None:
            return pl.BlockSpec(memory_space=pltpu.SMEM)
        return pl.BlockSpec(shape, index)

    def whole(a):
        return (a, a.shape, lambda i: (0,) * a.ndim)

    full = [entry if isinstance(entry, tuple) else whole(entry) for entry in ins]
    out_full = [entry if isinstance(entry, tuple) else whole(entry) for entry in outs]
    return pl.pallas_call(
        kernel,
        grid=(grid,),
        in_specs=[spec(shape, index) for _, shape, index in full]
        + [pl.BlockSpec(memory_space=pl.ANY)] * m,
        out_specs=tuple(spec(shape, index) for _, shape, index in out_full),
        out_shape=tuple(a for a, _, _ in out_full),
        scratch_shapes=scratch,
        compiler_params=VMEM,
        cost_estimate=SHORT,
    )(*[a for a, _, _ in full], *after)


def new(shape, dtype):
    return jax.ShapeDtypeStruct(shape, dtype)


def ordered(head_ref, own, other):
    first = head_ref[0] == 0
    return jnp.concatenate([jnp.where(first, own, other), jnp.where(first, other, own)], axis=1)


def my_half(head_ref, a):
    n = a.shape[1] // 2
    first = head_ref[0] == 0
    return jnp.where(first, a[:, :n], a[:, n:]), jnp.where(first, a[:, n:], a[:, :n])


def pack_kernel(count, *refs):
    out_ref, rows_ref = refs[-2:]
    rows, height = rows_ref.shape[0], out_ref.shape[0]
    at = 0
    for ref in refs[:count]:
        there = slice(at, at + ref.shape[1])
        at += ref.shape[1]
        out_ref[: ref.shape[0], there] = ref[...].astype(LOW)
        if ref.shape[0] < height:
            below = there
    rows_ref[...] = jnp.zeros_like(rows_ref)
    spot, width = 0, rows_ref.shape[1]
    for ref in refs[count:-2]:
        for i in range(ref.shape[0]):
            done, n = 0, ref.shape[1]
            while done < n:
                row, col = divmod(spot, width)
                part = min(n - done, width - col)
                rows_ref[row : row + 1, col : col + part] = ref[i : i + 1, done : done + part]
                done, spot = done + part, spot + part
    out_ref[height - rows :, below] = rows_ref[...].astype(LOW)


def unpack_kernel(shard, skip_rows, lengths, last_ref, skip_ref, rel_ref, *outs):
    group = last_ref.shape[0] // shard
    heads = rel_ref.shape[0] // NB
    width = last_ref.shape[1]
    for g in range(group):
        start = g * shard
        skip_ref[g * skip_rows : (g + 1) * skip_rows] = last_ref[start : start + skip_rows]
        rows = last_ref[start + skip_rows : start + shard].astype(F32)

        def piece(spot, n):
            parts, done = [], 0
            while done < n:
                row, col = divmod(spot + done, width)
                part = min(n - done, width - col)
                parts.append(rows[row : row + 1, col : col + part])
                done += part
            return parts[0] if len(parts) == 1 else jnp.concatenate(parts, axis=1)

        spot = 0
        for n, out in zip(lengths, outs):
            out[:, g * n : (g + 1) * n] = piece(spot, n)
            spot += n
        each = NB // group
        for h in range(heads):
            for j in range(each):
                row = h * NB + g * each + j
                rel_ref[row : row + 1] = piece(spot, KEY)
                spot += KEY


def pack_sums_kernel(shares, *refs):
    rel_ref, out_ref = refs[-2:]
    group = out_ref.shape[0]
    heads, each = rel_ref.shape[0] // NB, NB // group
    for g in range(group):
        spot = 0
        for (i, n), ref in zip(shares, refs):
            out_ref[g : g + 1, spot : spot + n] = ref[i : i + 1, g * n : (g + 1) * n]
            spot += n
        for h in range(heads):
            for j in range(each):
                row = h * NB + g * each + j
                out_ref[g : g + 1, spot : spot + KEY] = rel_ref[row : row + 1]
                spot += KEY


def project_kernel(rows, head_ref, *refs):
    own, other = refs[:rows], refs[rows : 2 * rows]
    gain_ref, bias_ref, qk_ref, v_ref, q_ref, kv_ref, normed_ref = refs[2 * rows :]
    width, kw = q_ref.shape
    for k in range(rows):
        x = ordered(head_ref, own[k][...].astype(F32), other[k][...].astype(F32))
        normed = (normalize(x)[0] * gain_ref[...] + bias_ref[...]).astype(LOW)
        at = slice(k * width, (k + 1) * width)
        normed_ref[at, :] = normed
        kv_ref[at, :kw] = nn(normed, qk_ref[:, kw:]).astype(LOW)
        kv_ref[at, kw:] = nn(normed, v_ref[...]).astype(LOW)
        if k == 0:
            q_ref[...] = (nn(normed, qk_ref[:, :kw]) * (KEY**-0.5)).astype(LOW)


def attend_out_kernel(q_ref, kv_ref, wr_ref, basis_ref, out_w_ref, out_ref, p_ref, part_ref):
    attend_kernel(q_ref, kv_ref, wr_ref, basis_ref, out_ref, p_ref)
    part_ref[...] = nt(out_ref[...], out_w_ref[...]).astype(LOW)


def ff_kernel(
    head_ref, own_ref, other_ref, p_ref, po_ref, gain_ref, bias_ref, b_up_ref, b_down_ref, up_ref, down_ref,
    hidden_ref, normed_ref, act_ref, slope_ref, mine_ref, send_ref, acc,
):
    step = pl.program_id(0)

    @pl.when(step == 0)
    def _():
        x = ordered(head_ref, own_ref[...].astype(F32), other_ref[...].astype(F32))
        hidden = x + (p_ref[...].astype(F32) + po_ref[...].astype(F32))
        hidden_ref[...] = hidden
        normed_ref[...] = (normalize(hidden)[0] * gain_ref[...] + bias_ref[...]).astype(LOW)
        acc[...] = hidden + b_down_ref[...]

    u = nn(normed_ref[...], up_ref[...]) + b_up_ref[...]
    t = jnp.tanh(G0 * (u + G1 * u * u * u))
    act = (0.5 * u * (1.0 + t)).astype(LOW)
    slope = 0.5 * (1.0 + t) + 0.5 * u * (1.0 - t * t) * (G0 * (1.0 + 3.0 * G1 * u * u))
    act_ref[...] = act
    slope_ref[...] = slope.astype(LOW)
    n = acc.shape[1] // 2
    part = nt(act, down_ref[...])
    mine, theirs = my_half(head_ref, part)

    @pl.when(step == 0)
    def _():
        mine_ref[...] = my_half(head_ref, acc[...])[0] + mine
        acc[:, :n] = theirs

    @pl.when(step > 0)
    def _():
        mine_ref[...] += mine
        acc[:, :n] += theirs

    @pl.when(step == pl.num_programs(0) - 1)
    def _():
        send_ref[...] = acc[:, :n].astype(LOW)


def ff_back_kernel(
    head_ref, own_ref, other_ref, slope_ref, up_ref, down_ref, *refs
):
    normed_ref, act_ref = refs[:2]
    grad_ref, pre_ref, part_ref, b_up_ref, b_down_ref = refs[2:7]
    step, acc = pl.program_id(0), refs[-1]

    @pl.when(step == 0)
    def _():
        grad = ordered(head_ref, own_ref[...], other_ref[...])
        grad_ref[...] = grad
        b_down_ref[...] = jnp.sum(grad.astype(F32), axis=0, keepdims=True)
        acc[...] = jnp.zeros_like(acc)

    pre = (slope_ref[...].astype(F32) * nn(grad_ref[...], down_ref[...])).astype(LOW)
    pre_ref[...] = pre
    b_up_ref[...] = jnp.sum(pre.astype(F32), axis=0, keepdims=True)
    acc[...] += nt(pre, up_ref[...])
    refs[7][...] = tn(grad_ref[...], act_ref[...]).astype(LOW)
    refs[8][...] = tn(normed_ref[...], pre).astype(LOW)

    @pl.when(step == pl.num_programs(0) - 1)
    def _():
        part_ref[...] = acc[...].astype(LOW)


def inner_back_kernel(
    fused, head_ref, p_ref, po_ref, hidden_ref, grad_ref, trans_ref, gain_ref, out_w_ref,
    q_ref, kv_ref, wr_ref, basis_ref, probs_ref, *refs
):
    spots_ref, normed_ref, out_ref = refs[:3] if fused else (None, None, None)
    outs = refs[3 * fused :]
    proj_ref, resid_ref, gain_sum_ref, bias_sum_ref, dq_ref, dkv_ref, dwr_ref, far_ref = outs[:8]
    attended = outs[-1]
    grad_normed = p_ref[...].astype(F32) + po_ref[...].astype(F32)
    hat, scale = normalize(hidden_ref[...])
    gain_sum_ref[...] = jnp.sum(grad_normed * hat, axis=0, keepdims=True)
    bias_sum_ref[...] = jnp.sum(grad_normed, axis=0, keepdims=True)
    through = norm_back(grad_normed, hat, scale, gain_ref[...])
    resid_ref[...] = trans_ref[...] + my_half(head_ref, through)[0]
    proj = (grad_ref[...].astype(F32) + through).astype(LOW)
    proj_ref[...] = proj
    attended[...] = nn(proj, out_w_ref[...]).astype(LOW)
    attend_back_kernel(
        q_ref, kv_ref, wr_ref, basis_ref, probs_ref, attended, dq_ref, dkv_ref, dwr_ref
    )
    far_ref[...] = dkv_ref[far_ref.shape[0] :]
    if fused:
        kw = dq_ref.shape[1]
        columns_product(spots_ref, proj_ref, out_ref[...], outs[8], slice(None))
        columns_product(spots_ref, normed_ref, dq_ref[...], outs[9], slice(0, kw))
        columns_product(spots_ref, normed_ref, dkv_ref[...], outs[9], slice(kw, None))


def point_back_kernel(head_ref, grad_ref, point_ref, mine_ref, send_ref, bias_ref):
    grad = grad_ref[...]
    bias_ref[...] = jnp.sum(grad[: grad.shape[0] - 16].astype(F32), axis=0, keepdims=True)
    mine, theirs = my_half(head_ref, nt(grad, point_ref[...]))
    mine_ref[...] = mine
    send_ref[...] = theirs.astype(LOW)


def before(a, edge):
    row = lax.broadcasted_iota(jnp.int32, a.shape, 0)
    return jnp.where(row == 0, edge, pltpu.roll(a, 1, 0))


def behind(a, edge):
    row = lax.broadcasted_iota(jnp.int32, a.shape, 0)
    return jnp.where(row == a.shape[0] - 1, edge, pltpu.roll(a, a.shape[0] - 1, 0))


def section_back_kernel(mine_ref, got_ref, tap0, tap1, tap2, gm_ref, low_ref, coarse_ref, bias_ref):
    n = coarse_ref.shape[0]
    gm = mine_ref[...] + got_ref[...].astype(F32)
    gm_ref[...] = gm[: 2 * n]
    even, odd = gm[:n], gm[n : 2 * n]
    prev, later = gm[2 * n : 2 * n + 1], gm[2 * n + 1 : 2 * n + 2]
    gs_even = tap0[...] * odd + tap1[...] * even + tap2[...] * before(odd, prev)
    gs_odd = tap0[...] * behind(even, later) + tap1[...] * odd + tap2[...] * even
    coarse_ref[...] = gs_even + gs_odd
    gs = jnp.concatenate([gs_even, gs_odd], axis=0).astype(LOW)
    low_ref[...] = gs
    bias_ref[...] = jnp.sum(gs.astype(F32), axis=0, keepdims=True)


def section_kernel(trans_ref, skip_ref, prev_ref, later_ref, gm_ref, tap0, tap1, tap2, mixed_ref, depth_ref):
    n = trans_ref.shape[0]
    coarse = gelu(trans_ref[...])
    s_even, s_odd = coarse + skip_ref[:n], coarse + skip_ref[n:]
    s_before, s_after = before(s_odd, prev_ref[...]), behind(s_even, later_ref[...])
    mixed_ref[:n] = (tap0[...] * s_before + tap1[...] * s_even + tap2[...] * s_odd).astype(LOW)
    mixed_ref[n:] = (tap0[...] * s_even + tap1[...] * s_odd + tap2[...] * s_after).astype(LOW)
    even, odd = gm_ref[:n], gm_ref[n:]
    for k, a, b in ((0, s_before, s_even), (1, s_even, s_odd), (2, s_odd, s_after)):
        depth_ref[k : k + 1] = jnp.sum(even * a + odd * b, axis=0, keepdims=True)


def project_back_kernel(rows, dq_ref, *refs):
    parts, (qk_ref, v_ref, out_ref) = refs[:rows], refs[rows:]
    kw = dq_ref.shape[1]
    dkv = parts[0][...].astype(F32)
    for k in range(1, rows):
        dkv = dkv + parts[k][...].astype(F32)
    dkv = dkv.astype(LOW)
    dqk = jnp.concatenate([dq_ref[...], dkv[:, :kw]], axis=1)
    out_ref[...] = (nt(dqk, qk_ref[...]) + nt(dkv[:, kw:], v_ref[...])).astype(LOW)


def outer_back_kernel(
    head_ref, own_ref, other_ref, p_ref, po_ref, gain_ref, resid_ref, grad_ref, gain_sum_ref, bias_sum_ref
):
    hat, scale = normalize(
        ordered(head_ref, own_ref[...].astype(F32), other_ref[...].astype(F32))
    )
    grad_normed = p_ref[...].astype(F32) + po_ref[...].astype(F32)
    gain_sum_ref[...] = jnp.sum(grad_normed * hat, axis=0, keepdims=True)
    bias_sum_ref[...] = jnp.sum(grad_normed, axis=0, keepdims=True)
    through = norm_back(grad_normed, hat, scale, gain_ref[...])
    grad_ref[...] = resid_ref[...] + my_half(head_ref, through)[0]


def position_windows(z, width, rows):
    seq = width * rows
    block = jnp.bitwise_xor(z, np.array(bit_order(rows), np.int32)) - z
    t = block[:, None] * width + (np.arange(2 * width) - (width - 1))[None, :]
    distance = t.reshape(-1).astype(F32)
    magnitude = jnp.abs(distance)[:, None]
    number = NB // 4
    steps_up = np.arange(number, dtype=np.float32)
    half_life = (3.0 * (seq / 3.0) ** (steps_up / max(number - 1, 1))).astype(np.float32)
    decays = jnp.exp(-0.6931471805599453 * magnitude / half_life)
    central = (2.0 ** (steps_up + 1.0) - 1.0 > magnitude).astype(F32)
    even = jnp.concatenate([decays, central], axis=1)
    return jnp.concatenate([even, jnp.sign(distance)[:, None] * even], axis=1).astype(LOW)


G0, G1 = 0.7978845608028654, 0.044715


def gelu(u):
    return 0.5 * u * (1.0 + jnp.tanh(G0 * (u + G1 * u * u * u)))


def gelu_slope(u):
    t = jnp.tanh(G0 * (u + G1 * u * u * u))
    return 0.5 * (1.0 + t) + 0.5 * u * (1.0 - t * t) * (G0 * (1.0 + 3.0 * G1 * u * u))


def normalize(values):
    centered = values - jnp.mean(values, axis=-1, keepdims=True)
    scale = lax.rsqrt(jnp.mean(centered * centered, axis=-1, keepdims=True) + EPS)
    return centered * scale, scale


def norm_back(grad, hat, scale, gain):
    gg = grad * gain
    return scale * (
        gg
        - jnp.mean(gg, axis=-1, keepdims=True)
        - hat * jnp.mean(gg * hat, axis=-1, keepdims=True)
    )


def pick(head, own, other):
    return jnp.where(head == 0, own, other), jnp.where(head == 0, other, own)


def both_halves(head, own, other):
    return jnp.concatenate(pick(head, own, other), axis=1)


def half(a, head):
    n = a.shape[1] // 2
    return lax.dynamic_slice_in_dim(a, head * n, n, 1)


def one_hot(select, height, width):
    ii = lax.broadcasted_iota(jnp.int32, (height, width), 0)
    jj = lax.broadcasted_iota(jnp.int32, (height, width), 1)
    return select(ii, jj).astype(LOW)


def from_before(row):
    n = lax.axis_size(RW)
    return lax.ppermute(row, RW, [(i, i + 1) for i in range(n - 1)])


def from_behind(row):
    n = lax.axis_size(RW)
    return lax.ppermute(row, RW, [(i + 1, i) for i in range(n - 1)])


def shards(
    inputs,
    skip_input,
    cotangent,
    track_mask,
    norm1_gain,
    norm1_bias,
    query_weight,
    key_weight,
    value_weight,
    rel_weight,
    out_weight,
    norm2_gain,
    norm2_bias,
    up_weight,
    up_bias,
    down_weight,
    down_bias,
    skip_weight,
    skip_bias,
    depth_weight,
    point_weight,
    point_bias,
):
    head = lax.axis_index(HD)
    _, _, z = place()
    rows = lax.axis_size(RW)
    group = lax.axis_size(IT) * rows
    width, chan = inputs.shape[1], inputs.shape[2]
    model = 2 * chan
    heads = rel_weight.shape[0]
    kw = heads * KEY
    shard = norm1_gain.shape[0]
    small = skip_bias.shape[1]
    rel_cols = rel_weight.shape[1]

    skip_rows = skip_weight.shape[0]
    flat = jnp.concatenate(
        [norm1_gain, norm1_bias, norm2_gain, norm2_bias, down_bias, up_bias[0]]
        + [skip_bias[0], depth_weight.reshape(-1), point_bias[0], rel_weight.reshape(-1)]
    ).astype(LOW)
    spare = shard - skip_rows
    singles = [norm1_gain, norm1_bias, norm2_gain, norm2_bias, down_bias, up_bias]
    singles += [skip_bias, depth_weight, point_bias, rel_weight]
    flat = jnp.pad(flat, (0, spare * chan - flat.size)).reshape(spare, chan)
    ff = up_weight.shape[1]
    order = [up_weight, down_weight.T, out_weight.T, point_weight]
    order += [jnp.concatenate([skip_weight.astype(LOW), flat], axis=0)]
    order += [value_weight, query_weight, key_weight]
    if shard % 16 == 0 and skip_rows % 16 == 0 and spare == 16:
        order[4] = skip_weight
        singles = [v.reshape(-1, v.shape[-1]) for v in singles]
        (piece,) = run(
            functools.partial(pack_kernel, len(order)),
            1,
            order + singles,
            [new((shard, sum(w.shape[1] for w in order)), LOW)],
            [pltpu.VMEM((spare, chan), F32)],
        )
    else:
        piece = jnp.concatenate([w.astype(LOW) for w in order], axis=1)
    big = lax.all_gather(piece, (IT, RW), axis=0, tiled=True)
    at = 2 * ff

    def columns(start, count):
        return (big, (model, count), lambda i: (0, start // count))

    w_out, w_value = columns(at, chan), columns(at + 3 * chan, heads * VAL)
    w_qk = columns(at + 3 * chan + heads * VAL, 2 * kw)
    w_point = columns(at + chan, chan)
    steps = 3
    cut = ff // steps
    w_up = (big, (model, cut), lambda i: (0, i))
    w_down = (big, (model, cut), lambda i: (0, steps + i))
    if shard % 16 == 0 and skip_rows % 16 == 0 and spare == 16 and NB % group == 0:
        lengths = [shard] * 6 + [small] * 5
        w_skip, w_rel, *singles = run(
            functools.partial(unpack_kernel, shard, skip_rows, lengths),
            1,
            [columns(at + 2 * chan, chan)],
            [new((group * skip_rows, chan), LOW), new((heads * NB, KEY), F32)]
            + [new((1, group * n), F32) for n in lengths],
        )
        gain_one, bias_one, gain_two, bias_two, b_down, b_up = singles[:6]
        b_skip, tap0, tap1, tap2, b_point = singles[6:]
    else:
        last = big[:, at + 2 * chan : at + 3 * chan].reshape(group, shard, chan)
        w_skip = last[:, :skip_rows].reshape(group * skip_rows, chan)
        tails = last[:, skip_rows:].reshape(group, -1)

        def vector(start, count):
            return wide(tails[:, start : start + count]).reshape(1, -1)

        gain_one, bias_one, gain_two, bias_two, b_down, b_up = (
            vector(i * shard, shard) for i in range(6)
        )
        at = 6 * shard
        b_skip, tap0, tap1, tap2, b_point = (vector(at + i * small, small) for i in range(5))
        at += 5 * small
        w_rel = tails[:, at : at + heads * rel_cols].reshape(group, heads, rel_cols)
        w_rel = w_rel.transpose(1, 0, 2).reshape(heads * NB, KEY)

    at_head = (head.reshape(1).astype(jnp.int32), None, None)
    even = one_hot(lambda i, j: j == 2 * i, width, 2 * width)
    odd = one_hot(lambda i, j: j == 2 * i + 1, width, 2 * width)
    apart = jnp.concatenate([even, odd], axis=0)
    masked = (wide(cotangent[0]) * wide(track_mask)).astype(LOW)
    edges = [from_before(masked[-1:]), from_behind(masked[:1]), jnp.zeros((14, chan), LOW)]
    grad_out = nn(apart, masked).astype(LOW)
    grad_rows = jnp.concatenate([grad_out] + edges, axis=0)
    skip_low = nn(apart, gelu(wide(skip_input[0])).astype(LOW)).astype(LOW)

    own_blocks = [to_bit(inputs[0], k) if k else inputs[0] for k in bit_order(rows)]
    other_blocks = [to_head(b) for b in own_blocks]
    basis = position_windows(z, width, rows)
    queries, kv, normed_all = run(
        functools.partial(project_kernel, rows),
        1,
        [at_head] + own_blocks + other_blocks + [gain_one, bias_one, w_qk, w_value],
        [new((width, kw), LOW), new((rows * width, kw + heads * VAL), LOW)]
        + [new((rows * width, model), LOW)],
        after=[skip_low, grad_rows, basis],
    )
    attended, probs, partial_attn = run(
        attend_out_kernel,
        1,
        [queries, kv, w_rel, basis, w_out],
        [new((width, heads * VAL), LOW), new((heads, width, rows * width), LOW)]
        + [new((width, model), LOW)],
    )
    skip_term = nn(skip_low, w_skip) + b_skip
    gm_mine, gm_send, grad_point_bias = run(
        point_back_kernel,
        1,
        [at_head, grad_rows, w_point],
        [new((2 * width + 16, chan), F32), new((2 * width + 16, chan), LOW), new((1, chan), F32)],
        after=[partial_attn],
    )
    grad_mixed, grad_skip_low, grad_coarse, grad_skip_bias = run(
        section_back_kernel,
        1,
        [gm_mine, to_head(gm_send), tap0, tap1, tap2],
        [new((2 * width, chan), F32), new((2 * width, chan), LOW)]
        + [new((width, chan), F32), new((1, chan), F32)],
    )

    by_cut = (width, cut), lambda i: (0, i)
    hidden, normed_two, activated, slope, trans, send = run(
        ff_kernel,
        steps,
        [at_head, own_blocks[0], other_blocks[0], partial_attn, to_head(partial_attn)]
        + [gain_two, bias_two, (b_up, (1, cut), lambda i: (0, i)), b_down, w_up, w_down],
        [new((width, model), F32), new((width, model), LOW), (new((width, ff), LOW), *by_cut)]
        + [(new((width, ff), LOW), *by_cut), new((width, chan), F32), new((width, chan), LOW)],
        [pltpu.VMEM((width, model), F32)],
        after=[skip_term],
    )
    trans = trans + wide(to_head(send))

    for_skip = Scatter([(skip_low, grad_skip_low)])

    s_first = gelu(trans[:1]) + skip_term[:1]
    s_last = gelu(trans[-1:]) + skip_term[-1:]
    prev, later = wide(from_before(low(s_last))), wide(from_behind(low(s_first)))

    grad_trans = gelu_slope(trans) * grad_coarse
    grad_own = low(grad_trans)
    owned = model // lax.axis_size(IT)
    fused = fits(owned)
    core_rows = model // 2
    spots = jnp.stack(spots_of(1 - place()[1], owned)).astype(jnp.int32), None, None
    extra = new((model, ff), LOW), (model, cut), lambda i: (0, i)
    grad_ff_low, grad_pre_low, partial_two, grad_up_bias, grad_down_bias, *theirs = run(
        ff_back_kernel,
        steps,
        [at_head, grad_own, to_head(grad_own), (slope, *by_cut), w_up, w_down]
        + [normed_two, (activated, *by_cut)],
        [new((width, model), LOW), (new((width, ff), LOW), *by_cut), new((width, model), LOW)]
        + [(new((1, ff), F32), (1, cut), lambda i: (0, i)), new((1, model), F32)]
        + [extra, extra],
        [pltpu.VMEM((width, model), F32)],
        after=[prev, later],
    )
    for_down, for_up = (
        RowSum(lax.psum_scatter(t, IT, scatter_dimension=0, tiled=True)) for t in theirs
    )
    mixed, grad_depth = run(
        section_kernel,
        1,
        [trans, skip_term, prev, later, grad_mixed, tap0, tap1, tap2],
        [new((2 * width, chan), LOW), new((3, chan), F32)],
    )
    grad_proj_low, resid, grad_gain_two, grad_bias_two, dq, dkv, grad_rel, far, *theirs = run(
        functools.partial(inner_back_kernel, fused),
        1,
        [at_head, partial_two, to_head(partial_two), hidden, grad_ff_low, grad_trans, gain_two]
        + [w_out, queries, kv, w_rel, basis, probs]
        + [spots, normed_all, attended][: 3 * fused],
        [new((width, model), LOW), new((width, chan), F32)]
        + [new((1, model), F32), new((1, model), F32)]
        + [new(queries.shape, LOW), new(kv.shape, LOW), new(w_rel.shape, F32)]
        + [new((kv.shape[0] // 2, kv.shape[1]), LOW)]
        + [new((core_rows, heads * VAL), LOW), new((core_rows, kw + kv.shape[1]), LOW)][: 2 * fused],
        [pltpu.VMEM((width, heads * VAL), LOW)],
        after=for_skip.send + [mixed],
    )
    dkv_parts, rest, bit, arrived = [dkv[:width]], dkv, 1, []
    summed = []
    while bit < rows:
        n = rest.shape[0] // 2
        got = to_bit(far if bit == 1 else rest[n:], bit)
        dkv_parts.append(got[:width])
        arrived.append(got)
        if n > width:
            rest = low(wide(rest[:n]) + wide(got))
            dkv_parts = [rest[:width]]
            summed.append(rest)
        bit *= 2
    skip_across = [for_skip.across(0)]
    mixed_other = to_head(mixed)
    skip_across = [for_skip.across(0)]
    for_skip.take(skip_across)
    for_attn = Scatter(
        [(grad_proj_low, attended), (normed_all, dq), (normed_all, dkv)],
        theirs or None,
        [],
        skip_across[0],
        [[0, 1, 2]],
    )
    mixed_full = both_halves(head, mixed, mixed_other)
    for_point = Scatter([(mixed_full, grad_out)], None, [], for_attn.send)
    for_down.step(for_point.theirs)
    attn_across = [for_attn.across(0)]
    for_attn.take(attn_across)
    point_across = for_point.across(0)
    for_point.take([point_across])
    (partial_one,) = run(
        functools.partial(project_back_kernel, len(dkv_parts)),
        1,
        [dq] + dkv_parts + [w_qk, w_value],
        [new((width, model), LOW)],
        after=for_point.send + [for_down.sent],
    )
    for_down.step([partial_one])
    for_up.step([for_down.sent])
    for_attn.step([for_up.sent])
    for_skip.step([for_attn.sent])
    for_point.step([for_skip.sent])
    input_grad, grad_gain_one, grad_bias_one = run(
        outer_back_kernel,
        1,
        [at_head, own_blocks[0], other_blocks[0], partial_one, to_head(partial_one)]
        + [gain_one, resid],
        [new((width, chan), F32), new((1, model), F32), new((1, model), F32)],
        after=[for_point.sent] + for_up.got + for_down.got,
    )
    input_grad = input_grad[None]
    for_attn.step([grad_gain_one])
    for_up.step([for_attn.sent] + for_skip.got)
    for_point.step([for_up.sent])
    for_skip.step([for_point.sent])
    early = last = [for_skip.sent]
    (grad_down,), (grad_up,) = for_down.finish(early), for_up.finish(early)
    (grad_skip,), (grad_point,) = for_skip.finish(last), for_point.finish(last)
    grad_out_w, *grad_qkv = for_attn.finish(early, [heads * VAL, kw, kw, heads * VAL])
    result = (nn(mixed_full, w_point[0][:, 2 * ff + chan : 2 * ff + 2 * chan]) + b_point).astype(LOW)
    block_output = tn(apart, result).astype(LOW)[None]
    parts = [grad_gain_one, grad_bias_one, grad_gain_two, grad_bias_two, grad_down_bias]
    parts += [grad_up_bias, grad_skip_bias] + [grad_depth] * 3 + [grad_point_bias]
    which = [0] * 7 + [0, 1, 2] + [0]
    if NB % group == 0:
        shares = [(i, p.shape[-1] // group) for i, p in zip(which, parts)]
        total = sum(n for _, n in shares) + heads * rel_cols
        (parts,) = run(
            functools.partial(pack_sums_kernel, shares),
            1,
            [p.reshape(-1, p.shape[-1]) for p in parts] + [grad_rel],
            [new((group, total), F32)],
        )
    else:
        parts = [p.reshape(-1, p.shape[-1])[i] for i, p in zip(which, parts)]
        rel_parts = grad_rel.reshape(heads, group, rel_cols).transpose(1, 0, 2)
        parts = [p.reshape(group, -1) for p in parts + [rel_parts]]
        parts = jnp.concatenate(parts, axis=1)
    sums = scatter_small(parts, last)

    def own(start, count):
        return sums[0, start : start + count]

    at = 6 * shard
    return (
        block_output,
        input_grad,
        own(0, shard),
        own(shard, shard),
        *grad_qkv,
        own(at + 5 * small, heads * rel_cols).reshape(heads, rel_cols),
        grad_out_w.T,
        own(2 * shard, shard),
        own(3 * shard, shard),
        grad_up,
        own(5 * shard, shard)[None],
        grad_down.T,
        own(4 * shard, shard),
        grad_skip,
        own(at, small)[None],
        own(at + small, 3 * small).reshape(3, 1, small),
        grad_point,
        own(at + 4 * small, small)[None],
    )


def solution(mesh):
    gr = (IT, RW)
    vec, cols, rws = P(gr), P(gr, HD), P(HD, gr)
    act = P(IT, RW, HD)
    taps = P(None, HD, gr)
    weights = (vec, vec, cols, cols, cols, rws, rws, vec, vec, cols, rws, rws, vec, cols, rws)
    weights += (taps, cols, rws)
    return jax.shard_map(
        shards,
        mesh=mesh,
        in_specs=(act, P(IT, RW, None), act, P(IT, HD)) + weights,
        out_specs=(act, act) + weights,
        check_vma=False,
    )
```

```python
import functools

import jax
import jax.numpy as jnp
import numpy as np
from jax import lax
from jax.experimental import pallas as pl
from jax.experimental.pallas import tpu as pltpu
from jax.sharding import PartitionSpec as P

KEY = 64
VAL = 192
NB = 32
EPS = 1e-05
IT, HD, RW = "items", "heads", "rows"
LOW = jnp.bfloat16
F32 = jnp.float32
VMEM = pltpu.CompilerParams(vmem_limit_bytes=56 * 2**20)
SHORT = pl.CostEstimate(flops=1, bytes_accessed=1, transcendentals=0)


def nn(a, b):
    return lax.dot_general(a, b, (((1,), (0,)), ((), ())), preferred_element_type=F32)


def nt(a, b):
    return lax.dot_general(a, b, (((1,), (1,)), ((), ())), preferred_element_type=F32)


def tn(a, b):
    return lax.dot_general(a, b, (((0,), (0,)), ((), ())), preferred_element_type=F32)


def wide(a):
    return a.astype(F32)


def low(a):
    return lax.reduce_precision(a, 8, 7).astype(LOW)


def bit_order(n):
    out, bit = [0], n // 2
    while bit:
        out += [i + bit for i in out]
        bit //= 2
    return out


def to_core(a):
    n = lax.axis_size(IT)
    return lax.ppermute(a, IT, [(i, i ^ 1) for i in range(n)])


def to_pair(a, k):
    n = lax.axis_size(IT)
    return lax.ppermute(a, IT, [(i, (i + 2 * k) % n) for i in range(n)])


def to_head(a):
    return lax.ppermute(a, HD, [(0, 1), (1, 0)])


def place():
    item = lax.axis_index(IT)
    return item // 2, item % 2, lax.axis_index(RW)


def to_bit(a, bit):
    n = lax.axis_size(RW)
    return lax.ppermute(a, RW, [(i, i ^ bit) for i in range(n)])


def halve(keep, got, pick_bit, pieces, after=()):
    w, n = keep.shape[0] // pieces, keep.shape[1]
    shape = (pieces // 2, 2, w, n)
    if w % 16:
        total = wide(keep)
        if got:
            total = total + wide(jnp.concatenate(got, axis=1))
        total = total.reshape(shape)
        mine = lax.dynamic_index_in_dim(total, pick_bit, 1, keepdims=False)
        send = lax.dynamic_index_in_dim(total, 1 - pick_bit, 1, keepdims=False)
        return mine.reshape(-1, n), low(send).reshape(-1, n)
    widths = [g.shape[1] for g in got]

    def body(bit_ref, keep_ref, *refs):
        got_refs, (mine_ref, send_ref) = refs[:-2], refs[-2:]

        def write(bit):
            if not got:
                mine_ref[0] = keep_ref[0, bit].astype(F32)
                send_ref[0] = keep_ref[0, 1 - bit].astype(LOW)
            at = 0
            for ref, count in zip(got_refs, widths):
                there = slice(at, at + count)
                at += count
                mine_ref[0, :, there] = keep_ref[0, bit, :, there] + ref[0, bit].astype(F32)
                total = keep_ref[0, 1 - bit, :, there] + ref[0, 1 - bit].astype(F32)
                send_ref[0, :, there] = total.astype(LOW)

        for bit in range(2):
            pl.when(bit_ref[0] == bit)(functools.partial(write, bit))

    def block(count):
        return (1, 2, w, count), lambda i: (i, 0, 0, 0)

    out = (1, w, n), lambda i: (i, 0, 0)
    half_shape = (pieces // 2, w, n)
    mine, send = run(
        body,
        pieces // 2,
        [(pick_bit.reshape(1), None, None), (keep.reshape(shape), *block(n))]
        + [(g.reshape(pieces // 2, 2, w, count), *block(count)) for g, count in zip(got, widths)],
        [(new(half_shape, F32), *out), (new(half_shape, LOW), *out)],
        after=after,
    )
    return mine.reshape(-1, n), send.reshape(-1, n)


def find(bounds, start, end):
    at = next(i for i, (a, b) in enumerate(bounds) if a <= start and end <= b)
    return at, slice(start - bounds[at][0], end - bounds[at][0])


def bounds_of(arrays):
    ends = [int(e) for e in np.cumsum([0] + [a.shape[1] for a in arrays])]
    return list(zip(ends, ends[1:]))


def spots_of(side, w):
    pairs = lax.axis_size(IT) // 2
    x, _, _ = place()
    return [(((x + k) % pairs) * 2 + side) for k in range(pairs)]


def fits(w):
    rows = lax.axis_size(RW)
    return lax.axis_size(IT) == 4 and w % 128 == 0 and (w // rows) % 16 == 0


def columns_product(spots_ref, left_ref, right, out_ref, there):
    count = spots_ref.shape[0]
    w = out_ref.shape[0] // count
    for k in range(count):
        start = pl.multiple_of(spots_ref[k] * w, 128)
        left = left_ref[pl.ds(0, right.shape[0]), pl.ds(start, w)]
        out_ref[k * w : (k + 1) * w, there] = tn(left, right).astype(LOW)


def add_last(keep, got, after, widths):
    ends = [int(e) for e in np.cumsum([0] + widths)]
    cuts = [slice(i, j) for i, j in zip(ends, ends[1:])]
    if keep.shape[0] % 16:
        return [(keep + wide(got))[:, cut] for cut in cuts]

    def body(keep_ref, got_ref, *outs):
        for cut, out_ref in zip(cuts, outs):
            out_ref[...] = keep_ref[:, cut] + got_ref[:, cut].astype(F32)

    outs = [new((keep.shape[0], n), F32) for n in widths]
    return list(run(body, 1, [keep, got], outs, after=after))


def side_product(pairs_of, side, got=None, after=(), groups=None, others=False):
    pairs = lax.axis_size(IT) // 2
    w = pairs_of[0][0].shape[1] // (2 * pairs)
    spots = spots_of(side, w)
    cols = [right.shape[1] for _, right in pairs_of]
    ends = [int(e) for e in np.cumsum([0] + cols)]
    groups = groups or [[k] for k in range(len(cols))]
    bounds = [(ends[g[0]], ends[g[-1] + 1]) for g in groups]
    if w % 128:
        out = []
        for left, right in pairs_of:
            part = [lax.dynamic_slice_in_dim(left, spot * w, w, 1) for spot in spots]
            out.append(tn(jnp.concatenate(part, axis=1)[: right.shape[0]], right))
        out = jnp.concatenate(out, axis=1)
        if got is None:
            return low(out)
        out = out + wide(jnp.concatenate(got, axis=1))
        return out[:w], [low(out[w:, i:j]) for i, j in bounds]
    n, count, m = sum(cols), len(pairs_of), len(after)
    first = int(others)
    got = got or []
    got_bounds = bounds_of(got)

    def body(spot_ref, *refs):
        lefts, rights = refs[:count], refs[count : 2 * count]
        gots = refs[2 * count : 2 * count + len(got)]
        outs = refs[2 * count + len(got) + m :]
        if others:
            outs = (None,) + tuple(outs)
        step = pl.program_id(0)
        for k in range(count):
            there = slice(ends[k], ends[k + 1])
            to = next(i for i, g in enumerate(groups) if k in g)
            inside = slice(ends[k] - bounds[to][0], ends[k + 1] - bounds[to][0])
            part = tn(lefts[k][...], rights[k][...])
            if not got:
                outs[0][:, there] = part.astype(LOW)
                continue
            which, where = find(got_bounds, ends[k], ends[k + 1])
            part = part + gots[which][:, where].astype(F32)

            if others:
                outs[1 + to][:, inside] = part.astype(LOW)
                continue

            @pl.when(step == 0)
            def _(part=part, there=there):
                outs[0][:, there] = part

            @pl.when(step > 0)
            def _(part=part, to=to, inside=inside):
                outs[1 + to][:, inside] = part.astype(LOW)

    specs = [
        pl.BlockSpec((right.shape[0], w), lambda i, spot: (0, spot[i])) for left, right in pairs_of
    ] + [pl.BlockSpec(right.shape, lambda i, spot: (0, 0)) for _, right in pairs_of]
    operands = [left for left, _ in pairs_of] + [right for _, right in pairs_of]
    specs += [pl.BlockSpec((w, g.shape[1]), lambda i, spot: (i + first, 0)) for g in got]
    operands += got
    if not got:
        out_specs = [pl.BlockSpec((w, n), lambda i, spot: (i, 0))]
        out_shape = [new((pairs * w, n), LOW)]
    else:
        out_specs, out_shape = [pl.BlockSpec((w, n), lambda i, spot: (0, 0))], [new((w, n), F32)]
        for c in [j - i for i, j in bounds]:
            out_specs.append(
                pl.BlockSpec((w, c), lambda i, spot: (jnp.maximum(i - 1 + first, 0), 0))
            )
            out_shape.append(new(((pairs - 1) * w, c), LOW))
        out_specs, out_shape = out_specs[first:], out_shape[first:]
    out = pl.pallas_call(
        body,
        grid_spec=pltpu.PrefetchScalarGridSpec(
            num_scalar_prefetch=1,
            grid=(pairs - first,),
            in_specs=specs + [pl.BlockSpec(memory_space=pl.ANY)] * m,
            out_specs=out_specs,
        ),
        out_shape=out_shape,
        compiler_params=VMEM,
        cost_estimate=SHORT,
    )(jnp.stack(spots[first:]).astype(jnp.int32), *operands, *after)
    if others:
        return list(out)
    return (out[0], list(out[1:])) if got else out[0]


def product_halve(pairs_of, spot, core, terms, pick_bit, pieces, after=()):
    w = pairs_of[0][0].shape[1] // (2 * (lax.axis_size(IT) // 2))
    cols = [right.shape[1] for _, right in pairs_of]
    ends = [int(e) for e in np.cumsum([0] + cols)]
    n, count, m = ends[-1], len(pairs_of), len(after)
    widths = [g.shape[1] for g in terms]
    piece = w // pieces
    core_bounds = bounds_of(core)

    def body(at_ref, *refs):
        lefts, rights = refs[:count], refs[count : 2 * count]
        at = 2 * count + len(core)
        core_refs, term_refs = refs[2 * count : at], refs[at : at + len(terms)]
        mine_ref, send_ref, total = refs[at + len(terms) + m :]
        for k in range(count):
            there = slice(ends[k], ends[k + 1])
            which, where = find(core_bounds, ends[k], ends[k + 1])
            part = core_refs[which][:, where].astype(F32)
            total[:, there] = tn(lefts[k][...], rights[k][...]) + part
        at = 0
        for ref, wide_n in zip(term_refs, widths):
            there = slice(at, at + wide_n)
            at += wide_n
            total[:, there] += ref[...].astype(F32)
        for i in range(pieces // 2):
            out = slice(i * piece, (i + 1) * piece)
            for bit in range(2):

                @pl.when(at_ref[1] == bit)
                def _(i=i, bit=bit, out=out):
                    mine = (2 * i + bit) * piece
                    send = (2 * i + 1 - bit) * piece
                    mine_ref[out] = total[mine : mine + piece]
                    send_ref[out] = total[send : send + piece].astype(LOW)

    in_specs = [
        pl.BlockSpec((right.shape[0], w), lambda i, at: (0, at[0])) for _, right in pairs_of
    ] + [pl.BlockSpec(right.shape, lambda i, at: (0, 0)) for _, right in pairs_of]
    in_specs += [pl.BlockSpec((w, g.shape[1]), lambda i, at: (0, 0)) for g in core]
    in_specs += [pl.BlockSpec(t.shape, lambda i, at: (0, 0)) for t in terms]
    out_spec = pl.BlockSpec((w // 2, n), lambda i, at: (0, 0))
    return pl.pallas_call(
        body,
        grid_spec=pltpu.PrefetchScalarGridSpec(
            num_scalar_prefetch=1,
            grid=(1,),
            in_specs=in_specs + [pl.BlockSpec(memory_space=pl.ANY)] * m,
            out_specs=[out_spec, out_spec],
            scratch_shapes=[pltpu.VMEM((w, n), F32)],
        ),
        out_shape=[new((w // 2, n), F32), new((w // 2, n), LOW)],
        compiler_params=VMEM,
        cost_estimate=SHORT,
    )(
        jnp.stack([spot, pick_bit]).astype(jnp.int32),
        *[left for left, _ in pairs_of],
        *[right for _, right in pairs_of],
        *core,
        *terms,
        *after,
    )


class Scatter:
    def __init__(self, pairs_of, theirs=None, after=(), after_more=(), groups=None):
        pairs = lax.axis_size(IT) // 2
        self.x, self.c, self.z = place()
        self.pairs_of, self.groups = pairs_of, groups
        self.plain = not fits(pairs_of[0][0].shape[1] // (2 * pairs))
        if theirs is None:
            theirs = [side_product(pairs_of, 1 - self.c, None, after)]
        self.theirs = theirs
        self.core = [to_core(t) for t in theirs]
        if self.plain:
            self.keep, self.send = side_product(pairs_of, self.c, self.core, after_more, groups)
        else:
            self.send = side_product(
                pairs_of, self.c, self.core, after_more, groups, others=True
            )
        self.bit = 1

    def across(self, i):
        pairs = lax.axis_size(IT) // 2
        w = self.send[i].shape[0] // (pairs - 1)
        return [to_pair(self.send[i][(k - 1) * w : k * w], k) for k in range(1, pairs)]

    def take(self, got):
        if self.plain:
            for terms in zip(*[g[:-1] for g in got]):
                self.keep = self.keep + wide(jnp.concatenate(terms, axis=1))
        self.got = [g[-1] for g in got]

    def step(self, after=()):
        pieces = lax.axis_size(RW) // self.bit
        pick_bit = (self.z // self.bit) % 2
        if self.bit == 1 and not self.plain:
            self.keep, self.sent = product_halve(
                self.pairs_of, self.x * 2 + self.c, self.core, self.got, pick_bit, pieces, after
            )
        else:
            self.keep, self.sent = halve(self.keep, self.got, pick_bit, pieces, after)
        self.got = [to_bit(self.sent, self.bit)]
        self.bit *= 2
        return self.got

    def finish(self, after=(), widths=None):
        while self.bit < lax.axis_size(RW):
            self.step(after)
        return add_last(self.keep, self.got[0], after, widths or [self.keep.shape[1]])


class RowSum:
    def __init__(self, keep):
        self.keep, self.got, self.bit = keep, [], 1
        self.z = lax.axis_index(RW)

    def step(self, after=()):
        pieces = lax.axis_size(RW) // self.bit
        pick_bit = (self.z // self.bit) % 2
        self.keep, self.sent = halve(self.keep, self.got, pick_bit, pieces, after)
        self.got = [to_bit(self.sent, self.bit)]
        self.bit *= 2
        return self.got

    def finish(self, after=(), widths=None):
        while self.bit < lax.axis_size(RW):
            self.step(after)
        return add_last(self.keep, self.got[0], after, widths or [self.keep.shape[1]])


def scatter_small(parts, after):
    pairs, rows = lax.axis_size(IT) // 2, lax.axis_size(RW)
    x, c, z = place()
    n = parts.shape[1]
    cube = parts.reshape(pairs, 2, rows, n)
    cube = lax.dynamic_index_in_dim(cube, c, 1, keepdims=False) + to_core(
        lax.dynamic_index_in_dim(cube, 1 - c, 1, keepdims=False)
    )
    plane = lax.dynamic_index_in_dim(cube, x, 0, keepdims=False)
    for k in range(1, pairs):
        plane = plane + to_pair(
            lax.dynamic_index_in_dim(cube, (x + k) % pairs, 0, keepdims=False), k
        )
    terms = [lax.dynamic_index_in_dim(plane, z, 0, keepdims=True)]
    for k in range(1, rows):
        spot = jnp.bitwise_xor(z, k)
        terms.append(to_bit(lax.dynamic_index_in_dim(plane, spot, 0, keepdims=True), k))

    def body(*refs):
        refs[-1][...] = sum(ref[...] for ref in refs[1:-1]) + refs[0][...]

    return run(body, 1, terms, [new(terms[0].shape, F32)], after=after)[0]


def attend_kernel(q_ref, kv_ref, wr_ref, basis_ref, out_ref, p_ref):
    rows, seq, heads = q_ref.shape[0], kv_ref.shape[0], p_ref.shape[0]
    width = heads * KEY
    basis = basis_ref[...]
    outs = []
    for h in range(heads):
        qh = q_ref[:, h * KEY : (h + 1) * KEY]
        kh = kv_ref[:, h * KEY : (h + 1) * KEY]
        vh = kv_ref[:, width + h * VAL : width + (h + 1) * VAL]
        features = nt(qh, wr_ref[h * NB : (h + 1) * NB, :].astype(LOW)).astype(LOW)
        table = nt(features, basis)
        rel = [
            pltpu.roll(
                table[:, k * 2 * rows : (k + 1) * 2 * rows], rows + 1, 1, stride=1, stride_axis=0
            )[:, :rows]
            for k in range(seq // rows)
        ]
        logits = nt(qh, kh) + jnp.concatenate(rel, axis=1)
        e = jnp.exp(logits - jnp.max(logits, axis=1, keepdims=True))
        p = (e * (1.0 / jnp.sum(e, axis=1, keepdims=True))).astype(LOW)
        p_ref[h] = p
        outs.append(nn(p, vh))
    out_ref[...] = jnp.concatenate(outs, axis=1).astype(LOW)


def attend_back_kernel(q_ref, kv_ref, wr_ref, basis_ref, p_ref, g_ref, dq_ref, dkv_ref, dwr_ref):
    rows, seq, heads = q_ref.shape[0], kv_ref.shape[0], p_ref.shape[0]
    width = heads * KEY
    basis = basis_ref[...]
    ii = lax.broadcasted_iota(jnp.int32, (rows, rows), 0)
    jj = lax.broadcasted_iota(jnp.int32, (rows, rows), 1)
    flip = (ii + jj == rows - 1).astype(F32).astype(LOW)
    dqs, dks, dvs = [], [], []
    for h in range(heads):
        qh = q_ref[:, h * KEY : (h + 1) * KEY]
        kh = kv_ref[:, h * KEY : (h + 1) * KEY]
        vh = kv_ref[:, width + h * VAL : width + (h + 1) * VAL]
        gh = g_ref[:, h * VAL : (h + 1) * VAL]
        wr = wr_ref[h * NB : (h + 1) * NB, :].astype(LOW)
        p = p_ref[h]
        probs = p.astype(F32)
        dp = nt(gh, vh)
        inner = jnp.sum(probs * dp, axis=1, keepdims=True)
        ds = (probs * (dp - inner)).astype(LOW)
        dvs.append(tn(p, gh))
        dks.append(tn(ds, qh))
        rev = nn(flip, ds)
        zeros = jnp.zeros((rows, rows), F32)
        tabs = [
            pltpu.roll(
                jnp.concatenate([rev[:, k * rows : (k + 1) * rows], zeros], axis=1),
                0,
                1,
                stride=1,
                stride_axis=0,
            ).astype(LOW)
            for k in range(seq // rows)
        ]
        features = nn(jnp.concatenate(tabs, axis=1), basis).astype(LOW)
        features = nn(flip, features).astype(LOW)
        dqs.append(nn(ds, kh) + nn(features, wr))
        dwr_ref[h * NB : (h + 1) * NB, :] = tn(features, qh)
    dq = jnp.concatenate(dqs, axis=1).astype(LOW).astype(F32) * (KEY**-0.5)
    dq_ref[...] = dq.astype(LOW)
    dkv_ref[...] = jnp.concatenate(dks + dvs, axis=1).astype(LOW)


def run(body, grid, ins, outs, scratch=(), after=()):
    n, m = len(ins), len(after)

    def kernel(*refs):
        body(*refs[:n], *refs[n + m :])

    def spec(shape, index):
        if index is None:
            return pl.BlockSpec(memory_space=pltpu.SMEM)
        return pl.BlockSpec(shape, index)

    def whole(a):
        return (a, a.shape, lambda i: (0,) * a.ndim)

    full = [entry if isinstance(entry, tuple) else whole(entry) for entry in ins]
    out_full = [entry if isinstance(entry, tuple) else whole(entry) for entry in outs]
    return pl.pallas_call(
        kernel,
        grid=(grid,),
        in_specs=[spec(shape, index) for _, shape, index in full]
        + [pl.BlockSpec(memory_space=pl.ANY)] * m,
        out_specs=tuple(spec(shape, index) for _, shape, index in out_full),
        out_shape=tuple(a for a, _, _ in out_full),
        scratch_shapes=scratch,
        compiler_params=VMEM,
        cost_estimate=SHORT,
    )(*[a for a, _, _ in full], *after)


def new(shape, dtype):
    return jax.ShapeDtypeStruct(shape, dtype)


def ordered(head_ref, own, other):
    first = head_ref[0] == 0
    return jnp.concatenate([jnp.where(first, own, other), jnp.where(first, other, own)], axis=1)


def my_half(head_ref, a):
    n = a.shape[1] // 2
    first = head_ref[0] == 0
    return jnp.where(first, a[:, :n], a[:, n:]), jnp.where(first, a[:, n:], a[:, :n])


def pack_kernel(count, *refs):
    out_ref, rows_ref = refs[-2:]
    rows, height = rows_ref.shape[0], out_ref.shape[0]
    at = 0
    for ref in refs[:count]:
        there = slice(at, at + ref.shape[1])
        at += ref.shape[1]
        out_ref[: ref.shape[0], there] = ref[...].astype(LOW)
        if ref.shape[0] < height:
            below = there
    rows_ref[...] = jnp.zeros_like(rows_ref)
    spot, width = 0, rows_ref.shape[1]
    for ref in refs[count:-2]:
        for i in range(ref.shape[0]):
            done, n = 0, ref.shape[1]
            while done < n:
                row, col = divmod(spot, width)
                part = min(n - done, width - col)
                rows_ref[row : row + 1, col : col + part] = ref[i : i + 1, done : done + part]
                done, spot = done + part, spot + part
    out_ref[height - rows :, below] = rows_ref[...].astype(LOW)


def unpack_kernel(shard, skip_rows, lengths, last_ref, skip_ref, rel_ref, *outs):
    group = last_ref.shape[0] // shard
    heads = rel_ref.shape[0] // NB
    width = last_ref.shape[1]
    for g in range(group):
        start = g * shard
        skip_ref[g * skip_rows : (g + 1) * skip_rows] = last_ref[start : start + skip_rows]
        rows = last_ref[start + skip_rows : start + shard].astype(F32)

        def piece(spot, n):
            parts, done = [], 0
            while done < n:
                row, col = divmod(spot + done, width)
                part = min(n - done, width - col)
                parts.append(rows[row : row + 1, col : col + part])
                done += part
            return parts[0] if len(parts) == 1 else jnp.concatenate(parts, axis=1)

        spot = 0
        for n, out in zip(lengths, outs):
            out[:, g * n : (g + 1) * n] = piece(spot, n)
            spot += n
        each = NB // group
        for h in range(heads):
            for j in range(each):
                row = h * NB + g * each + j
                rel_ref[row : row + 1] = piece(spot, KEY)
                spot += KEY


def pack_sums_kernel(shares, *refs):
    rel_ref, out_ref = refs[-2:]
    group = out_ref.shape[0]
    heads, each = rel_ref.shape[0] // NB, NB // group
    for g in range(group):
        spot = 0
        for (i, n), ref in zip(shares, refs):
            out_ref[g : g + 1, spot : spot + n] = ref[i : i + 1, g * n : (g + 1) * n]
            spot += n
        for h in range(heads):
            for j in range(each):
                row = h * NB + g * each + j
                out_ref[g : g + 1, spot : spot + KEY] = rel_ref[row : row + 1]
                spot += KEY


def project_kernel(rows, head_ref, *refs):
    own, other = refs[:rows], refs[rows : 2 * rows]
    gain_ref, bias_ref, qk_ref, v_ref, q_ref, kv_ref, normed_ref = refs[2 * rows :]
    width, kw = q_ref.shape
    for k in range(rows):
        x = ordered(head_ref, own[k][...].astype(F32), other[k][...].astype(F32))
        normed = (normalize(x)[0] * gain_ref[...] + bias_ref[...]).astype(LOW)
        at = slice(k * width, (k + 1) * width)
        normed_ref[at, :] = normed
        kv_ref[at, :kw] = nn(normed, qk_ref[:, kw:]).astype(LOW)
        kv_ref[at, kw:] = nn(normed, v_ref[...]).astype(LOW)
        if k == 0:
            q_ref[...] = (nn(normed, qk_ref[:, :kw]) * (KEY**-0.5)).astype(LOW)


def attend_out_kernel(q_ref, kv_ref, wr_ref, basis_ref, out_w_ref, out_ref, p_ref, part_ref):
    attend_kernel(q_ref, kv_ref, wr_ref, basis_ref, out_ref, p_ref)
    part_ref[...] = nt(out_ref[...], out_w_ref[...]).astype(LOW)


def ff_kernel(
    head_ref, own_ref, other_ref, p_ref, po_ref, gain_ref, bias_ref, b_up_ref, b_down_ref, up_ref, down_ref,
    hidden_ref, normed_ref, act_ref, slope_ref, mine_ref, send_ref, acc,
):
    step = pl.program_id(0)

    @pl.when(step == 0)
    def _():
        x = ordered(head_ref, own_ref[...].astype(F32), other_ref[...].astype(F32))
        hidden = x + (p_ref[...].astype(F32) + po_ref[...].astype(F32))
        hidden_ref[...] = hidden
        normed_ref[...] = (normalize(hidden)[0] * gain_ref[...] + bias_ref[...]).astype(LOW)
        acc[...] = hidden + b_down_ref[...]

    u = nn(normed_ref[...], up_ref[...]) + b_up_ref[...]
    t = jnp.tanh(G0 * (u + G1 * u * u * u))
    act = (0.5 * u * (1.0 + t)).astype(LOW)
    slope = 0.5 * (1.0 + t) + 0.5 * u * (1.0 - t * t) * (G0 * (1.0 + 3.0 * G1 * u * u))
    act_ref[...] = act
    slope_ref[...] = slope.astype(LOW)
    n = acc.shape[1] // 2
    part = nt(act, down_ref[...])
    mine, theirs = my_half(head_ref, part)

    @pl.when(step == 0)
    def _():
        mine_ref[...] = my_half(head_ref, acc[...])[0] + mine
        acc[:, :n] = theirs

    @pl.when(step > 0)
    def _():
        mine_ref[...] += mine
        acc[:, :n] += theirs

    @pl.when(step == pl.num_programs(0) - 1)
    def _():
        send_ref[...] = acc[:, :n].astype(LOW)


def ff_back_kernel(
    head_ref, own_ref, other_ref, slope_ref, up_ref, down_ref, *refs
):
    normed_ref, act_ref = refs[:2]
    grad_ref, pre_ref, part_ref, b_up_ref, b_down_ref = refs[2:7]
    step, acc = pl.program_id(0), refs[-1]

    @pl.when(step == 0)
    def _():
        grad = ordered(head_ref, own_ref[...], other_ref[...])
        grad_ref[...] = grad
        b_down_ref[...] = jnp.sum(grad.astype(F32), axis=0, keepdims=True)
        acc[...] = jnp.zeros_like(acc)

    pre = (slope_ref[...].astype(F32) * nn(grad_ref[...], down_ref[...])).astype(LOW)
    pre_ref[...] = pre
    b_up_ref[...] = jnp.sum(pre.astype(F32), axis=0, keepdims=True)
    acc[...] += nt(pre, up_ref[...])
    refs[7][...] = tn(grad_ref[...], act_ref[...]).astype(LOW)
    refs[8][...] = tn(normed_ref[...], pre).astype(LOW)

    @pl.when(step == pl.num_programs(0) - 1)
    def _():
        part_ref[...] = acc[...].astype(LOW)


def inner_back_kernel(
    fused, head_ref, p_ref, po_ref, hidden_ref, grad_ref, trans_ref, gain_ref, out_w_ref,
    q_ref, kv_ref, wr_ref, basis_ref, probs_ref, *refs
):
    spots_ref, normed_ref, out_ref = refs[:3] if fused else (None, None, None)
    outs = refs[3 * fused :]
    proj_ref, resid_ref, gain_sum_ref, bias_sum_ref, dq_ref, dkv_ref, dwr_ref, far_ref = outs[:8]
    attended = outs[-1]
    grad_normed = p_ref[...].astype(F32) + po_ref[...].astype(F32)
    hat, scale = normalize(hidden_ref[...])
    gain_sum_ref[...] = jnp.sum(grad_normed * hat, axis=0, keepdims=True)
    bias_sum_ref[...] = jnp.sum(grad_normed, axis=0, keepdims=True)
    through = norm_back(grad_normed, hat, scale, gain_ref[...])
    resid_ref[...] = trans_ref[...] + my_half(head_ref, through)[0]
    proj = (grad_ref[...].astype(F32) + through).astype(LOW)
    proj_ref[...] = proj
    attended[...] = nn(proj, out_w_ref[...]).astype(LOW)
    attend_back_kernel(
        q_ref, kv_ref, wr_ref, basis_ref, probs_ref, attended, dq_ref, dkv_ref, dwr_ref
    )
    far_ref[...] = dkv_ref[far_ref.shape[0] :]
    if fused:
        kw = dq_ref.shape[1]
        columns_product(spots_ref, proj_ref, out_ref[...], outs[8], slice(None))
        columns_product(spots_ref, normed_ref, dq_ref[...], outs[9], slice(0, kw))
        columns_product(spots_ref, normed_ref, dkv_ref[...], outs[9], slice(kw, None))


def point_back_kernel(head_ref, grad_ref, point_ref, mine_ref, send_ref, bias_ref):
    grad = grad_ref[...]
    bias_ref[...] = jnp.sum(grad[: grad.shape[0] - 16].astype(F32), axis=0, keepdims=True)
    mine, theirs = my_half(head_ref, nt(grad, point_ref[...]))
    mine_ref[...] = mine
    send_ref[...] = theirs.astype(LOW)


def before(a, edge):
    row = lax.broadcasted_iota(jnp.int32, a.shape, 0)
    return jnp.where(row == 0, edge, pltpu.roll(a, 1, 0))


def behind(a, edge):
    row = lax.broadcasted_iota(jnp.int32, a.shape, 0)
    return jnp.where(row == a.shape[0] - 1, edge, pltpu.roll(a, a.shape[0] - 1, 0))


def section_back_kernel(mine_ref, got_ref, tap0, tap1, tap2, gm_ref, low_ref, coarse_ref, bias_ref):
    n = coarse_ref.shape[0]
    gm = mine_ref[...] + got_ref[...].astype(F32)
    gm_ref[...] = gm[: 2 * n]
    even, odd = gm[:n], gm[n : 2 * n]
    prev, later = gm[2 * n : 2 * n + 1], gm[2 * n + 1 : 2 * n + 2]
    gs_even = tap0[...] * odd + tap1[...] * even + tap2[...] * before(odd, prev)
    gs_odd = tap0[...] * behind(even, later) + tap1[...] * odd + tap2[...] * even
    coarse_ref[...] = gs_even + gs_odd
    gs = jnp.concatenate([gs_even, gs_odd], axis=0).astype(LOW)
    low_ref[...] = gs
    bias_ref[...] = jnp.sum(gs.astype(F32), axis=0, keepdims=True)


def section_kernel(trans_ref, skip_ref, prev_ref, later_ref, gm_ref, tap0, tap1, tap2, mixed_ref, depth_ref):
    n = trans_ref.shape[0]
    coarse = gelu(trans_ref[...])
    s_even, s_odd = coarse + skip_ref[:n], coarse + skip_ref[n:]
    s_before, s_after = before(s_odd, prev_ref[...]), behind(s_even, later_ref[...])
    mixed_ref[:n] = (tap0[...] * s_before + tap1[...] * s_even + tap2[...] * s_odd).astype(LOW)
    mixed_ref[n:] = (tap0[...] * s_even + tap1[...] * s_odd + tap2[...] * s_after).astype(LOW)
    even, odd = gm_ref[:n], gm_ref[n:]
    for k, a, b in ((0, s_before, s_even), (1, s_even, s_odd), (2, s_odd, s_after)):
        depth_ref[k : k + 1] = jnp.sum(even * a + odd * b, axis=0, keepdims=True)


def project_back_kernel(rows, dq_ref, *refs):
    parts, (qk_ref, v_ref, out_ref) = refs[:rows], refs[rows:]
    kw = dq_ref.shape[1]
    dkv = parts[0][...].astype(F32)
    for k in range(1, rows):
        dkv = dkv + parts[k][...].astype(F32)
    dkv = dkv.astype(LOW)
    dqk = jnp.concatenate([dq_ref[...], dkv[:, :kw]], axis=1)
    out_ref[...] = (nt(dqk, qk_ref[...]) + nt(dkv[:, kw:], v_ref[...])).astype(LOW)


def outer_back_kernel(
    head_ref, own_ref, other_ref, p_ref, po_ref, gain_ref, resid_ref, grad_ref, gain_sum_ref, bias_sum_ref
):
    hat, scale = normalize(
        ordered(head_ref, own_ref[...].astype(F32), other_ref[...].astype(F32))
    )
    grad_normed = p_ref[...].astype(F32) + po_ref[...].astype(F32)
    gain_sum_ref[...] = jnp.sum(grad_normed * hat, axis=0, keepdims=True)
    bias_sum_ref[...] = jnp.sum(grad_normed, axis=0, keepdims=True)
    through = norm_back(grad_normed, hat, scale, gain_ref[...])
    grad_ref[...] = resid_ref[...] + my_half(head_ref, through)[0]


def position_windows(z, width, rows):
    seq = width * rows
    block = jnp.bitwise_xor(z, np.array(bit_order(rows), np.int32)) - z
    t = block[:, None] * width + (np.arange(2 * width) - (width - 1))[None, :]
    distance = t.reshape(-1).astype(F32)
    magnitude = jnp.abs(distance)[:, None]
    number = NB // 4
    steps_up = np.arange(number, dtype=np.float32)
    half_life = (3.0 * (seq / 3.0) ** (steps_up / max(number - 1, 1))).astype(np.float32)
    decays = jnp.exp(-0.6931471805599453 * magnitude / half_life)
    central = (2.0 ** (steps_up + 1.0) - 1.0 > magnitude).astype(F32)
    even = jnp.concatenate([decays, central], axis=1)
    return jnp.concatenate([even, jnp.sign(distance)[:, None] * even], axis=1).astype(LOW)


G0, G1 = 0.7978845608028654, 0.044715


def gelu(u):
    return 0.5 * u * (1.0 + jnp.tanh(G0 * (u + G1 * u * u * u)))


def gelu_slope(u):
    t = jnp.tanh(G0 * (u + G1 * u * u * u))
    return 0.5 * (1.0 + t) + 0.5 * u * (1.0 - t * t) * (G0 * (1.0 + 3.0 * G1 * u * u))


def normalize(values):
    centered = values - jnp.mean(values, axis=-1, keepdims=True)
    scale = lax.rsqrt(jnp.mean(centered * centered, axis=-1, keepdims=True) + EPS)
    return centered * scale, scale


def norm_back(grad, hat, scale, gain):
    gg = grad * gain
    return scale * (
        gg
        - jnp.mean(gg, axis=-1, keepdims=True)
        - hat * jnp.mean(gg * hat, axis=-1, keepdims=True)
    )


def pick(head, own, other):
    return jnp.where(head == 0, own, other), jnp.where(head == 0, other, own)


def both_halves(head, own, other):
    return jnp.concatenate(pick(head, own, other), axis=1)


def half(a, head):
    n = a.shape[1] // 2
    return lax.dynamic_slice_in_dim(a, head * n, n, 1)


def one_hot(select, height, width):
    ii = lax.broadcasted_iota(jnp.int32, (height, width), 0)
    jj = lax.broadcasted_iota(jnp.int32, (height, width), 1)
    return select(ii, jj).astype(LOW)


def from_before(row):
    n = lax.axis_size(RW)
    return lax.ppermute(row, RW, [(i, i + 1) for i in range(n - 1)])


def from_behind(row):
    n = lax.axis_size(RW)
    return lax.ppermute(row, RW, [(i + 1, i) for i in range(n - 1)])


def shards(
    inputs,
    skip_input,
    cotangent,
    track_mask,
    norm1_gain,
    norm1_bias,
    query_weight,
    key_weight,
    value_weight,
    rel_weight,
    out_weight,
    norm2_gain,
    norm2_bias,
    up_weight,
    up_bias,
    down_weight,
    down_bias,
    skip_weight,
    skip_bias,
    depth_weight,
    point_weight,
    point_bias,
):
    head = lax.axis_index(HD)
    _, _, z = place()
    rows = lax.axis_size(RW)
    group = lax.axis_size(IT) * rows
    width, chan = inputs.shape[1], inputs.shape[2]
    model = 2 * chan
    heads = rel_weight.shape[0]
    kw = heads * KEY
    shard = norm1_gain.shape[0]
    small = skip_bias.shape[1]
    rel_cols = rel_weight.shape[1]

    skip_rows = skip_weight.shape[0]
    flat = jnp.concatenate(
        [norm1_gain, norm1_bias, norm2_gain, norm2_bias, down_bias, up_bias[0]]
        + [skip_bias[0], depth_weight.reshape(-1), point_bias[0], rel_weight.reshape(-1)]
    ).astype(LOW)
    spare = shard - skip_rows
    singles = [norm1_gain, norm1_bias, norm2_gain, norm2_bias, down_bias, up_bias]
    singles += [skip_bias, depth_weight, point_bias, rel_weight]
    flat = jnp.pad(flat, (0, spare * chan - flat.size)).reshape(spare, chan)
    ff = up_weight.shape[1]
    order = [up_weight, down_weight.T, out_weight.T, point_weight]
    order += [jnp.concatenate([skip_weight.astype(LOW), flat], axis=0)]
    order += [value_weight, query_weight, key_weight]
    if shard % 16 == 0 and skip_rows % 16 == 0 and spare == 16:
        order[4] = skip_weight
        singles = [v.reshape(-1, v.shape[-1]) for v in singles]
        (piece,) = run(
            functools.partial(pack_kernel, len(order)),
            1,
            order + singles,
            [new((shard, sum(w.shape[1] for w in order)), LOW)],
            [pltpu.VMEM((spare, chan), F32)],
        )
    else:
        piece = jnp.concatenate([w.astype(LOW) for w in order], axis=1)
    big = lax.all_gather(piece, (IT, RW), axis=0, tiled=True)
    at = 2 * ff

    def columns(start, count):
        return (big, (model, count), lambda i: (0, start // count))

    w_out, w_value = columns(at, chan), columns(at + 3 * chan, heads * VAL)
    w_qk = columns(at + 3 * chan + heads * VAL, 2 * kw)
    w_point = columns(at + chan, chan)
    steps = 3
    cut = ff // steps
    w_up = (big, (model, cut), lambda i: (0, i))
    w_down = (big, (model, cut), lambda i: (0, steps + i))
    if shard % 16 == 0 and skip_rows % 16 == 0 and spare == 16 and NB % group == 0:
        lengths = [shard] * 6 + [small] * 5
        w_skip, w_rel, *singles = run(
            functools.partial(unpack_kernel, shard, skip_rows, lengths),
            1,
            [columns(at + 2 * chan, chan)],
            [new((group * skip_rows, chan), LOW), new((heads * NB, KEY), F32)]
            + [new((1, group * n), F32) for n in lengths],
        )
        gain_one, bias_one, gain_two, bias_two, b_down, b_up = singles[:6]
        b_skip, tap0, tap1, tap2, b_point = singles[6:]
    else:
        last = big[:, at + 2 * chan : at + 3 * chan].reshape(group, shard, chan)
        w_skip = last[:, :skip_rows].reshape(group * skip_rows, chan)
        tails = last[:, skip_rows:].reshape(group, -1)

        def vector(start, count):
            return wide(tails[:, start : start + count]).reshape(1, -1)

        gain_one, bias_one, gain_two, bias_two, b_down, b_up = (
            vector(i * shard, shard) for i in range(6)
        )
        at = 6 * shard
        b_skip, tap0, tap1, tap2, b_point = (vector(at + i * small, small) for i in range(5))
        at += 5 * small
        w_rel = tails[:, at : at + heads * rel_cols].reshape(group, heads, rel_cols)
        w_rel = w_rel.transpose(1, 0, 2).reshape(heads * NB, KEY)

    at_head = (head.reshape(1).astype(jnp.int32), None, None)
    even = one_hot(lambda i, j: j == 2 * i, width, 2 * width)
    odd = one_hot(lambda i, j: j == 2 * i + 1, width, 2 * width)
    apart = jnp.concatenate([even, odd], axis=0)
    masked = (wide(cotangent[0]) * wide(track_mask)).astype(LOW)
    edges = [from_before(masked[-1:]), from_behind(masked[:1]), jnp.zeros((14, chan), LOW)]
    grad_out = nn(apart, masked).astype(LOW)
    grad_rows = jnp.concatenate([grad_out] + edges, axis=0)
    skip_low = nn(apart, gelu(wide(skip_input[0])).astype(LOW)).astype(LOW)

    own_blocks = [to_bit(inputs[0], k) if k else inputs[0] for k in bit_order(rows)]
    other_blocks = [to_head(b) for b in own_blocks]
    basis = position_windows(z, width, rows)
    queries, kv, normed_all = run(
        functools.partial(project_kernel, rows),
        1,
        [at_head] + own_blocks + other_blocks + [gain_one, bias_one, w_qk, w_value],
        [new((width, kw), LOW), new((rows * width, kw + heads * VAL), LOW)]
        + [new((rows * width, model), LOW)],
        after=[skip_low, grad_rows, basis],
    )
    attended, probs, partial_attn = run(
        attend_out_kernel,
        1,
        [queries, kv, w_rel, basis, w_out],
        [new((width, heads * VAL), LOW), new((heads, width, rows * width), LOW)]
        + [new((width, model), LOW)],
    )
    skip_term = nn(skip_low, w_skip) + b_skip
    gm_mine, gm_send, grad_point_bias = run(
        point_back_kernel,
        1,
        [at_head, grad_rows, w_point],
        [new((2 * width + 16, chan), F32), new((2 * width + 16, chan), LOW), new((1, chan), F32)],
        after=[partial_attn],
    )
    grad_mixed, grad_skip_low, grad_coarse, grad_skip_bias = run(
        section_back_kernel,
        1,
        [gm_mine, to_head(gm_send), tap0, tap1, tap2],
        [new((2 * width, chan), F32), new((2 * width, chan), LOW)]
        + [new((width, chan), F32), new((1, chan), F32)],
    )

    by_cut = (width, cut), lambda i: (0, i)
    hidden, normed_two, activated, slope, trans, send = run(
        ff_kernel,
        steps,
        [at_head, own_blocks[0], other_blocks[0], partial_attn, to_head(partial_attn)]
        + [gain_two, bias_two, (b_up, (1, cut), lambda i: (0, i)), b_down, w_up, w_down],
        [new((width, model), F32), new((width, model), LOW), (new((width, ff), LOW), *by_cut)]
        + [(new((width, ff), LOW), *by_cut), new((width, chan), F32), new((width, chan), LOW)],
        [pltpu.VMEM((width, model), F32)],
        after=[skip_term],
    )
    trans = trans + wide(to_head(send))

    for_skip = Scatter([(skip_low, grad_skip_low)])

    s_first = gelu(trans[:1]) + skip_term[:1]
    s_last = gelu(trans[-1:]) + skip_term[-1:]
    prev, later = wide(from_before(low(s_last))), wide(from_behind(low(s_first)))

    grad_trans = gelu_slope(trans) * grad_coarse
    grad_own = low(grad_trans)
    owned = model // lax.axis_size(IT)
    fused = fits(owned)
    core_rows = model // 2
    spots = jnp.stack(spots_of(1 - place()[1], owned)).astype(jnp.int32), None, None
    extra = new((model, ff), LOW), (model, cut), lambda i: (0, i)
    grad_ff_low, grad_pre_low, partial_two, grad_up_bias, grad_down_bias, *theirs = run(
        ff_back_kernel,
        steps,
        [at_head, grad_own, to_head(grad_own), (slope, *by_cut), w_up, w_down]
        + [normed_two, (activated, *by_cut)],
        [new((width, model), LOW), (new((width, ff), LOW), *by_cut), new((width, model), LOW)]
        + [(new((1, ff), F32), (1, cut), lambda i: (0, i)), new((1, model), F32)]
        + [extra, extra],
        [pltpu.VMEM((width, model), F32)],
        after=[prev, later],
    )
    for_down, for_up = (
        RowSum(lax.psum_scatter(t, IT, scatter_dimension=0, tiled=True)) for t in theirs
    )
    mixed, grad_depth = run(
        section_kernel,
        1,
        [trans, skip_term, prev, later, grad_mixed, tap0, tap1, tap2],
        [new((2 * width, chan), LOW), new((3, chan), F32)],
    )
    grad_proj_low, resid, grad_gain_two, grad_bias_two, dq, dkv, grad_rel, far, *theirs = run(
        functools.partial(inner_back_kernel, fused),
        1,
        [at_head, partial_two, to_head(partial_two), hidden, grad_ff_low, grad_trans, gain_two]
        + [w_out, queries, kv, w_rel, basis, probs]
        + [spots, normed_all, attended][: 3 * fused],
        [new((width, model), LOW), new((width, chan), F32)]
        + [new((1, model), F32), new((1, model), F32)]
        + [new(queries.shape, LOW), new(kv.shape, LOW), new(w_rel.shape, F32)]
        + [new((kv.shape[0] // 2, kv.shape[1]), LOW)]
        + [new((core_rows, heads * VAL), LOW), new((core_rows, kw + kv.shape[1]), LOW)][: 2 * fused],
        [pltpu.VMEM((width, heads * VAL), LOW)],
        after=for_skip.send + [mixed],
    )
    dkv_parts, rest, bit, arrived = [dkv[:width]], dkv, 1, []
    summed = []
    while bit < rows:
        n = rest.shape[0] // 2
        got = to_bit(far if bit == 1 else rest[n:], bit)
        dkv_parts.append(got[:width])
        arrived.append(got)
        if n > width:
            rest = low(wide(rest[:n]) + wide(got))
            dkv_parts = [rest[:width]]
            summed.append(rest)
        bit *= 2
    skip_across = [for_skip.across(0)]
    mixed_other = to_head(mixed)
    skip_across = [for_skip.across(0)]
    for_skip.take(skip_across)
    for_attn = Scatter(
        [(grad_proj_low, attended), (normed_all, dq), (normed_all, dkv)],
        theirs or None,
        [],
        skip_across[0],
        [[0, 1, 2]],
    )
    mixed_full = both_halves(head, mixed, mixed_other)
    for_point = Scatter([(mixed_full, grad_out)], None, [], for_attn.send)
    for_down.step(for_point.theirs)
    attn_across = [for_attn.across(0)]
    for_attn.take(attn_across)
    point_across = for_point.across(0)
    for_point.take([point_across])
    (partial_one,) = run(
        functools.partial(project_back_kernel, len(dkv_parts)),
        1,
        [dq] + dkv_parts + [w_qk, w_value],
        [new((width, model), LOW)],
        after=for_point.send + [for_down.sent],
    )
    for_down.step([partial_one])
    for_up.step([for_down.sent])
    for_attn.step([for_up.sent])
    for_skip.step([for_attn.sent])
    input_grad, grad_gain_one, grad_bias_one = run(
        outer_back_kernel,
        1,
        [at_head, own_blocks[0], other_blocks[0], partial_one, to_head(partial_one)]
        + [gain_one, resid],
        [new((width, chan), F32), new((1, model), F32), new((1, model), F32)],
        after=[for_skip.sent] + point_across + for_up.got + for_down.got,
    )
    input_grad = input_grad[None]
    for_attn.step([grad_gain_one])
    for_up.step([for_attn.sent] + for_skip.got)
    for_point.step([for_up.sent])
    for_skip.step([for_point.sent])
    early = [for_point.sent]
    for_point.step([for_skip.sent] + for_attn.got + for_up.got)
    last = [for_point.sent]
    (grad_down,), (grad_up,) = for_down.finish(early), for_up.finish(early)
    (grad_skip,), (grad_point,) = for_skip.finish(last), for_point.finish(last)
    grad_out_w, *grad_qkv = for_attn.finish(early, [heads * VAL, kw, kw, heads * VAL])
    result = (nn(mixed_full, w_point[0][:, 2 * ff + chan : 2 * ff + 2 * chan]) + b_point).astype(LOW)
    block_output = tn(apart, result).astype(LOW)[None]
    parts = [grad_gain_one, grad_bias_one, grad_gain_two, grad_bias_two, grad_down_bias]
    parts += [grad_up_bias, grad_skip_bias] + [grad_depth] * 3 + [grad_point_bias]
    which = [0] * 7 + [0, 1, 2] + [0]
    if NB % group == 0:
        shares = [(i, p.shape[-1] // group) for i, p in zip(which, parts)]
        total = sum(n for _, n in shares) + heads * rel_cols
        (parts,) = run(
            functools.partial(pack_sums_kernel, shares),
            1,
            [p.reshape(-1, p.shape[-1]) for p in parts] + [grad_rel],
            [new((group, total), F32)],
        )
    else:
        parts = [p.reshape(-1, p.shape[-1])[i] for i, p in zip(which, parts)]
        rel_parts = grad_rel.reshape(heads, group, rel_cols).transpose(1, 0, 2)
        parts = [p.reshape(group, -1) for p in parts + [rel_parts]]
        parts = jnp.concatenate(parts, axis=1)
    sums = scatter_small(parts, last)

    def own(start, count):
        return sums[0, start : start + count]

    at = 6 * shard
    return (
        block_output,
        input_grad,
        own(0, shard),
        own(shard, shard),
        *grad_qkv,
        own(at + 5 * small, heads * rel_cols).reshape(heads, rel_cols),
        grad_out_w.T,
        own(2 * shard, shard),
        own(3 * shard, shard),
        grad_up,
        own(5 * shard, shard)[None],
        grad_down.T,
        own(4 * shard, shard),
        grad_skip,
        own(at, small)[None],
        own(at + small, 3 * small).reshape(3, 1, small),
        grad_point,
        own(at + 4 * small, small)[None],
    )


def solution(mesh):
    gr = (IT, RW)
    vec, cols, rws = P(gr), P(gr, HD), P(HD, gr)
    act = P(IT, RW, HD)
    taps = P(None, HD, gr)
    weights = (vec, vec, cols, cols, cols, rws, rws, vec, vec, cols, rws, rws, vec, cols, rws)
    weights += (taps, cols, rws)
    return jax.shard_map(
        shards,
        mesh=mesh,
        in_specs=(act, P(IT, RW, None), act, P(IT, HD)) + weights,
        out_specs=(act, act) + weights,
        check_vma=False,
    )
```

```python
import functools

import jax
import jax.numpy as jnp
import numpy as np
from jax import lax
from jax.experimental import pallas as pl
from jax.experimental.pallas import tpu as pltpu
from jax.sharding import PartitionSpec as P

KEY = 64
VAL = 192
NB = 32
EPS = 1e-05
IT, HD, RW = "items", "heads", "rows"
LOW = jnp.bfloat16
F32 = jnp.float32
VMEM = pltpu.CompilerParams(vmem_limit_bytes=56 * 2**20)
SHORT = pl.CostEstimate(flops=1, bytes_accessed=1, transcendentals=0)


def nn(a, b):
    return lax.dot_general(a, b, (((1,), (0,)), ((), ())), preferred_element_type=F32)


def nt(a, b):
    return lax.dot_general(a, b, (((1,), (1,)), ((), ())), preferred_element_type=F32)


def tn(a, b):
    return lax.dot_general(a, b, (((0,), (0,)), ((), ())), preferred_element_type=F32)


def wide(a):
    return a.astype(F32)


def low(a):
    return lax.reduce_precision(a, 8, 7).astype(LOW)


def bit_order(n):
    out, bit = [0], n // 2
    while bit:
        out += [i + bit for i in out]
        bit //= 2
    return out


def to_core(a):
    n = lax.axis_size(IT)
    return lax.ppermute(a, IT, [(i, i ^ 1) for i in range(n)])


def to_pair(a, k):
    n = lax.axis_size(IT)
    return lax.ppermute(a, IT, [(i, (i + 2 * k) % n) for i in range(n)])


def to_head(a):
    return lax.ppermute(a, HD, [(0, 1), (1, 0)])


def place():
    item = lax.axis_index(IT)
    return item // 2, item % 2, lax.axis_index(RW)


def to_bit(a, bit):
    n = lax.axis_size(RW)
    return lax.ppermute(a, RW, [(i, i ^ bit) for i in range(n)])


def halve(keep, got, pick_bit, pieces, after=()):
    w, n = keep.shape[0] // pieces, keep.shape[1]
    shape = (pieces // 2, 2, w, n)
    if w % 16:
        total = wide(keep)
        if got:
            total = total + wide(jnp.concatenate(got, axis=1))
        total = total.reshape(shape)
        mine = lax.dynamic_index_in_dim(total, pick_bit, 1, keepdims=False)
        send = lax.dynamic_index_in_dim(total, 1 - pick_bit, 1, keepdims=False)
        return mine.reshape(-1, n), low(send).reshape(-1, n)
    widths = [g.shape[1] for g in got]

    def body(bit_ref, keep_ref, *refs):
        got_refs, (mine_ref, send_ref) = refs[:-2], refs[-2:]

        def write(bit):
            if not got:
                mine_ref[0] = keep_ref[0, bit].astype(F32)
                send_ref[0] = keep_ref[0, 1 - bit].astype(LOW)
            at = 0
            for ref, count in zip(got_refs, widths):
                there = slice(at, at + count)
                at += count
                mine_ref[0, :, there] = keep_ref[0, bit, :, there] + ref[0, bit].astype(F32)
                total = keep_ref[0, 1 - bit, :, there] + ref[0, 1 - bit].astype(F32)
                send_ref[0, :, there] = total.astype(LOW)

        for bit in range(2):
            pl.when(bit_ref[0] == bit)(functools.partial(write, bit))

    def block(count):
        return (1, 2, w, count), lambda i: (i, 0, 0, 0)

    out = (1, w, n), lambda i: (i, 0, 0)
    half_shape = (pieces // 2, w, n)
    mine, send = run(
        body,
        pieces // 2,
        [(pick_bit.reshape(1), None, None), (keep.reshape(shape), *block(n))]
        + [(g.reshape(pieces // 2, 2, w, count), *block(count)) for g, count in zip(got, widths)],
        [(new(half_shape, F32), *out), (new(half_shape, LOW), *out)],
        after=after,
    )
    return mine.reshape(-1, n), send.reshape(-1, n)


def find(bounds, start, end):
    at = next(i for i, (a, b) in enumerate(bounds) if a <= start and end <= b)
    return at, slice(start - bounds[at][0], end - bounds[at][0])


def bounds_of(arrays):
    ends = [int(e) for e in np.cumsum([0] + [a.shape[1] for a in arrays])]
    return list(zip(ends, ends[1:]))


def spots_of(side, w):
    pairs = lax.axis_size(IT) // 2
    x, _, _ = place()
    return [(((x + k) % pairs) * 2 + side) for k in range(pairs)]


def fits(w):
    rows = lax.axis_size(RW)
    return lax.axis_size(IT) == 4 and w % 128 == 0 and (w // rows) % 16 == 0


def columns_product(spots_ref, left_ref, right, out_ref, there):
    count = spots_ref.shape[0]
    w = out_ref.shape[0] // count
    for k in range(count):
        start = pl.multiple_of(spots_ref[k] * w, 128)
        left = left_ref[pl.ds(0, right.shape[0]), pl.ds(start, w)]
        out_ref[k * w : (k + 1) * w, there] = tn(left, right).astype(LOW)


def add_last(keep, got, after, widths):
    ends = [int(e) for e in np.cumsum([0] + widths)]
    cuts = [slice(i, j) for i, j in zip(ends, ends[1:])]
    if keep.shape[0] % 16:
        return [(keep + wide(got))[:, cut] for cut in cuts]

    def body(keep_ref, got_ref, *outs):
        for cut, out_ref in zip(cuts, outs):
            out_ref[...] = keep_ref[:, cut] + got_ref[:, cut].astype(F32)

    outs = [new((keep.shape[0], n), F32) for n in widths]
    return list(run(body, 1, [keep, got], outs, after=after))


def side_product(pairs_of, side, got=None, after=(), groups=None, others=False):
    pairs = lax.axis_size(IT) // 2
    w = pairs_of[0][0].shape[1] // (2 * pairs)
    spots = spots_of(side, w)
    cols = [right.shape[1] for _, right in pairs_of]
    ends = [int(e) for e in np.cumsum([0] + cols)]
    groups = groups or [[k] for k in range(len(cols))]
    bounds = [(ends[g[0]], ends[g[-1] + 1]) for g in groups]
    if w % 128:
        out = []
        for left, right in pairs_of:
            part = [lax.dynamic_slice_in_dim(left, spot * w, w, 1) for spot in spots]
            out.append(tn(jnp.concatenate(part, axis=1)[: right.shape[0]], right))
        out = jnp.concatenate(out, axis=1)
        if got is None:
            return low(out)
        out = out + wide(jnp.concatenate(got, axis=1))
        return out[:w], [low(out[w:, i:j]) for i, j in bounds]
    n, count, m = sum(cols), len(pairs_of), len(after)
    first = int(others)
    got = got or []
    got_bounds = bounds_of(got)

    def body(spot_ref, *refs):
        lefts, rights = refs[:count], refs[count : 2 * count]
        gots = refs[2 * count : 2 * count + len(got)]
        outs = refs[2 * count + len(got) + m :]
        if others:
            outs = (None,) + tuple(outs)
        step = pl.program_id(0)
        for k in range(count):
            there = slice(ends[k], ends[k + 1])
            to = next(i for i, g in enumerate(groups) if k in g)
            inside = slice(ends[k] - bounds[to][0], ends[k + 1] - bounds[to][0])
            part = tn(lefts[k][...], rights[k][...])
            if not got:
                outs[0][:, there] = part.astype(LOW)
                continue
            which, where = find(got_bounds, ends[k], ends[k + 1])
            part = part + gots[which][:, where].astype(F32)

            if others:
                outs[1 + to][:, inside] = part.astype(LOW)
                continue

            @pl.when(step == 0)
            def _(part=part, there=there):
                outs[0][:, there] = part

            @pl.when(step > 0)
            def _(part=part, to=to, inside=inside):
                outs[1 + to][:, inside] = part.astype(LOW)

    specs = [
        pl.BlockSpec((right.shape[0], w), lambda i, spot: (0, spot[i])) for left, right in pairs_of
    ] + [pl.BlockSpec(right.shape, lambda i, spot: (0, 0)) for _, right in pairs_of]
    operands = [left for left, _ in pairs_of] + [right for _, right in pairs_of]
    specs += [pl.BlockSpec((w, g.shape[1]), lambda i, spot: (i + first, 0)) for g in got]
    operands += got
    if not got:
        out_specs = [pl.BlockSpec((w, n), lambda i, spot: (i, 0))]
        out_shape = [new((pairs * w, n), LOW)]
    else:
        out_specs, out_shape = [pl.BlockSpec((w, n), lambda i, spot: (0, 0))], [new((w, n), F32)]
        for c in [j - i for i, j in bounds]:
            out_specs.append(
                pl.BlockSpec((w, c), lambda i, spot: (jnp.maximum(i - 1 + first, 0), 0))
            )
            out_shape.append(new(((pairs - 1) * w, c), LOW))
        out_specs, out_shape = out_specs[first:], out_shape[first:]
    out = pl.pallas_call(
        body,
        grid_spec=pltpu.PrefetchScalarGridSpec(
            num_scalar_prefetch=1,
            grid=(pairs - first,),
            in_specs=specs + [pl.BlockSpec(memory_space=pl.ANY)] * m,
            out_specs=out_specs,
        ),
        out_shape=out_shape,
        compiler_params=VMEM,
        cost_estimate=SHORT,
    )(jnp.stack(spots[first:]).astype(jnp.int32), *operands, *after)
    if others:
        return list(out)
    return (out[0], list(out[1:])) if got else out[0]


def product_halve(pairs_of, spot, core, terms, pick_bit, pieces, after=()):
    w = pairs_of[0][0].shape[1] // (2 * (lax.axis_size(IT) // 2))
    cols = [right.shape[1] for _, right in pairs_of]
    ends = [int(e) for e in np.cumsum([0] + cols)]
    n, count, m = ends[-1], len(pairs_of), len(after)
    widths = [g.shape[1] for g in terms]
    piece = w // pieces
    core_bounds = bounds_of(core)

    def body(at_ref, *refs):
        lefts, rights = refs[:count], refs[count : 2 * count]
        at = 2 * count + len(core)
        core_refs, term_refs = refs[2 * count : at], refs[at : at + len(terms)]
        mine_ref, send_ref, total = refs[at + len(terms) + m :]
        for k in range(count):
            there = slice(ends[k], ends[k + 1])
            which, where = find(core_bounds, ends[k], ends[k + 1])
            part = core_refs[which][:, where].astype(F32)
            total[:, there] = tn(lefts[k][...], rights[k][...]) + part
        at = 0
        for ref, wide_n in zip(term_refs, widths):
            there = slice(at, at + wide_n)
            at += wide_n
            total[:, there] += ref[...].astype(F32)
        for i in range(pieces // 2):
            out = slice(i * piece, (i + 1) * piece)
            for bit in range(2):

                @pl.when(at_ref[1] == bit)
                def _(i=i, bit=bit, out=out):
                    mine = (2 * i + bit) * piece
                    send = (2 * i + 1 - bit) * piece
                    mine_ref[out] = total[mine : mine + piece]
                    send_ref[out] = total[send : send + piece].astype(LOW)

    in_specs = [
        pl.BlockSpec((right.shape[0], w), lambda i, at: (0, at[0])) for _, right in pairs_of
    ] + [pl.BlockSpec(right.shape, lambda i, at: (0, 0)) for _, right in pairs_of]
    in_specs += [pl.BlockSpec((w, g.shape[1]), lambda i, at: (0, 0)) for g in core]
    in_specs += [pl.BlockSpec(t.shape, lambda i, at: (0, 0)) for t in terms]
    out_spec = pl.BlockSpec((w // 2, n), lambda i, at: (0, 0))
    return pl.pallas_call(
        body,
        grid_spec=pltpu.PrefetchScalarGridSpec(
            num_scalar_prefetch=1,
            grid=(1,),
            in_specs=in_specs + [pl.BlockSpec(memory_space=pl.ANY)] * m,
            out_specs=[out_spec, out_spec],
            scratch_shapes=[pltpu.VMEM((w, n), F32)],
        ),
        out_shape=[new((w // 2, n), F32), new((w // 2, n), LOW)],
        compiler_params=VMEM,
        cost_estimate=SHORT,
    )(
        jnp.stack([spot, pick_bit]).astype(jnp.int32),
        *[left for left, _ in pairs_of],
        *[right for _, right in pairs_of],
        *core,
        *terms,
        *after,
    )


class Scatter:
    def __init__(self, pairs_of, theirs=None, after=(), after_more=(), groups=None):
        pairs = lax.axis_size(IT) // 2
        self.x, self.c, self.z = place()
        self.pairs_of, self.groups = pairs_of, groups
        self.plain = not fits(pairs_of[0][0].shape[1] // (2 * pairs))
        if theirs is None:
            theirs = [side_product(pairs_of, 1 - self.c, None, after)]
        self.theirs = theirs
        self.core = [to_core(t) for t in theirs]
        if self.plain:
            self.keep, self.send = side_product(pairs_of, self.c, self.core, after_more, groups)
        else:
            self.send = side_product(
                pairs_of, self.c, self.core, after_more, groups, others=True
            )
        self.bit = 1

    def across(self, i):
        pairs = lax.axis_size(IT) // 2
        w = self.send[i].shape[0] // (pairs - 1)
        return [to_pair(self.send[i][(k - 1) * w : k * w], k) for k in range(1, pairs)]

    def take(self, got):
        if self.plain:
            for terms in zip(*[g[:-1] for g in got]):
                self.keep = self.keep + wide(jnp.concatenate(terms, axis=1))
        self.got = [g[-1] for g in got]

    def step(self, after=()):
        pieces = lax.axis_size(RW) // self.bit
        pick_bit = (self.z // self.bit) % 2
        if self.bit == 1 and not self.plain:
            self.keep, self.sent = product_halve(
                self.pairs_of, self.x * 2 + self.c, self.core, self.got, pick_bit, pieces, after
            )
        else:
            self.keep, self.sent = halve(self.keep, self.got, pick_bit, pieces, after)
        self.got = [to_bit(self.sent, self.bit)]
        self.bit *= 2
        return self.got

    def finish(self, after=(), widths=None):
        while self.bit < lax.axis_size(RW):
            self.step(after)
        return add_last(self.keep, self.got[0], after, widths or [self.keep.shape[1]])


class RowSum:
    def __init__(self, keep):
        self.keep, self.got, self.bit = keep, [], 1
        self.z = lax.axis_index(RW)

    def step(self, after=()):
        pieces = lax.axis_size(RW) // self.bit
        pick_bit = (self.z // self.bit) % 2
        self.keep, self.sent = halve(self.keep, self.got, pick_bit, pieces, after)
        self.got = [to_bit(self.sent, self.bit)]
        self.bit *= 2
        return self.got

    def finish(self, after=(), widths=None):
        while self.bit < lax.axis_size(RW):
            self.step(after)
        return add_last(self.keep, self.got[0], after, widths or [self.keep.shape[1]])


def scatter_small(parts, after):
    pairs, rows = lax.axis_size(IT) // 2, lax.axis_size(RW)
    x, c, z = place()
    n = parts.shape[1]
    cube = parts.reshape(pairs, 2, rows, n)
    cube = lax.dynamic_index_in_dim(cube, c, 1, keepdims=False) + to_core(
        lax.dynamic_index_in_dim(cube, 1 - c, 1, keepdims=False)
    )
    plane = lax.dynamic_index_in_dim(cube, x, 0, keepdims=False)
    for k in range(1, pairs):
        plane = plane + to_pair(
            lax.dynamic_index_in_dim(cube, (x + k) % pairs, 0, keepdims=False), k
        )
    terms = [lax.dynamic_index_in_dim(plane, z, 0, keepdims=True)]
    for k in range(1, rows):
        spot = jnp.bitwise_xor(z, k)
        terms.append(to_bit(lax.dynamic_index_in_dim(plane, spot, 0, keepdims=True), k))

    def body(*refs):
        refs[-1][...] = sum(ref[...] for ref in refs[1:-1]) + refs[0][...]

    return run(body, 1, terms, [new(terms[0].shape, F32)], after=after)[0]


def attend_kernel(q_ref, kv_ref, wr_ref, basis_ref, out_ref, p_ref):
    rows, seq, heads = q_ref.shape[0], kv_ref.shape[0], p_ref.shape[0]
    width = heads * KEY
    basis = basis_ref[...]
    outs = []
    for h in range(heads):
        qh = q_ref[:, h * KEY : (h + 1) * KEY]
        kh = kv_ref[:, h * KEY : (h + 1) * KEY]
        vh = kv_ref[:, width + h * VAL : width + (h + 1) * VAL]
        features = nt(qh, wr_ref[h * NB : (h + 1) * NB, :].astype(LOW)).astype(LOW)
        table = nt(features, basis)
        rel = [
            pltpu.roll(
                table[:, k * 2 * rows : (k + 1) * 2 * rows], rows + 1, 1, stride=1, stride_axis=0
            )[:, :rows]
            for k in range(seq // rows)
        ]
        logits = nt(qh, kh) + jnp.concatenate(rel, axis=1)
        e = jnp.exp(logits - jnp.max(logits, axis=1, keepdims=True))
        p = (e * (1.0 / jnp.sum(e, axis=1, keepdims=True))).astype(LOW)
        p_ref[h] = p
        outs.append(nn(p, vh))
    out_ref[...] = jnp.concatenate(outs, axis=1).astype(LOW)


def attend_back_kernel(q_ref, kv_ref, wr_ref, basis_ref, p_ref, g_ref, dq_ref, dkv_ref, dwr_ref):
    rows, seq, heads = q_ref.shape[0], kv_ref.shape[0], p_ref.shape[0]
    width = heads * KEY
    basis = basis_ref[...]
    ii = lax.broadcasted_iota(jnp.int32, (rows, rows), 0)
    jj = lax.broadcasted_iota(jnp.int32, (rows, rows), 1)
    flip = (ii + jj == rows - 1).astype(F32).astype(LOW)
    dqs, dks, dvs = [], [], []
    for h in range(heads):
        qh = q_ref[:, h * KEY : (h + 1) * KEY]
        kh = kv_ref[:, h * KEY : (h + 1) * KEY]
        vh = kv_ref[:, width + h * VAL : width + (h + 1) * VAL]
        gh = g_ref[:, h * VAL : (h + 1) * VAL]
        wr = wr_ref[h * NB : (h + 1) * NB, :].astype(LOW)
        p = p_ref[h]
        probs = p.astype(F32)
        dp = nt(gh, vh)
        inner = jnp.sum(probs * dp, axis=1, keepdims=True)
        ds = (probs * (dp - inner)).astype(LOW)
        dvs.append(tn(p, gh))
        dks.append(tn(ds, qh))
        rev = nn(flip, ds)
        zeros = jnp.zeros((rows, rows), F32)
        tabs = [
            pltpu.roll(
                jnp.concatenate([rev[:, k * rows : (k + 1) * rows], zeros], axis=1),
                0,
                1,
                stride=1,
                stride_axis=0,
            ).astype(LOW)
            for k in range(seq // rows)
        ]
        features = nn(jnp.concatenate(tabs, axis=1), basis).astype(LOW)
        features = nn(flip, features).astype(LOW)
        dqs.append(nn(ds, kh) + nn(features, wr))
        dwr_ref[h * NB : (h + 1) * NB, :] = tn(features, qh)
    dq = jnp.concatenate(dqs, axis=1).astype(LOW).astype(F32) * (KEY**-0.5)
    dq_ref[...] = dq.astype(LOW)
    dkv_ref[...] = jnp.concatenate(dks + dvs, axis=1).astype(LOW)


def run(body, grid, ins, outs, scratch=(), after=()):
    n, m = len(ins), len(after)

    def kernel(*refs):
        body(*refs[:n], *refs[n + m :])

    def spec(shape, index):
        if index is None:
            return pl.BlockSpec(memory_space=pltpu.SMEM)
        return pl.BlockSpec(shape, index)

    def whole(a):
        return (a, a.shape, lambda i: (0,) * a.ndim)

    full = [entry if isinstance(entry, tuple) else whole(entry) for entry in ins]
    out_full = [entry if isinstance(entry, tuple) else whole(entry) for entry in outs]
    return pl.pallas_call(
        kernel,
        grid=(grid,),
        in_specs=[spec(shape, index) for _, shape, index in full]
        + [pl.BlockSpec(memory_space=pl.ANY)] * m,
        out_specs=tuple(spec(shape, index) for _, shape, index in out_full),
        out_shape=tuple(a for a, _, _ in out_full),
        scratch_shapes=scratch,
        compiler_params=VMEM,
        cost_estimate=SHORT,
    )(*[a for a, _, _ in full], *after)


def new(shape, dtype):
    return jax.ShapeDtypeStruct(shape, dtype)


def ordered(head_ref, own, other):
    first = head_ref[0] == 0
    return jnp.concatenate([jnp.where(first, own, other), jnp.where(first, other, own)], axis=1)


def my_half(head_ref, a):
    n = a.shape[1] // 2
    first = head_ref[0] == 0
    return jnp.where(first, a[:, :n], a[:, n:]), jnp.where(first, a[:, n:], a[:, :n])


def pack_kernel(count, *refs):
    out_ref, rows_ref = refs[-2:]
    rows, height = rows_ref.shape[0], out_ref.shape[0]
    at = 0
    for ref in refs[:count]:
        there = slice(at, at + ref.shape[1])
        at += ref.shape[1]
        out_ref[: ref.shape[0], there] = ref[...].astype(LOW)
        if ref.shape[0] < height:
            below = there
    rows_ref[...] = jnp.zeros_like(rows_ref)
    spot, width = 0, rows_ref.shape[1]
    for ref in refs[count:-2]:
        for i in range(ref.shape[0]):
            done, n = 0, ref.shape[1]
            while done < n:
                row, col = divmod(spot, width)
                part = min(n - done, width - col)
                rows_ref[row : row + 1, col : col + part] = ref[i : i + 1, done : done + part]
                done, spot = done + part, spot + part
    out_ref[height - rows :, below] = rows_ref[...].astype(LOW)


def unpack_kernel(shard, skip_rows, lengths, last_ref, skip_ref, rel_ref, *outs):
    group = last_ref.shape[0] // shard
    heads = rel_ref.shape[0] // NB
    width = last_ref.shape[1]
    for g in range(group):
        start = g * shard
        skip_ref[g * skip_rows : (g + 1) * skip_rows] = last_ref[start : start + skip_rows]
        rows = last_ref[start + skip_rows : start + shard].astype(F32)

        def piece(spot, n):
            parts, done = [], 0
            while done < n:
                row, col = divmod(spot + done, width)
                part = min(n - done, width - col)
                parts.append(rows[row : row + 1, col : col + part])
                done += part
            return parts[0] if len(parts) == 1 else jnp.concatenate(parts, axis=1)

        spot = 0
        for n, out in zip(lengths, outs):
            out[:, g * n : (g + 1) * n] = piece(spot, n)
            spot += n
        each = NB // group
        for h in range(heads):
            for j in range(each):
                row = h * NB + g * each + j
                rel_ref[row : row + 1] = piece(spot, KEY)
                spot += KEY


def pack_sums_kernel(shares, *refs):
    rel_ref, out_ref = refs[-2:]
    group = out_ref.shape[0]
    heads, each = rel_ref.shape[0] // NB, NB // group
    for g in range(group):
        spot = 0
        for (i, n), ref in zip(shares, refs):
            out_ref[g : g + 1, spot : spot + n] = ref[i : i + 1, g * n : (g + 1) * n]
            spot += n
        for h in range(heads):
            for j in range(each):
                row = h * NB + g * each + j
                out_ref[g : g + 1, spot : spot + KEY] = rel_ref[row : row + 1]
                spot += KEY


def project_kernel(rows, head_ref, *refs):
    own, other = refs[:rows], refs[rows : 2 * rows]
    gain_ref, bias_ref, qk_ref, v_ref, q_ref, kv_ref, normed_ref = refs[2 * rows :]
    width, kw = q_ref.shape
    for k in range(rows):
        x = ordered(head_ref, own[k][...].astype(F32), other[k][...].astype(F32))
        normed = (normalize(x)[0] * gain_ref[...] + bias_ref[...]).astype(LOW)
        at = slice(k * width, (k + 1) * width)
        normed_ref[at, :] = normed
        kv_ref[at, :kw] = nn(normed, qk_ref[:, kw:]).astype(LOW)
        kv_ref[at, kw:] = nn(normed, v_ref[...]).astype(LOW)
        if k == 0:
            q_ref[...] = (nn(normed, qk_ref[:, :kw]) * (KEY**-0.5)).astype(LOW)


def attend_out_kernel(q_ref, kv_ref, wr_ref, basis_ref, out_w_ref, out_ref, p_ref, part_ref):
    attend_kernel(q_ref, kv_ref, wr_ref, basis_ref, out_ref, p_ref)
    part_ref[...] = nt(out_ref[...], out_w_ref[...]).astype(LOW)


def ff_kernel(
    head_ref, own_ref, other_ref, p_ref, po_ref, gain_ref, bias_ref, b_up_ref, b_down_ref, up_ref, down_ref,
    hidden_ref, normed_ref, act_ref, slope_ref, mine_ref, send_ref, acc,
):
    step = pl.program_id(0)

    @pl.when(step == 0)
    def _():
        x = ordered(head_ref, own_ref[...].astype(F32), other_ref[...].astype(F32))
        hidden = x + (p_ref[...].astype(F32) + po_ref[...].astype(F32))
        hidden_ref[...] = hidden
        normed_ref[...] = (normalize(hidden)[0] * gain_ref[...] + bias_ref[...]).astype(LOW)
        acc[...] = hidden + b_down_ref[...]

    u = nn(normed_ref[...], up_ref[...]) + b_up_ref[...]
    t = jnp.tanh(G0 * (u + G1 * u * u * u))
    act = (0.5 * u * (1.0 + t)).astype(LOW)
    slope = 0.5 * (1.0 + t) + 0.5 * u * (1.0 - t * t) * (G0 * (1.0 + 3.0 * G1 * u * u))
    act_ref[...] = act
    slope_ref[...] = slope.astype(LOW)
    n = acc.shape[1] // 2
    part = nt(act, down_ref[...])
    mine, theirs = my_half(head_ref, part)

    @pl.when(step == 0)
    def _():
        mine_ref[...] = my_half(head_ref, acc[...])[0] + mine
        acc[:, :n] = theirs

    @pl.when(step > 0)
    def _():
        mine_ref[...] += mine
        acc[:, :n] += theirs

    @pl.when(step == pl.num_programs(0) - 1)
    def _():
        send_ref[...] = acc[:, :n].astype(LOW)


def ff_back_kernel(
    head_ref, own_ref, other_ref, slope_ref, up_ref, down_ref, *refs
):
    normed_ref, act_ref = refs[:2]
    grad_ref, pre_ref, part_ref, b_up_ref, b_down_ref = refs[2:7]
    step, acc = pl.program_id(0), refs[-1]

    @pl.when(step == 0)
    def _():
        grad = ordered(head_ref, own_ref[...], other_ref[...])
        grad_ref[...] = grad
        b_down_ref[...] = jnp.sum(grad.astype(F32), axis=0, keepdims=True)
        acc[...] = jnp.zeros_like(acc)

    pre = (slope_ref[...].astype(F32) * nn(grad_ref[...], down_ref[...])).astype(LOW)
    pre_ref[...] = pre
    b_up_ref[...] = jnp.sum(pre.astype(F32), axis=0, keepdims=True)
    acc[...] += nt(pre, up_ref[...])
    refs[7][...] = tn(grad_ref[...], act_ref[...]).astype(LOW)
    refs[8][...] = tn(normed_ref[...], pre).astype(LOW)

    @pl.when(step == pl.num_programs(0) - 1)
    def _():
        part_ref[...] = acc[...].astype(LOW)


def inner_back_kernel(
    fused, head_ref, p_ref, po_ref, hidden_ref, grad_ref, trans_ref, gain_ref, out_w_ref,
    q_ref, kv_ref, wr_ref, basis_ref, probs_ref, *refs
):
    spots_ref, normed_ref, out_ref = refs[:3] if fused else (None, None, None)
    outs = refs[3 * fused :]
    proj_ref, resid_ref, gain_sum_ref, bias_sum_ref, dq_ref, dkv_ref, dwr_ref, far_ref = outs[:8]
    attended = outs[-1]
    grad_normed = p_ref[...].astype(F32) + po_ref[...].astype(F32)
    hat, scale = normalize(hidden_ref[...])
    gain_sum_ref[...] = jnp.sum(grad_normed * hat, axis=0, keepdims=True)
    bias_sum_ref[...] = jnp.sum(grad_normed, axis=0, keepdims=True)
    through = norm_back(grad_normed, hat, scale, gain_ref[...])
    resid_ref[...] = trans_ref[...] + my_half(head_ref, through)[0]
    proj = (grad_ref[...].astype(F32) + through).astype(LOW)
    proj_ref[...] = proj
    attended[...] = nn(proj, out_w_ref[...]).astype(LOW)
    attend_back_kernel(
        q_ref, kv_ref, wr_ref, basis_ref, probs_ref, attended, dq_ref, dkv_ref, dwr_ref
    )
    far_ref[...] = dkv_ref[far_ref.shape[0] :]
    if fused:
        kw = dq_ref.shape[1]
        columns_product(spots_ref, proj_ref, out_ref[...], outs[8], slice(None))
        columns_product(spots_ref, normed_ref, dq_ref[...], outs[9], slice(0, kw))
        columns_product(spots_ref, normed_ref, dkv_ref[...], outs[9], slice(kw, None))


def point_back_kernel(head_ref, grad_ref, point_ref, mine_ref, send_ref, bias_ref):
    grad = grad_ref[...]
    bias_ref[...] = jnp.sum(grad[: grad.shape[0] - 16].astype(F32), axis=0, keepdims=True)
    mine, theirs = my_half(head_ref, nt(grad, point_ref[...]))
    mine_ref[...] = mine
    send_ref[...] = theirs.astype(LOW)


def before(a, edge):
    row = lax.broadcasted_iota(jnp.int32, a.shape, 0)
    return jnp.where(row == 0, edge, pltpu.roll(a, 1, 0))


def behind(a, edge):
    row = lax.broadcasted_iota(jnp.int32, a.shape, 0)
    return jnp.where(row == a.shape[0] - 1, edge, pltpu.roll(a, a.shape[0] - 1, 0))


def section_back_kernel(mine_ref, got_ref, tap0, tap1, tap2, gm_ref, low_ref, coarse_ref, bias_ref):
    n = coarse_ref.shape[0]
    gm = mine_ref[...] + got_ref[...].astype(F32)
    gm_ref[...] = gm[: 2 * n]
    even, odd = gm[:n], gm[n : 2 * n]
    prev, later = gm[2 * n : 2 * n + 1], gm[2 * n + 1 : 2 * n + 2]
    gs_even = tap0[...] * odd + tap1[...] * even + tap2[...] * before(odd, prev)
    gs_odd = tap0[...] * behind(even, later) + tap1[...] * odd + tap2[...] * even
    coarse_ref[...] = gs_even + gs_odd
    gs = jnp.concatenate([gs_even, gs_odd], axis=0).astype(LOW)
    low_ref[...] = gs
    bias_ref[...] = jnp.sum(gs.astype(F32), axis=0, keepdims=True)


def section_kernel(trans_ref, skip_ref, prev_ref, later_ref, gm_ref, tap0, tap1, tap2, mixed_ref, depth_ref):
    n = trans_ref.shape[0]
    coarse = gelu(trans_ref[...])
    s_even, s_odd = coarse + skip_ref[:n], coarse + skip_ref[n:]
    s_before, s_after = before(s_odd, prev_ref[...]), behind(s_even, later_ref[...])
    mixed_ref[:n] = (tap0[...] * s_before + tap1[...] * s_even + tap2[...] * s_odd).astype(LOW)
    mixed_ref[n:] = (tap0[...] * s_even + tap1[...] * s_odd + tap2[...] * s_after).astype(LOW)
    even, odd = gm_ref[:n], gm_ref[n:]
    for k, a, b in ((0, s_before, s_even), (1, s_even, s_odd), (2, s_odd, s_after)):
        depth_ref[k : k + 1] = jnp.sum(even * a + odd * b, axis=0, keepdims=True)


def project_back_kernel(rows, dq_ref, *refs):
    parts, (qk_ref, v_ref, out_ref) = refs[:rows], refs[rows:]
    kw = dq_ref.shape[1]
    dkv = parts[0][...].astype(F32)
    for k in range(1, rows):
        dkv = dkv + parts[k][...].astype(F32)
    dkv = dkv.astype(LOW)
    dqk = jnp.concatenate([dq_ref[...], dkv[:, :kw]], axis=1)
    out_ref[...] = (nt(dqk, qk_ref[...]) + nt(dkv[:, kw:], v_ref[...])).astype(LOW)


def outer_back_kernel(
    head_ref, own_ref, other_ref, p_ref, po_ref, gain_ref, resid_ref, grad_ref, gain_sum_ref, bias_sum_ref
):
    hat, scale = normalize(
        ordered(head_ref, own_ref[...].astype(F32), other_ref[...].astype(F32))
    )
    grad_normed = p_ref[...].astype(F32) + po_ref[...].astype(F32)
    gain_sum_ref[...] = jnp.sum(grad_normed * hat, axis=0, keepdims=True)
    bias_sum_ref[...] = jnp.sum(grad_normed, axis=0, keepdims=True)
    through = norm_back(grad_normed, hat, scale, gain_ref[...])
    grad_ref[...] = resid_ref[...] + my_half(head_ref, through)[0]


def position_windows(z, width, rows):
    seq = width * rows
    block = jnp.bitwise_xor(z, np.array(bit_order(rows), np.int32)) - z
    t = block[:, None] * width + (np.arange(2 * width) - (width - 1))[None, :]
    distance = t.reshape(-1).astype(F32)
    magnitude = jnp.abs(distance)[:, None]
    number = NB // 4
    steps_up = np.arange(number, dtype=np.float32)
    half_life = (3.0 * (seq / 3.0) ** (steps_up / max(number - 1, 1))).astype(np.float32)
    decays = jnp.exp(-0.6931471805599453 * magnitude / half_life)
    central = (2.0 ** (steps_up + 1.0) - 1.0 > magnitude).astype(F32)
    even = jnp.concatenate([decays, central], axis=1)
    return jnp.concatenate([even, jnp.sign(distance)[:, None] * even], axis=1).astype(LOW)


G0, G1 = 0.7978845608028654, 0.044715


def gelu(u):
    return 0.5 * u * (1.0 + jnp.tanh(G0 * (u + G1 * u * u * u)))


def gelu_slope(u):
    t = jnp.tanh(G0 * (u + G1 * u * u * u))
    return 0.5 * (1.0 + t) + 0.5 * u * (1.0 - t * t) * (G0 * (1.0 + 3.0 * G1 * u * u))


def normalize(values):
    centered = values - jnp.mean(values, axis=-1, keepdims=True)
    scale = lax.rsqrt(jnp.mean(centered * centered, axis=-1, keepdims=True) + EPS)
    return centered * scale, scale


def norm_back(grad, hat, scale, gain):
    gg = grad * gain
    return scale * (
        gg
        - jnp.mean(gg, axis=-1, keepdims=True)
        - hat * jnp.mean(gg * hat, axis=-1, keepdims=True)
    )


def pick(head, own, other):
    return jnp.where(head == 0, own, other), jnp.where(head == 0, other, own)


def both_halves(head, own, other):
    return jnp.concatenate(pick(head, own, other), axis=1)


def half(a, head):
    n = a.shape[1] // 2
    return lax.dynamic_slice_in_dim(a, head * n, n, 1)


def one_hot(select, height, width):
    ii = lax.broadcasted_iota(jnp.int32, (height, width), 0)
    jj = lax.broadcasted_iota(jnp.int32, (height, width), 1)
    return select(ii, jj).astype(LOW)


def from_before(row):
    n = lax.axis_size(RW)
    return lax.ppermute(row, RW, [(i, i + 1) for i in range(n - 1)])


def from_behind(row):
    n = lax.axis_size(RW)
    return lax.ppermute(row, RW, [(i + 1, i) for i in range(n - 1)])


def shards(
    inputs,
    skip_input,
    cotangent,
    track_mask,
    norm1_gain,
    norm1_bias,
    query_weight,
    key_weight,
    value_weight,
    rel_weight,
    out_weight,
    norm2_gain,
    norm2_bias,
    up_weight,
    up_bias,
    down_weight,
    down_bias,
    skip_weight,
    skip_bias,
    depth_weight,
    point_weight,
    point_bias,
):
    head = lax.axis_index(HD)
    _, _, z = place()
    rows = lax.axis_size(RW)
    group = lax.axis_size(IT) * rows
    width, chan = inputs.shape[1], inputs.shape[2]
    model = 2 * chan
    heads = rel_weight.shape[0]
    kw = heads * KEY
    shard = norm1_gain.shape[0]
    small = skip_bias.shape[1]
    rel_cols = rel_weight.shape[1]

    skip_rows = skip_weight.shape[0]
    flat = jnp.concatenate(
        [norm1_gain, norm1_bias, norm2_gain, norm2_bias, down_bias, up_bias[0]]
        + [skip_bias[0], depth_weight.reshape(-1), point_bias[0], rel_weight.reshape(-1)]
    ).astype(LOW)
    spare = shard - skip_rows
    singles = [norm1_gain, norm1_bias, norm2_gain, norm2_bias, down_bias, up_bias]
    singles += [skip_bias, depth_weight, point_bias, rel_weight]
    flat = jnp.pad(flat, (0, spare * chan - flat.size)).reshape(spare, chan)
    ff = up_weight.shape[1]
    order = [up_weight, down_weight.T, out_weight.T, point_weight]
    order += [jnp.concatenate([skip_weight.astype(LOW), flat], axis=0)]
    order += [value_weight, query_weight, key_weight]
    if shard % 16 == 0 and skip_rows % 16 == 0 and spare == 16:
        order[4] = skip_weight
        singles = [v.reshape(-1, v.shape[-1]) for v in singles]
        (piece,) = run(
            functools.partial(pack_kernel, len(order)),
            1,
            order + singles,
            [new((shard, sum(w.shape[1] for w in order)), LOW)],
            [pltpu.VMEM((spare, chan), F32)],
        )
    else:
        piece = jnp.concatenate([w.astype(LOW) for w in order], axis=1)
    big = lax.all_gather(piece, (IT, RW), axis=0, tiled=True)
    at = 2 * ff

    def columns(start, count):
        return (big, (model, count), lambda i: (0, start // count))

    w_out, w_value = columns(at, chan), columns(at + 3 * chan, heads * VAL)
    w_qk = columns(at + 3 * chan + heads * VAL, 2 * kw)
    w_point = columns(at + chan, chan)
    steps = 3
    cut = ff // steps
    w_up = (big, (model, cut), lambda i: (0, i))
    w_down = (big, (model, cut), lambda i: (0, steps + i))
    if shard % 16 == 0 and skip_rows % 16 == 0 and spare == 16 and NB % group == 0:
        lengths = [shard] * 6 + [small] * 5
        w_skip, w_rel, *singles = run(
            functools.partial(unpack_kernel, shard, skip_rows, lengths),
            1,
            [columns(at + 2 * chan, chan)],
            [new((group * skip_rows, chan), LOW), new((heads * NB, KEY), F32)]
            + [new((1, group * n), F32) for n in lengths],
        )
        gain_one, bias_one, gain_two, bias_two, b_down, b_up = singles[:6]
        b_skip, tap0, tap1, tap2, b_point = singles[6:]
    else:
        last = big[:, at + 2 * chan : at + 3 * chan].reshape(group, shard, chan)
        w_skip = last[:, :skip_rows].reshape(group * skip_rows, chan)
        tails = last[:, skip_rows:].reshape(group, -1)

        def vector(start, count):
            return wide(tails[:, start : start + count]).reshape(1, -1)

        gain_one, bias_one, gain_two, bias_two, b_down, b_up = (
            vector(i * shard, shard) for i in range(6)
        )
        at = 6 * shard
        b_skip, tap0, tap1, tap2, b_point = (vector(at + i * small, small) for i in range(5))
        at += 5 * small
        w_rel = tails[:, at : at + heads * rel_cols].reshape(group, heads, rel_cols)
        w_rel = w_rel.transpose(1, 0, 2).reshape(heads * NB, KEY)

    at_head = (head.reshape(1).astype(jnp.int32), None, None)
    even = one_hot(lambda i, j: j == 2 * i, width, 2 * width)
    odd = one_hot(lambda i, j: j == 2 * i + 1, width, 2 * width)
    apart = jnp.concatenate([even, odd], axis=0)
    masked = (wide(cotangent[0]) * wide(track_mask)).astype(LOW)
    edges = [from_before(masked[-1:]), from_behind(masked[:1]), jnp.zeros((14, chan), LOW)]
    grad_out = nn(apart, masked).astype(LOW)
    grad_rows = jnp.concatenate([grad_out] + edges, axis=0)
    skip_low = nn(apart, gelu(wide(skip_input[0])).astype(LOW)).astype(LOW)

    own_blocks = [to_bit(inputs[0], k) if k else inputs[0] for k in bit_order(rows)]
    other_blocks = [to_head(b) for b in own_blocks]
    basis = position_windows(z, width, rows)
    queries, kv, normed_all = run(
        functools.partial(project_kernel, rows),
        1,
        [at_head] + own_blocks + other_blocks + [gain_one, bias_one, w_qk, w_value],
        [new((width, kw), LOW), new((rows * width, kw + heads * VAL), LOW)]
        + [new((rows * width, model), LOW)],
        after=[skip_low, grad_rows, basis],
    )
    attended, probs, partial_attn = run(
        attend_out_kernel,
        1,
        [queries, kv, w_rel, basis, w_out],
        [new((width, heads * VAL), LOW), new((heads, width, rows * width), LOW)]
        + [new((width, model), LOW)],
    )
    skip_term = nn(skip_low, w_skip) + b_skip
    gm_mine, gm_send, grad_point_bias = run(
        point_back_kernel,
        1,
        [at_head, grad_rows, w_point],
        [new((2 * width + 16, chan), F32), new((2 * width + 16, chan), LOW), new((1, chan), F32)],
        after=[partial_attn],
    )
    grad_mixed, grad_skip_low, grad_coarse, grad_skip_bias = run(
        section_back_kernel,
        1,
        [gm_mine, to_head(gm_send), tap0, tap1, tap2],
        [new((2 * width, chan), F32), new((2 * width, chan), LOW)]
        + [new((width, chan), F32), new((1, chan), F32)],
    )

    by_cut = (width, cut), lambda i: (0, i)
    hidden, normed_two, activated, slope, trans, send = run(
        ff_kernel,
        steps,
        [at_head, own_blocks[0], other_blocks[0], partial_attn, to_head(partial_attn)]
        + [gain_two, bias_two, (b_up, (1, cut), lambda i: (0, i)), b_down, w_up, w_down],
        [new((width, model), F32), new((width, model), LOW), (new((width, ff), LOW), *by_cut)]
        + [(new((width, ff), LOW), *by_cut), new((width, chan), F32), new((width, chan), LOW)],
        [pltpu.VMEM((width, model), F32)],
        after=[skip_term],
    )
    trans = trans + wide(to_head(send))

    for_skip = Scatter([(skip_low, grad_skip_low)])

    s_first = gelu(trans[:1]) + skip_term[:1]
    s_last = gelu(trans[-1:]) + skip_term[-1:]
    prev, later = wide(from_before(low(s_last))), wide(from_behind(low(s_first)))

    grad_trans = gelu_slope(trans) * grad_coarse
    grad_own = low(grad_trans)
    owned = model // lax.axis_size(IT)
    fused = fits(owned)
    core_rows = model // 2
    spots = jnp.stack(spots_of(1 - place()[1], owned)).astype(jnp.int32), None, None
    extra = new((model, ff), LOW), (model, cut), lambda i: (0, i)
    grad_ff_low, grad_pre_low, partial_two, grad_up_bias, grad_down_bias, *theirs = run(
        ff_back_kernel,
        steps,
        [at_head, grad_own, to_head(grad_own), (slope, *by_cut), w_up, w_down]
        + [normed_two, (activated, *by_cut)],
        [new((width, model), LOW), (new((width, ff), LOW), *by_cut), new((width, model), LOW)]
        + [(new((1, ff), F32), (1, cut), lambda i: (0, i)), new((1, model), F32)]
        + [extra, extra],
        [pltpu.VMEM((width, model), F32)],
        after=[prev, later],
    )
    for_down, for_up = (
        RowSum(lax.psum_scatter(t, IT, scatter_dimension=0, tiled=True)) for t in theirs
    )
    mixed, grad_depth = run(
        section_kernel,
        1,
        [trans, skip_term, prev, later, grad_mixed, tap0, tap1, tap2],
        [new((2 * width, chan), LOW), new((3, chan), F32)],
    )
    grad_proj_low, resid, grad_gain_two, grad_bias_two, dq, dkv, grad_rel, far, *theirs = run(
        functools.partial(inner_back_kernel, fused),
        1,
        [at_head, partial_two, to_head(partial_two), hidden, grad_ff_low, grad_trans, gain_two]
        + [w_out, queries, kv, w_rel, basis, probs]
        + [spots, normed_all, attended][: 3 * fused],
        [new((width, model), LOW), new((width, chan), F32)]
        + [new((1, model), F32), new((1, model), F32)]
        + [new(queries.shape, LOW), new(kv.shape, LOW), new(w_rel.shape, F32)]
        + [new((kv.shape[0] // 2, kv.shape[1]), LOW)]
        + [new((core_rows, heads * VAL), LOW), new((core_rows, kw + kv.shape[1]), LOW)][: 2 * fused],
        [pltpu.VMEM((width, heads * VAL), LOW)],
        after=for_skip.send + [mixed],
    )
    dkv_parts, rest, bit, arrived = [dkv[:width]], dkv, 1, []
    summed = []
    while bit < rows:
        n = rest.shape[0] // 2
        got = to_bit(far if bit == 1 else rest[n:], bit)
        dkv_parts.append(got[:width])
        arrived.append(got)
        if n > width:
            rest = low(wide(rest[:n]) + wide(got))
            dkv_parts = [rest[:width]]
            summed.append(rest)
        bit *= 2
    skip_across = [for_skip.across(0)]
    mixed_other = to_head(mixed)
    skip_across = [for_skip.across(0)]
    for_skip.take(skip_across)
    for_attn = Scatter(
        [(grad_proj_low, attended), (normed_all, dq), (normed_all, dkv)],
        theirs or None,
        [],
        skip_across[0],
        [[0, 1, 2]],
    )
    mixed_full = both_halves(head, mixed, mixed_other)
    for_point = Scatter([(mixed_full, grad_out)], None, [], for_attn.send)
    for_down.step(for_point.theirs)
    attn_across = [for_attn.across(0)]
    for_attn.take(attn_across)
    point_across = for_point.across(0)
    for_point.take([point_across])
    (partial_one,) = run(
        functools.partial(project_back_kernel, len(dkv_parts)),
        1,
        [dq] + dkv_parts + [w_qk, w_value],
        [new((width, model), LOW)],
        after=for_point.send + [for_down.sent],
    )
    for_down.step([partial_one])
    for_up.step([for_down.sent])
    for_attn.step([for_up.sent])
    for_skip.step([for_attn.sent])
    input_grad, grad_gain_one, grad_bias_one = run(
        outer_back_kernel,
        1,
        [at_head, own_blocks[0], other_blocks[0], partial_one, to_head(partial_one)]
        + [gain_one, resid],
        [new((width, chan), F32), new((1, model), F32), new((1, model), F32)],
        after=[for_skip.sent] + point_across + for_up.got + for_down.got,
    )
    input_grad = input_grad[None]
    for_attn.step([grad_gain_one])
    for_up.step([for_attn.sent] + for_skip.got)
    for_point.step([for_up.sent])
    for_skip.step([for_point.sent])
    early = [for_point.sent]
    for_point.step([for_skip.sent] + for_attn.got)
    last = [for_point.sent]
    (grad_down,), (grad_up,) = for_down.finish(early), for_up.finish(early)
    (grad_skip,), (grad_point,) = for_skip.finish(last), for_point.finish(last)
    grad_out_w, *grad_qkv = for_attn.finish(early, [heads * VAL, kw, kw, heads * VAL])
    result = (nn(mixed_full, w_point[0][:, 2 * ff + chan : 2 * ff + 2 * chan]) + b_point).astype(LOW)
    block_output = tn(apart, result).astype(LOW)[None]
    parts = [grad_gain_one, grad_bias_one, grad_gain_two, grad_bias_two, grad_down_bias]
    parts += [grad_up_bias, grad_skip_bias] + [grad_depth] * 3 + [grad_point_bias]
    which = [0] * 7 + [0, 1, 2] + [0]
    if NB % group == 0:
        shares = [(i, p.shape[-1] // group) for i, p in zip(which, parts)]
        total = sum(n for _, n in shares) + heads * rel_cols
        (parts,) = run(
            functools.partial(pack_sums_kernel, shares),
            1,
            [p.reshape(-1, p.shape[-1]) for p in parts] + [grad_rel],
            [new((group, total), F32)],
        )
    else:
        parts = [p.reshape(-1, p.shape[-1])[i] for i, p in zip(which, parts)]
        rel_parts = grad_rel.reshape(heads, group, rel_cols).transpose(1, 0, 2)
        parts = [p.reshape(group, -1) for p in parts + [rel_parts]]
        parts = jnp.concatenate(parts, axis=1)
    sums = scatter_small(parts, last)

    def own(start, count):
        return sums[0, start : start + count]

    at = 6 * shard
    return (
        block_output,
        input_grad,
        own(0, shard),
        own(shard, shard),
        *grad_qkv,
        own(at + 5 * small, heads * rel_cols).reshape(heads, rel_cols),
        grad_out_w.T,
        own(2 * shard, shard),
        own(3 * shard, shard),
        grad_up,
        own(5 * shard, shard)[None],
        grad_down.T,
        own(4 * shard, shard),
        grad_skip,
        own(at, small)[None],
        own(at + small, 3 * small).reshape(3, 1, small),
        grad_point,
        own(at + 4 * small, small)[None],
    )


def solution(mesh):
    gr = (IT, RW)
    vec, cols, rws = P(gr), P(gr, HD), P(HD, gr)
    act = P(IT, RW, HD)
    taps = P(None, HD, gr)
    weights = (vec, vec, cols, cols, cols, rws, rws, vec, vec, cols, rws, rws, vec, cols, rws)
    weights += (taps, cols, rws)
    return jax.shard_map(
        shards,
        mesh=mesh,
        in_specs=(act, P(IT, RW, None), act, P(IT, HD)) + weights,
        out_specs=(act, act) + weights,
        check_vma=False,
    )
```
